32 devices in a mesh: dp: 4 (over y, x), seq: 8 (over z, core).
Axes of the slice: x: 2, y: 2, z: 4, core: 2. Of those that a mesh axis runs over, the one named last changes fastest.
Arguments:
- tokens: bfloat16 [8, 512, 2048], P('dp', 'seq'), may hold values from -6 to 6
- resets: int32 [8, 512], P('dp', 'seq'), may hold values from 0 to 1, as said below
- cotangent: bfloat16 [8, 512, 2048], P('dp', 'seq'), may hold values from -6 to 6
- w_in: bfloat16 [2, 2048, 8512], P(None, ('dp', 'seq')), may hold values from -0.125 to 0.125
- w_out: bfloat16 [2, 4096, 2048], P(None, ('dp', 'seq')), may hold values from -0.09375 to 0.09375
- gain_in: float32 [2, 2048], replicated, may hold values from 0.5 to 1.5
- gain_mid: float32 [2, 4096], replicated, may hold values from 0.5 to 1.5
- conv_w: float32 [2, 4, 4352], replicated, may hold values from -3 to 3
- conv_b: float32 [2, 4352], replicated, may hold values from -1.5 to 1.5
- dt_bias: float32 [2, 64], replicated, may hold values from -1 to 0.5
- a_log: float32 [2, 64], replicated, may hold values from -12 to -2
- d_skip: float32 [2, 64], replicated, may hold values from 1 to 4
Outputs:
- outputs: bfloat16 [8, 512, 2048], P('dp', 'seq')
- grad_tokens: float32 [8, 512, 2048], P('dp', 'seq')
- grad_w_in: float32 [2, 2048, 8512], P(None, ('dp', 'seq'))
- grad_w_out: float32 [2, 4096, 2048], P(None, ('dp', 'seq'))
- grad_gain_in: float32 [2, 2048], replicated
- grad_gain_mid: float32 [2, 4096], replicated
- grad_conv_w: float32 [2, 4, 4352], replicated
- grad_conv_b: float32 [2, 4352], replicated
- grad_dt_bias: float32 [2, 64], replicated
- grad_a_log: float32 [2, 64], replicated
- grad_d_skip: float32 [2, 64], replicated
The draws below stay inside these ranges and needn't reach their ends.
Inputs may be any that keep to these rules, and one draw needn't show every extreme that they name: `resets`: 1 marks the first token of a document, 0 any other token; the first token of every row is 1; of the 2 rows of each index of dp, one holds no other 1.
All inputs are finite; a program needn't handle non-finite values.
Results may differ from the reference program's by a relative error of at most 0.0086.
Values may be sent and summed in bfloat16 or wider, within the bound.
A program may use at most 576 MiB of HBM per device.

```python
import math
import jax
import jax.numpy as jnp
from jax import lax

D = 2048
HEADS = 64
HEAD = 64
STATE = 128
CONVW = 4
LAYERS = 2
SEG = 64
ROWS_DEV = 2
DI = 4096
CONV_CH = 4352
IN_W = 8512
ROW_LEN = 512
ROWS = 8
N_SEQ = 8


def draw_resets(key, part):
    key = jax.random.fold_in(key, 11)
    mark_key, edge_key, place_key, row_key = jax.random.split(key, 4)
    spans = ROW_LEN // SEG
    marks = (jax.random.randint(mark_key, (ROWS, ROW_LEN), 0, 3 * SEG) == 0).astype(jnp.int32)
    picked = jax.random.randint(edge_key, (ROWS, spans), 0, 4) == 0
    offset = jax.random.randint(place_key, (ROWS, spans), 1 - CONVW, CONVW - 1)
    bounds = jnp.arange(spans) * SEG
    places = bounds[None, :] + offset
    usable = picked & (jnp.arange(spans) > 0)[None, :]
    spots = (places[:, :, None] == jnp.arange(ROW_LEN)[None, None, :]) & usable[:, :, None]
    marks = jnp.maximum(marks, jnp.any(spots, axis=1).astype(jnp.int32))
    groups = ROWS // ROWS_DEV
    whole_row = jax.random.randint(row_key, (groups,), 0, ROWS_DEV)
    row_ids = jnp.arange(ROWS)
    single = row_ids % ROWS_DEV == whole_row[row_ids // ROWS_DEV]
    marks = jnp.where(single[:, None], 0, marks)
    first = (jnp.arange(ROW_LEN) == 0).astype(jnp.int32)
    return jnp.maximum(marks, first[None, :])


def draw_a_log(key, part):
    key = jax.random.fold_in(key, 23)
    kind_key, slow_key, fast_key = jax.random.split(key, 3)
    slow = jax.random.randint(kind_key, (LAYERS, HEADS), 0, 2) > 0
    slow_rate = jax.random.uniform(slow_key, (LAYERS, HEADS), jnp.float32, math.log(0.2), math.log(1.5)) - math.log(ROW_LEN)
    fast_rate = jax.random.uniform(fast_key, (LAYERS, HEADS), jnp.float32, math.log(0.02), math.log(0.1))
    return jnp.where(slow, slow_rate, fast_rate)


def block_levels(own_key, extent, cuts, smallest, top_value):
    loudness, own = 1.0, jax.random.fold_in(own_key, 6)
    for position, blocks in cuts:
        heights = jnp.exp(jax.random.uniform(jax.random.fold_in(own, position), (blocks,), jnp.float32, smallest / len(cuts), top_value / len(cuts)))
        loudness = loudness * jnp.repeat(heights, extent[position] // blocks).reshape([-1 if axis == position else 1 for axis in range(len(extent))])
    return loudness


def normal_values(stream_key, dims, deviation, most, cuts=(), kind=jnp.bfloat16):
    drawn = deviation * jax.random.normal(stream_key, dims, jnp.float32)
    if cuts:
        drawn = drawn * block_levels(stream_key, dims, cuts, -0.22, 0.18)
    return jnp.clip(drawn, -most, most).astype(kind)


def setup_inputs(seed: int = 0) -> dict:
    key_list = jax.random.split(jax.random.key(seed), 13)
    tokens = normal_values(key_list[0], (ROWS, ROW_LEN, D), 1.0, 6.0, ((0, 4), (1, 8)))
    resets = draw_resets(jax.random.fold_in(key_list[12], 71), 0)
    cotangent = normal_values(key_list[2], (ROWS, ROW_LEN, D), 1.0, 6.0, ((0, 4), (1, 8)))
    w_in = normal_values(key_list[3], (LAYERS, D, IN_W), D ** -0.5, 0.125, ((1, 32),))
    w_out = normal_values(key_list[4], (LAYERS, DI, D), DI ** -0.5, 0.09375, ((1, 32),))
    gain_in = jnp.clip(1.0 + 0.1 * jax.random.normal(key_list[5], (LAYERS, D), jnp.float32), 0.5, 1.5)
    gain_mid = jnp.clip(1.0 + 0.1 * jax.random.normal(key_list[6], (LAYERS, DI), jnp.float32), 0.5, 1.5)
    conv_w = normal_values(key_list[7], (LAYERS, CONVW, CONV_CH), CONVW ** -0.5, 3.0, (), jnp.float32)
    conv_b = normal_values(key_list[8], (LAYERS, CONV_CH), 0.3, 1.5, (), jnp.float32)
    dt_bias = jnp.clip(jax.random.uniform(key_list[9], (LAYERS, HEADS), jnp.float32, -1.0, 0.5), -1.0, 0.5)
    a_log = draw_a_log(jax.random.fold_in(key_list[12], 71), 0)
    d_skip = jnp.clip(jax.random.uniform(key_list[11], (LAYERS, HEADS), jnp.float32, 1.0, 4.0), 1.0, 4.0)
    return {"tokens": tokens, "resets": resets, "cotangent": cotangent, "w_in": w_in, "w_out": w_out, "gain_in": gain_in, "gain_mid": gain_mid, "conv_w": conv_w, "conv_b": conv_b, "dt_bias": dt_bias, "a_log": a_log, "d_skip": d_skip}


EPS = 1e-05
HIGH = lax.Precision.HIGHEST

@jax.custom_vjp
def low(v):
    return lax.optimization_barrier(v.astype(jnp.bfloat16)).astype(jnp.float32)

@jax.custom_vjp
def low_back(v):
    return v

def low_keep(v):
    return (low(v), None)

def low_pass(kept, grad):
    return (grad,)

def back_keep(v):
    return (v, None)

def back_low(kept, grad):
    return (low(grad),)
low.defvjp(low_keep, low_pass)
low_back.defvjp(back_keep, back_low)

def rms_norm(values, gain):
    return values * lax.rsqrt(lax.optimization_barrier(jnp.mean(values * values, axis=-1, keepdims=True)) + EPS) * gain

def scan_row(xs, bmat, cmat, dt, a_log, counts):
    cum = jnp.cumsum(dt * -jnp.exp(a_log), axis=1)
    last = counts[:, -1:]
    to_end = jnp.where((counts == last)[..., None], jnp.exp(cum[:, -1:, :] - cum), 0.0) * dt
    states = jnp.einsum('ksh,kshp,ksn->khpn', to_end, xs, bmat, precision=HIGH)
    passing = jnp.where(last == 0.0, jnp.exp(cum[:, -1, :]), 0.0)

    def link(state, item):
        return (item[0][:, None, None] * state + item[1], state)
    start = jnp.zeros((HEADS, HEAD, STATE), jnp.float32)
    incoming = lax.scan(link, start, (passing, states))[1]
    order = jnp.arange(SEG)
    inside = (order[:, None] >= order[None, :]) & (counts[:, :, None] == counts[:, None, :])
    inside = inside[..., None]
    gap = cum[:, :, None, :] - cum[:, None, :, :]
    decay = jnp.where(inside, jnp.exp(jnp.where(inside, gap, 0.0)), 0.0)
    scores = jnp.einsum('kqn,ksn->kqs', cmat, bmat, precision=HIGH)
    weights = scores[..., None] * decay * dt[:, None, :, :]
    y_inner = jnp.einsum('kqsh,kshp->kqhp', weights, xs, precision=HIGH)
    reach = jnp.where((counts == 0.0)[..., None], jnp.exp(cum), 0.0)
    y_outer = reach[..., None] * jnp.einsum('kqn,khpn->kqhp', cmat, incoming, precision=HIGH)
    return y_inner + y_outer

def mixer(row, doc, counts, w_in, w_out, gain_in, gain_mid, conv_w, conv_b, dt_bias, a_log, d_skip):
    hidden = low(rms_norm(row, gain_in))
    proj = low_back(jnp.dot(hidden, w_in, precision=HIGH))
    gate_z = proj[:, :DI]
    xbc = proj[:, DI:DI + CONV_CH]
    dt_raw = proj[:, DI + CONV_CH:]
    conv = conv_b + conv_w[CONVW - 1] * xbc
    for back in range(1, CONVW):
        moved = jnp.pad(xbc, ((back, 0), (0, 0)))[:ROW_LEN]
        before = jnp.pad(doc, (back, 0), constant_values=-1.0)[:ROW_LEN]
        conv = conv + conv_w[CONVW - 1 - back] * jnp.where((before == doc)[:, None], moved, 0.0)
    act = jax.nn.silu(conv)
    xs = act[:, :DI].reshape(N_SEQ, SEG, HEADS, HEAD)
    bmat = act[:, DI:DI + STATE].reshape(N_SEQ, SEG, STATE)
    cmat = act[:, DI + STATE:].reshape(N_SEQ, SEG, STATE)
    dt = jax.nn.softplus(dt_raw + dt_bias).reshape(N_SEQ, SEG, HEADS)
    y_seq = scan_row(xs, bmat, cmat, dt, a_log, counts)
    y_all = (y_seq + d_skip[:, None] * xs).reshape(ROW_LEN, DI)
    mid = low(rms_norm(y_all * jax.nn.silu(gate_z), gain_mid))
    branch = low_back(jnp.dot(mid, w_out, precision=HIGH))
    return row + branch

def model_row(params, row, marks_row):
    w_in, w_out, gain_in, gain_mid, conv_w, conv_b, dt_bias, a_log, d_skip = params
    marks = marks_row.astype(jnp.float32)
    doc = jnp.cumsum(marks)
    counts = jnp.cumsum(marks.reshape(N_SEQ, SEG), axis=1)
    for level in range(LAYERS):
        row = mixer(row, doc, counts, w_in[level], w_out[level], gain_in[level], gain_mid[level], conv_w[level], conv_b[level], dt_bias[level], a_log[level], d_skip[level])
    return row

def reference(tokens, resets, cotangent, w_in, w_out, gain_in, gain_mid, conv_w, conv_b, dt_bias, a_log, d_skip):
    params = (w_in.astype(jnp.float32), w_out.astype(jnp.float32), gain_in.astype(jnp.float32), gain_mid.astype(jnp.float32), conv_w.astype(jnp.float32), conv_b.astype(jnp.float32), dt_bias.astype(jnp.float32), a_log.astype(jnp.float32), d_skip.astype(jnp.float32))
    start = tokens.astype(jnp.float32)

    def forward(weights, inputs):

        def step(carry, item):
            return (carry, jax.checkpoint(model_row)(weights, item[0], item[1]))
        return lax.scan(step, jnp.zeros((), jnp.float32), (inputs, resets))[1]
    final, pull = jax.vjp(forward, params, start)
    grad_params, grad_start = pull(cotangent.astype(jnp.float32))
    return (final.astype(jnp.bfloat16), grad_start, grad_params[0], grad_params[1], grad_params[2], grad_params[3], grad_params[4], grad_params[5], grad_params[6], grad_params[7], grad_params[8])
```

```python
import functools

import jax
import jax.numpy as jnp
from jax import lax
from jax.experimental import pallas as pl
from jax.experimental.pallas import tpu as pltpu
from jax.sharding import PartitionSpec as P

HEADS = 64
HEAD = 64
STATE = 128
DI = 4096
CONV_CH = 4352
CHUNK = 128
LANES = 128
TAPS = 4
EPS = 1e-05
HIGH = lax.Precision.HIGHEST
BF = jnp.bfloat16
F32 = jnp.float32
FAR = -1e30
BOTH = ("dp", "seq")


def dot(a, b, dims=((1,), (0,)), precision=None):
    return lax.dot_general(a, b, (dims, ((), ())), preferred_element_type=F32, precision=precision)


NT = ((1,), (1,))
TN = ((0,), (0,))


def head_matrix(inner):
    row = lax.broadcasted_iota(jnp.int32, (8, inner), 0)
    col = lax.broadcasted_iota(jnp.int32, (8, inner), 1)
    return (col // HEAD == row).astype(F32)


def by_pair(cols, first, pair):
    q = cols.shape[0]
    lane = lax.broadcasted_iota(jnp.int32, (q, LANES), 1)
    at = first + 2 * pair
    return jnp.where(lane < HEAD, cols[:, at : at + 1], cols[:, at + 1 : at + 2])


def spread(cols, first, inner):
    return jnp.concatenate([by_pair(cols, first, j) for j in range(inner // LANES)], axis=1)


def stacked_halves(x):
    lane = lax.broadcasted_iota(jnp.int32, x.shape, 1)
    zero = jnp.zeros_like(x)
    return jnp.concatenate([jnp.where(lane < HEAD, x, zero), jnp.where(lane < HEAD, zero, x)], axis=0)


def chunk_masks(marks_ref, at, first):
    here = marks_ref[pl.ds(at, 1)]
    past = marks_ref[pl.ds(jnp.maximum(at - 1, 0), 1)]
    same = 1.0 - jnp.concatenate([jnp.where(first, 1.0, past), here], axis=1)
    same = jnp.broadcast_to(same, (8, 2 * CHUNK))
    rows = [same]
    for back in range(1, TAPS - 1):
        rows.append(rows[-1] * pltpu.roll(same, back, 1))
    rows = [row[:1, CHUNK:] for row in rows]
    row = lax.broadcasted_iota(jnp.int32, (CHUNK, CHUNK), 0)
    col = lax.broadcasted_iota(jnp.int32, (CHUNK, CHUNK), 1)
    counts = dot(jnp.broadcast_to(here, (8, CHUNK)), (row <= col).astype(F32))[:1]
    return jnp.concatenate(rows + [counts] + [jnp.zeros_like(counts)] * (8 - TAPS), axis=0), counts


def chunk_rows(dt_block, hp, cr):
    raw = jnp.transpose(dt_block)[:8] + hp[0]
    dt = jnp.maximum(raw, 0.0) + jnp.log1p(jnp.exp(-jnp.abs(raw)))
    rate = jnp.exp(hp[1])
    row = lax.broadcasted_iota(jnp.int32, (CHUNK, CHUNK), 0)
    col = lax.broadcasted_iota(jnp.int32, (CHUNK, CHUNK), 1)
    cum = dot(-dt * rate, (row <= col).astype(F32), precision=HIGH)
    end = cum[:, CHUNK - 1 :]
    last = cr[:, CHUNK - 1 :]
    reach = jnp.where(cr == 0.0, jnp.exp(cum), 0.0)
    to_end = jnp.where(cr == last, jnp.exp(end - cum), 0.0)
    passing = jnp.where(last == 0.0, jnp.exp(end), 0.0)
    return raw, dt, rate, cum, reach, to_end, passing


def conv_in(ext, xbc, mk, cw):
    total = cw[4:5] + cw[TAPS - 1 : TAPS] * xbc
    moved = []
    for back in range(1, TAPS):
        m = pltpu.roll(ext, back, 0)[8:] * mk[:, back - 1 : back]
        moved.append(m)
        total = total + cw[TAPS - 1 - back : TAPS - back] * m
    return total, moved


def decay_of(cols, cum, mask, head):
    return jnp.exp(cols[:, head : head + 1] - cum[head : head + 1] + mask)


def chunk_mask(mk, cr):
    row = lax.broadcasted_iota(jnp.int32, (CHUNK, CHUNK), 0)
    col = lax.broadcasted_iota(jnp.int32, (CHUNK, CHUNK), 1)
    return jnp.where((row >= col) & (mk[:, 3:4] == cr), 0.0, FAR)


def mix_fwd_kernel(inner, proj_ref, marks_ref, cw_ref, hp_ref, gated_ref, ss_ref, ys_ref, sin_ref, s_scr, tail_scr):
    bc = CONV_CH - DI

    @pl.when(pl.program_id(1) == 0)
    def _():
        s_scr[...] = jnp.zeros_like(s_scr)
        tail_scr[...] = jnp.zeros_like(tail_scr)

    at = pl.program_id(0) * pl.num_programs(1) + pl.program_id(1)
    masks, cr = chunk_masks(marks_ref, at, pl.program_id(1) == 0)
    mk = jnp.transpose(masks)
    cw = cw_ref[...]
    xbc = proj_ref[0, :, LANES + inner :]
    ext = jnp.concatenate([tail_scr[...], xbc], axis=0)
    tail_scr[...] = xbc[CHUNK - 8 :]
    conv, _ = conv_in(ext, xbc, mk, cw)
    act = conv * jax.nn.sigmoid(conv)
    xs = act[:, :inner]
    bmat = act[:, inner : inner + STATE].astype(BF)
    cmat = act[:, inner + STATE :].astype(BF)
    raw, dt, rate, cum, reach, to_end, passing = chunk_rows(proj_ref[0, :, :LANES], hp_ref, cr)
    cols = jnp.transpose(jnp.concatenate([cum, dt, reach, to_end], axis=0))
    mask = chunk_mask(mk, cr)
    xd = xs * spread(cols, 8, inner)
    xdb = xd.astype(BF)
    state = s_scr[...]
    sin_ref[0, 0] = state
    scores = dot(cmat, bmat, NT)
    y = spread(cols, 16, inner) * dot(cmat, state.astype(BF))
    inner_parts = []
    for j in range(inner // LANES):
        w = [(scores * decay_of(cols, cum, mask, 2 * j + i)).astype(BF) for i in range(2)]
        inner_parts.append(dot(jnp.concatenate(w, axis=1), stacked_halves(xdb[:, j * LANES : (j + 1) * LANES])))
    y = y + jnp.concatenate(inner_parts, axis=1)
    ys_ref[0] = y
    keep = jnp.sum(passing * head_matrix(inner), axis=0, keepdims=True)
    s_scr[...] = keep * state + dot(bmat, (xd * spread(cols, 24, inner)).astype(BF), TN)
    z = proj_ref[0, :, LANES : LANES + inner]
    gated = (y + cw[5:6, :inner] * xs) * (z * jax.nn.sigmoid(z))
    gated_ref[0] = gated
    ss_ref[pl.ds(at, 1)] = dot(jnp.ones((8, inner), F32), gated * gated, NT, HIGH)[:1]


def mix_fwd(proj, marks, cw, hp, inner):
    rows, length, cols = proj.shape
    chunks = length // CHUNK
    bc = CONV_CH - DI
    whole = lambda r, c: (0, 0)
    return pl.pallas_call(
        functools.partial(mix_fwd_kernel, inner),
        grid=(rows, chunks),
        in_specs=[
            pl.BlockSpec((1, CHUNK, cols), lambda r, c: (r, c, 0)),
            pl.BlockSpec(marks.shape, whole),
            pl.BlockSpec(cw.shape, whole),
            pl.BlockSpec(hp.shape, lambda r, c: (0, 0, 0)),
        ],
        out_specs=[
            pl.BlockSpec((1, CHUNK, inner), lambda r, c: (r, c, 0)),
            pl.BlockSpec((rows * chunks, CHUNK), whole),
            pl.BlockSpec((1, CHUNK, inner), lambda r, c: (r, c, 0)),
            pl.BlockSpec((1, 1, STATE, inner), lambda r, c: (r, c, 0, 0)),
        ],
        out_shape=[
            jax.ShapeDtypeStruct((rows, length, inner), F32),
            jax.ShapeDtypeStruct((rows * chunks, CHUNK), F32),
            jax.ShapeDtypeStruct((rows, length, inner), F32),
            jax.ShapeDtypeStruct((rows, chunks, STATE, inner), F32),
        ],
        scratch_shapes=[pltpu.VMEM((STATE, inner), F32), pltpu.VMEM((8, inner + bc), F32)],
        compiler_params=pltpu.CompilerParams(
            dimension_semantics=("arbitrary", "arbitrary"), vmem_limit_bytes=60 * 2**20
        ),
        cost_estimate=pl.CostEstimate(flops=3 * 10**9, bytes_accessed=18 * 2**20, transcendentals=10**6),
    )(proj, marks, cw, hp)


def silu_slope(v, s):
    return s * (1.0 + v * (1.0 - s))


def mix_bwd_kernel(
    inner, chunks, proj_ref, prev_ref, marks_ref, cw_ref, hp_ref, ys_ref, sin_ref, dmid_ref, scale_ref, cube_ref, gain_ref,
    dp_ref, dbc_ref, gc_ref, gh_ref, ds_scr, gam_scr, head_scr,
):
    bc = CONV_CH - DI
    wide = inner + bc
    step = pl.program_id(1)

    @pl.when((step == 0) & (pl.program_id(0) == 0))
    def _():
        gc_ref[...] = jnp.zeros_like(gc_ref)
        gh_ref[...] = jnp.zeros_like(gh_ref)

    @pl.when(step == 0)
    def _():
        ds_scr[...] = jnp.zeros_like(ds_scr)
        gam_scr[...] = jnp.zeros_like(gam_scr)
        head_scr[...] = jnp.zeros_like(head_scr)

    at = pl.program_id(0) * chunks + chunks - 1 - step
    masks, cr = chunk_masks(marks_ref, at, step == chunks - 1)
    mk = jnp.transpose(masks)
    cw = cw_ref[...]
    heads = head_matrix(inner)
    xbc = proj_ref[0, :, LANES + inner :]
    ext = jnp.concatenate([prev_ref[0, :, LANES + inner :], xbc], axis=0)
    conv, moved = conv_in(ext, xbc, mk, cw)
    sig = jax.nn.sigmoid(conv)
    act = conv * sig
    xs = act[:, :inner]
    bmat = act[:, inner : inner + STATE].astype(BF)
    cmat = act[:, inner + STATE :].astype(BF)
    raw, dt, rate, cum, reach, to_end, passing = chunk_rows(proj_ref[0, :, :LANES], hp_ref, cr)
    norm = [scale_ref[pl.ds(at, 1)], cube_ref[pl.ds(at, 1)], jnp.zeros((6, CHUNK), F32)]
    cols = jnp.transpose(jnp.concatenate([cum, dt, reach, to_end] + norm, axis=0))
    mask = chunk_mask(mk, cr)
    dt_e = spread(cols, 8, inner)
    reach_e = spread(cols, 16, inner)
    end_e = spread(cols, 24, inner)
    xd = xs * dt_e
    xdb = xd.astype(BF)

    z = proj_ref[0, :, LANES : LANES + inner]
    sz = jax.nn.sigmoid(z)
    silu_z = z * sz
    ys = ys_ref[0]
    skip = cw[5:6, :inner]
    y = ys + skip * xs
    gated = y * silu_z
    d_mid = dmid_ref[0]
    r_mid = d_mid * cols[:, 32:33]
    d_gated = r_mid * gain_ref[...] - gated * cols[:, 33:34]
    d_gain = jnp.sum(r_mid * gated, axis=0, keepdims=True)
    dy = d_gated * silu_z
    dyb = dy.astype(BF)
    dyr = dyb.astype(F32)
    dz = d_gated * y * silu_slope(z, sz)

    state = sin_ref[0, 0]
    d_state = ds_scr[...]
    dsb = d_state.astype(BF)
    scores = dot(cmat, bmat, NT)
    reached = (reach_e * dyr).astype(BF)
    ended = (end_e * xd).astype(BF)
    d_xd = end_e * dot(bmat, dsb)
    d_scores = jnp.zeros((CHUNK, CHUNK), F32)
    parts = []
    for j in range(inner // LANES):
        lanes = slice(j * LANES, (j + 1) * LANES)
        pair_dy = stacked_halves(dyb[:, lanes])
        d_w = dot(pair_dy, xdb[:, lanes], NT)
        ws = []
        for i in range(2):
            decay = decay_of(cols, cum, mask, 2 * j + i)
            ws.append((scores * decay).astype(BF))
            d_scores = d_scores + d_w[i * CHUNK : (i + 1) * CHUNK] * decay
        parts.append(dot(jnp.concatenate(ws, axis=0), pair_dy, TN))
    d_xd = d_xd + jnp.concatenate(parts, axis=1)
    dgb = d_scores.astype(BF)
    d_c = dot(reached, state.astype(BF), NT) + dot(dgb, bmat)
    d_b = dot(ended, dsb, NT) + dot(dgb, cmat, TN)
    keep = jnp.sum(passing * heads, axis=0, keepdims=True)
    new_ds = keep * d_state + dot(cmat, reached, TN)
    alpha = dot(heads, dyr * ys, NT, HIGH)
    beta = dot(heads, xs * d_xd, NT, HIGH)
    lane = lax.broadcasted_iota(jnp.int32, (8, CHUNK), 1)
    d_cum = alpha - dt * beta + jnp.where(lane == CHUNK - 1, gam_scr[...], 0.0)
    row = lax.broadcasted_iota(jnp.int32, (CHUNK, CHUNK), 0)
    col = lax.broadcasted_iota(jnp.int32, (CHUNK, CHUNK), 1)
    d_log = dot(d_cum, (row >= col).astype(F32), precision=HIGH)
    d_dt = beta - rate * d_log
    d_raw = d_dt * jax.nn.sigmoid(raw)
    gh_ref[0] += d_raw
    gh_ref[1] += -rate * dt * d_log
    ds_scr[...] = new_ds
    gam_scr[...] = jnp.broadcast_to(
        jnp.sum(heads * jnp.sum(new_ds * state, axis=0, keepdims=True), axis=1, keepdims=True), gam_scr.shape
    )
    d_xs = dt_e * d_xd + skip * dy

    d_conv = jnp.concatenate([d_xs, d_b, d_c], axis=1) * silu_slope(conv, sig)
    d_xbc = cw[TAPS - 1 : TAPS] * d_conv
    gc_ref[TAPS - 1 : TAPS] += jnp.sum(d_conv * xbc, axis=0, keepdims=True)
    for back in range(1, TAPS):
        u = d_conv * mk[:, back - 1 : back]
        full = jnp.concatenate([u, head_scr[back - 1]], axis=0)
        head_scr[back - 1] = u[:8]
        d_xbc = d_xbc + cw[TAPS - 1 - back : TAPS - back] * pltpu.roll(full, CHUNK + 8 - back, 0)[:CHUNK]
        gc_ref[TAPS - 1 - back : TAPS - back] += jnp.sum(d_conv * moved[back - 1], axis=0, keepdims=True)
    gc_ref[4:5] += jnp.sum(d_conv, axis=0, keepdims=True)
    gc_ref[5:6, :inner] += jnp.sum(dy * xs, axis=0, keepdims=True)
    gc_ref[6:7, :inner] += d_gain
    dbc_ref[0] = d_xbc[:, inner:]
    dp_ref[0, :, LANES : LANES + inner] = dz.astype(BF)
    dp_ref[0, :, LANES + inner :] = d_xbc[:, :inner].astype(BF)
    d_rawt = jnp.transpose(jnp.concatenate([d_raw, jnp.zeros((LANES - 8, CHUNK), F32)], axis=0))
    dp_ref[0, :, :LANES] = d_rawt.astype(BF)


def mix_bwd(proj, marks, cw, hp, ys, sin, d_mid, scale, cube, gain, inner):
    rows, length, cols = proj.shape
    chunks = length // CHUNK
    bc = CONV_CH - DI
    at = lambda r, c: (r, chunks - 1 - c, 0)
    whole = lambda r, c: (0, 0)
    return pl.pallas_call(
        functools.partial(mix_bwd_kernel, inner, chunks),
        grid=(rows, chunks),
        in_specs=[
            pl.BlockSpec((1, CHUNK, cols), at),
            pl.BlockSpec((1, 8, cols), lambda r, c: (r, jnp.maximum((chunks - 1 - c) * (CHUNK // 8) - 1, 0), 0)),
            pl.BlockSpec(marks.shape, whole),
            pl.BlockSpec(cw.shape, whole),
            pl.BlockSpec(hp.shape, lambda r, c: (0, 0, 0)),
            pl.BlockSpec((1, CHUNK, inner), at),
            pl.BlockSpec((1, 1, STATE, inner), lambda r, c: (r, chunks - 1 - c, 0, 0)),
            pl.BlockSpec((1, CHUNK, inner), at),
            pl.BlockSpec(scale.shape, whole),
            pl.BlockSpec(cube.shape, whole),
            pl.BlockSpec(gain.shape, whole),
        ],
        out_specs=[
            pl.BlockSpec((1, CHUNK, 2 * inner + LANES), at),
            pl.BlockSpec((1, CHUNK, bc), at),
            pl.BlockSpec((8, inner + bc), whole),
            pl.BlockSpec((2, 8, CHUNK), lambda r, c: (0, 0, 0)),
        ],
        out_shape=[
            jax.ShapeDtypeStruct((rows, length, 2 * inner + LANES), BF),
            jax.ShapeDtypeStruct((rows, length, bc), F32),
            jax.ShapeDtypeStruct((8, inner + bc), F32),
            jax.ShapeDtypeStruct((2, 8, CHUNK), F32),
        ],
        scratch_shapes=[
            pltpu.VMEM((STATE, inner), F32),
            pltpu.VMEM((8, LANES), F32),
            pltpu.VMEM((TAPS - 1, 8, inner + bc), F32),
        ],
        compiler_params=pltpu.CompilerParams(
            dimension_semantics=("arbitrary", "arbitrary"), vmem_limit_bytes=60 * 2**20
        ),
        cost_estimate=pl.CostEstimate(flops=8 * 10**9, bytes_accessed=26 * 2**20, transcendentals=2 * 10**6),
    )(proj, proj, marks, cw, hp, ys, sin, d_mid, scale, cube, gain)


MESH = pl.DeviceIdType.MESH


def meet(peers):
    barrier = pltpu.get_barrier_semaphore()
    count = 0
    for here, peer in peers:
        if here is None:
            count = count + 1
            pl.semaphore_signal(barrier, inc=1, device_id=peer, device_id_type=MESH)
        else:
            count = count + here.astype(jnp.int32)

            @pl.when(here)
            def _():
                pl.semaphore_signal(barrier, inc=1, device_id=peer, device_id_type=MESH)

    pl.semaphore_wait(barrier, count)


def line_place(n_seq):
    me = lax.axis_index("seq")
    return me // 2, me % 2, {"seq": me + 1 - 2 * (me % 2)}, {"seq": me - 2}, {"seq": me + 2}


def line_peers(n):
    chip, core, sib, left, right = line_place(2 * n)
    return [(None, sib), (chip > 0, left), (chip < n - 1, right)]


def all_peers(axis, size):
    me = lax.axis_index(axis)
    return [(None, {axis: (me + k) % size}) for k in range(1, size)]


def remote(src, dst, send, recv, device):
    return pltpu.make_async_remote_copy(
        src_ref=src, dst_ref=dst, send_sem=send, recv_sem=recv, device_id=device, device_id_type=MESH
    )


def share_start(axis, size, source, slots, send, recv):
    me = lax.axis_index(axis)
    copies = []
    for k in range(1, size):
        to = (me + k) % size
        copy = remote(source(to), slots.at[k - 1], send.at[k - 1], recv.at[k - 1], {axis: to})
        copy.start()
        copies.append(copy)
    return copies


def share_sum(copies, own, slots):
    total = own.astype(F32)
    for k, copy in enumerate(copies):
        copy.wait_recv()
        total = total + slots[k].astype(F32)
    return total


def share_end(copies):
    for copy in copies:
        copy.wait_send()


def line_gather(n, rows, span, buf, sems, use, begun=None, between=None):
    right_s, left_s, sib_s, line_r, sib_r = sems
    chip, core, sib, left, right = line_place(2 * n)
    have_left, have_right = chip > 0, chip < n - 1

    def block(r, j, c):
        return buf.at[r, j, pl.ds(pl.multiple_of(c * span, span), span)]

    def to_sib(r, j, c):
        at = j * rows + r
        return remote(block(r, j, c), block(r, j, c), sib_s.at[at], sib_r.at[at], sib)

    def to_right(r, j):
        at = j * rows + r
        return remote(block(r, j, core), block(r, j, core), right_s.at[at], line_r.at[at], right)

    def to_left(r, j):
        at = j * rows + r
        return remote(block(r, j, core), block(r, j, core), left_s.at[at], line_r.at[at], left)

    def pass_on(r, j, way):
        if way >= 0:

            @pl.when(have_right)
            def _():
                to_right(r, j).start()

        if way <= 0:

            @pl.when(have_left)
            def _():
                to_left(r, j).start()

        to_sib(r, j, core).start()

    def finish(j):
        for r in range(rows):
            to_sib(r, j, 1 - core).wait_recv()
        use(j)

    for r in range(rows):
        pass_on(r, chip, 0)
    if begun is not None:
        begun()
    finish(chip)

    def step(t, _):
        low, high = chip - t, chip + t
        for r in range(rows):

            @pl.when(low >= 0)
            def _():
                to_right(r, low).wait_recv()
                pass_on(r, low, 1)

            @pl.when(high < n)
            def _():
                to_left(r, high).wait_recv()
                pass_on(r, high, -1)

        def one(k, _):
            j = jnp.where(k == 0, low, high)

            @pl.when((j >= 0) & (j < n))
            def _():
                finish(j)

            return 0

        lax.fori_loop(0, 2, one, 0)
        if between is not None:
            between(t)
        return 0

    lax.fori_loop(1, n, step, 0)

    def done(j, _):
        for r in range(rows):
            to_sib(r, j, core).wait_send()

            @pl.when(have_right & (j <= chip))
            def _():
                to_right(r, j).wait_send()

            @pl.when(have_left & (j >= chip))
            def _():
                to_left(r, j).wait_send()

        return 0

    lax.fori_loop(0, n, done, 0)


def line_sum(n, rows, emit, between, own, sib_out, sib_in, out, into, sems):
    sib_s, right_s, left_s, sib_r, right_r, left_r = sems
    chip, core, sib, left, right = line_place(2 * n)
    have_left, have_right = chip > 0, chip < n - 1

    def to_sib(j, r):
        at = j * rows + r
        return remote(sib_out.at[j, r], sib_in.at[j, r], sib_s.at[at], sib_r.at[at], sib)

    def to_right(j, r):
        at = j * rows + r
        return remote(out.at[j, r], into.at[j, r], right_s.at[at], right_r.at[at], right)

    def left_slot(j, owner):
        return jnp.where(j == owner, n, j)

    def to_left(j, r):
        at = j * rows + r
        return remote(out.at[j, r], into.at[left_slot(j, chip - 1), r], left_s.at[at], left_r.at[at], left)

    def from_right(j, r):
        at = j * rows + r
        return remote(out.at[j, r], into.at[left_slot(j, chip), r], left_s.at[at], left_r.at[at], right)

    def make(j):
        emit(j)
        for r in range(rows):
            to_sib(j, r).start()

    def right_j(tau):
        j = n - 1 - (tau - chip)
        return j, (tau >= chip) & (j > chip)

    def left_j(tau):
        j = tau - (n - 1 - chip)
        return j, (j >= 0) & (j < chip)

    def prepare(tau):
        def one(k, _):
            jr, on_r = right_j(tau)
            jl, on_l = left_j(tau)
            j = jnp.where(k == 0, jr, jl)

            @pl.when(((k == 0) & on_r) | ((k == 1) & on_l))
            def _():
                make(j)

            return 0

        lax.fori_loop(0, 2, one, 0)

    prepare(0)

    def step(tau, _):
        jr, on_r = right_j(tau)
        jl, on_l = left_j(tau)
        for r in range(rows):

            @pl.when(on_r)
            def _():
                to_sib(jr, r).wait_recv()

                @pl.when(have_left)
                def _():
                    to_right(jr, r).wait_recv()
                    out[jr, r] = (own[jr, r] + sib_in[jr, r].astype(F32) + into[jr, r].astype(F32)).astype(BF)

                @pl.when(chip == 0)
                def _():
                    out[jr, r] = (own[jr, r] + sib_in[jr, r].astype(F32)).astype(BF)

                to_right(jr, r).start()

            @pl.when(on_l)
            def _():
                to_sib(jl, r).wait_recv()

                @pl.when(have_right)
                def _():
                    from_right(jl, r).wait_recv()
                    out[jl, r] = (own[jl, r] + sib_in[jl, r].astype(F32) + into[jl, r].astype(F32)).astype(BF)

                @pl.when(chip == n - 1)
                def _():
                    out[jl, r] = (own[jl, r] + sib_in[jl, r].astype(F32)).astype(BF)

                to_left(jl, r).start()

        prepare(tau + 1)
        between(tau)
        return 0

    lax.fori_loop(0, n - 1, step, 0)
    make(chip)
    for r in range(rows):
        to_sib(chip, r).wait_recv()
        own[chip, r] = own[chip, r] + sib_in[chip, r].astype(F32)

        @pl.when(have_left)
        def _():
            to_right(chip, r).wait_recv()
            own[chip, r] = own[chip, r] + into[chip, r].astype(F32)

        @pl.when(have_right)
        def _():
            from_right(chip, r).wait_recv()
            own[chip, r] = own[chip, r] + into[n, r].astype(F32)

    def done(j, _):
        for r in range(rows):
            to_sib(j, r).wait_send()

            @pl.when(j > chip)
            def _():
                to_right(j, r).wait_send()

            @pl.when(j < chip)
            def _():
                to_left(j, r).wait_send()

        return 0

    lax.fori_loop(0, n, done, 0)


def halves(own, so, j, core, start, p, rows, span):
    stop = start + p.shape[1]
    for r in range(rows):
        low, high = p[r * CHUNK : r * CHUNK + span], p[r * CHUNK + span : (r + 1) * CHUNK]
        own[j, r, :, start:stop] = jnp.where(core == 0, low, high)
        so[j, r, :, start:stop] = jnp.where(core == 0, high, low).astype(BF)


def line_scratch(n, rows, span, wide):
    shape = (n, rows, span, wide)
    return [pltpu.VMEM(shape, F32)] + [pltpu.VMEM(shape, BF)] * 3 + [pltpu.VMEM((n + 1,) + shape[1:], BF)]


def dma(*counts):
    return [pltpu.SemaphoreType.DMA((count,)) for count in counts]


def dp_neighbours():
    d = lax.axis_index("dp")
    return d, d + 1 - 2 * (d % 2), (d + 2) % 4, 3 - d


def either(even, yes, no):
    @pl.when(even)
    def _():
        yes()

    @pl.when(jnp.logical_not(even))
    def _():
        no()


class Spread:
    def __init__(self, n_dp, at, count, sems):
        self.n_dp, self.at, self.count = n_dp, at, count
        self.s, self.r = sems

    @staticmethod
    def scratch(n_dp, count):
        return dma((n_dp - 1) * count, (n_dp - 1) * count)

    def copy(self, kind, owner, i, to):
        where = self.at(owner, i)
        sem = kind * self.count + i
        return remote(where, where, self.s.at[sem], self.r.at[sem], {"dp": to})

    def hand(self, i):
        d = lax.axis_index("dp")
        if self.n_dp == 4:
            d, x, y, _ = dp_neighbours()
            self.copy(0, d, i, x).start()
            self.copy(1, d, i, y).start()
        else:
            for k in range(1, self.n_dp):
                self.copy(k - 1, d, i, (d + k) % self.n_dp).start()

    def relay(self, i):
        if self.n_dp == 4:
            d, x, y, _ = dp_neighbours()

            def by_x():
                self.copy(0, x, i, x).wait_recv()
                self.copy(2, x, i, y).start()

            def by_y():
                self.copy(1, y, i, y).wait_recv()
                self.copy(2, y, i, x).start()

            either(i % 2 == 0, by_x, by_y)

    def end(self, i):
        d = lax.axis_index("dp")
        if self.n_dp == 4:
            d, x, y, across = dp_neighbours()

            def by_x():
                self.copy(1, y, i, y).wait_recv()
                self.copy(2, across, i, y).wait_recv()
                self.copy(2, x, i, y).wait_send()

            def by_y():
                self.copy(0, x, i, x).wait_recv()
                self.copy(2, across, i, x).wait_recv()
                self.copy(2, y, i, x).wait_send()

            either(i % 2 == 0, by_x, by_y)
            self.copy(0, d, i, x).wait_send()
            self.copy(1, d, i, y).wait_send()
        else:
            for k in range(1, self.n_dp):
                source = (d - k + self.n_dp) % self.n_dp
                self.copy(k - 1, source, i, source).wait_recv()
                self.copy(k - 1, d, i, (d + k) % self.n_dp).wait_send()


class DpSum:
    def __init__(self, n_dp, term, slots, piece, sems):
        self.n_dp, self.term, self.slots, self.piece = n_dp, term, slots, piece
        self.count = term.shape[1] // piece
        self.s, self.r = sems

    @staticmethod
    def scratch(n_dp, rows, cols, piece):
        count = (n_dp - 1) * (rows // piece)
        return [pltpu.VMEM((n_dp - 1, rows, cols), BF)] + dma(count, count)

    def rows_of(self, i):
        return pl.ds(pl.multiple_of(i * self.piece, self.piece), self.piece)

    def copy(self, kind, source, i, to):
        sem = kind * self.count + i
        return remote(source, self.slots.at[kind, self.rows_of(i)], self.s.at[sem], self.r.at[sem], {"dp": to})

    def part(self, kind, owner, i, to):
        return self.copy(kind, self.term.at[owner, self.rows_of(i)], i, to)

    def on(self, i):
        return self.copy(2, self.slots.at[1, self.rows_of(i)], i, self.axes(i)[1])

    def axes(self, i):
        d, x, y, across = dp_neighbours()
        even = i % 2 == 0
        return jnp.where(even, x, y), jnp.where(even, y, x), across, d

    def send(self, i):
        if self.n_dp == 4:
            first, second, across, d = self.axes(i)
            self.part(1, across, i, first).start()
            self.part(0, first, i, first).start()
        else:
            d = lax.axis_index("dp")
            for k in range(1, self.n_dp):
                to = (d + k) % self.n_dp
                self.part(k - 1, to, i, to).start()

    def middle(self, i):
        if self.n_dp == 4:
            first, second, across, d = self.axes(i)
            here = self.rows_of(i)
            self.part(1, across, i, first).wait_recv()
            self.slots[1, here] = (self.term[second, here].astype(F32) + self.slots[1, here].astype(F32)).astype(BF)
            self.on(i).start()

    def total(self, i):
        d = lax.axis_index("dp")
        here = self.rows_of(i)
        total = self.term[d, here].astype(F32)
        if self.n_dp == 4:
            first, second, across, d = self.axes(i)
            self.part(0, first, i, first).wait_recv()
            self.on(i).wait_recv()
            return total + self.slots[0, here].astype(F32) + self.slots[2, here].astype(F32)
        for k in range(1, self.n_dp):
            to = (d + k) % self.n_dp
            self.part(k - 1, to, i, to).wait_recv()
            total = total + self.slots[k - 1, here].astype(F32)
        return total

    def end(self, i):
        if self.n_dp == 4:
            first, second, across, d = self.axes(i)
            self.part(1, across, i, first).wait_send()
            self.part(0, first, i, first).wait_send()
            self.on(i).wait_send()
        else:
            d = lax.axis_index("dp")
            for k in range(1, self.n_dp):
                to = (d + k) % self.n_dp
                self.part(k - 1, to, i, to).wait_send()


class Pieces:
    def __init__(self, n_dp, n_seq, term, got, refs):
        self.n_seq, self.got = n_seq, got
        self.piece = got.shape[1]
        slots, dp_s, dp_r, self.sums, self.seq_s, self.seq_r = refs
        self.sum = DpSum(n_dp, term, slots, self.piece, (dp_s, dp_r))
        self.per = LANES // self.piece
        self.tiles = n_seq // self.per

    @staticmethod
    def scratch(n_dp, n_seq, rows, cols):
        piece = rows // n_seq
        return DpSum.scratch(n_dp, rows, cols, piece) + [pltpu.VMEM((n_seq, piece, cols), BF)] + dma(n_seq, n_seq)

    def tile(self, i):
        if 2 * self.tiles == self.n_seq:
            return (lax.axis_index("seq") // 2 + 1 + i) % self.tiles
        return i

    def each(self, i, act):
        def one(k, _):
            act(self.tile(i) * self.per + k)
            return 0

        lax.fori_loop(0, self.per, one, 0)

    def over_seq(self, s):
        me = lax.axis_index("seq")
        return remote(self.sums.at[s], self.got.at[me], self.seq_s.at[s], self.seq_r.at[me], {"seq": s})

    def from_seq(self, s):
        me = lax.axis_index("seq")
        return remote(self.sums.at[me], self.got.at[s], self.seq_s.at[me], self.seq_r.at[s], {"seq": s})

    def finish(self, s):
        me = lax.axis_index("seq")
        total = self.sum.total(s).astype(BF)

        def away():
            self.sums[s] = total
            self.over_seq(s).start()

        def stay():
            self.got[s] = total

        either(s != me, away, stay)

    def stage(self, q, product=None, sent=False):
        def one(k, _):
            i = 2 * q + k

            if not sent:

                @pl.when(i < self.tiles)
                def _():
                    product(self.tile(i))
                    self.each(i, self.sum.send)

            @pl.when((i >= 2) & (i - 2 < self.tiles))
            def _():
                self.each(i - 2, self.sum.middle)

            @pl.when((i >= 4) & (i - 4 < self.tiles))
            def _():
                self.each(i - 4, self.finish)

            return 0

        lax.fori_loop(0, 2, one, 0)

    def stages(self):
        return (self.tiles + 1) // 2 + 2

    def end(self):
        def one(s, _):
            self.sum.end(s)

            @pl.when(s != lax.axis_index("seq"))
            def _():
                self.over_seq(s).wait_send()
                self.from_seq(s).wait_recv()

            return 0

        lax.fori_loop(0, self.n_seq, one, 0)


class Shared:
    def __init__(self, n, n_dp, hid_ref, hcol, acc, low, slots, sems):
        self.n, self.n_dp, self.hid_ref = n, n_dp, hid_ref
        self.hcol, self.acc, self.low, self.slots = hcol, acc, low, slots
        self.load_sem, self.dp_s, self.dp_r = sems
        self.piece = low.shape[1]

    @staticmethod
    def scratch(n, n_dp, n_seq, rows, width, bc):
        piece = width // (n_dp * n_seq)
        return [
            pltpu.VMEM((n_dp, rows, n, CHUNK, LANES), BF),
            pltpu.VMEM((n_dp, LANES, bc), F32),
            pltpu.VMEM((n_dp, piece, bc), BF),
            pltpu.VMEM((n_dp - 1, piece, bc), BF),
        ] + dma(n_dp, n_dp - 1, n_dp - 1)

    def loads(self):
        at = lax.axis_index("seq") * self.piece // LANES * LANES
        group = self.hid_ref.shape[3] // self.n_dp
        return [
            pltpu.make_async_copy(
                self.hid_ref.at[:, :, :, pl.ds(pl.multiple_of(d * group + at, LANES), LANES)],
                self.hcol.at[d],
                self.load_sem.at[d],
            )
            for d in range(self.n_dp)
        ]

    def start(self):
        for copy in self.loads():
            copy.start()
        self.acc[...] = jnp.zeros_like(self.acc)

    def loaded(self):
        for copy in self.loads():
            copy.wait()

    def add(self, j, p_bc):
        for d in range(self.n_dp):
            h = self.hcol[d, :, j]
            self.acc[d] += dot(h.reshape(h.shape[0] * CHUNK, LANES), p_bc, TN)

    def send(self):
        base = lax.axis_index("seq") * self.piece
        at = pl.multiple_of(base - base // LANES * LANES, self.piece)
        for d in range(self.n_dp):
            self.low[d] = self.acc[d, pl.ds(at, self.piece)].astype(BF)
        self.copies = share_start("dp", self.n_dp, lambda to: self.low.at[to], self.slots, self.dp_s, self.dp_r)

    def total(self):
        return share_sum(self.copies, self.low[lax.axis_index("dp")], self.slots)

    def end(self):
        share_end(self.copies)


VMEM_SPEC = pl.BlockSpec(memory_space=pltpu.VMEM)
ANY_SPEC = pl.BlockSpec(memory_space=pl.ANY)


def comm_params(name):
    return pltpu.CompilerParams(collective_id=name, has_side_effects=True, vmem_limit_bytes=60 * 2**20)


def project_kernel(n, n_dp, fetch, x_ref, gain_ref, *refs):
    refs = list(refs)
    n_seq = 2 * n
    rows, span, width = x_ref.shape
    if fetch:
        parts_ref, wo_ref, marks_ref = refs[:3]
        hid_ref, proj_ref, w_ref, wout_ref, all_ref = refs[3:8]
        buf, wv, po = refs[8:11]
        line, (w_sem, hid_sem, out_sem) = refs[11:16], refs[16:19]
        a_s, a_r, p_s, p_r, o_s, o_r, m_s, m_r, mall = refs[19:]
    else:
        w_ref, hid_ref, proj_ref, buf, wv, po = refs[:6]
        line, (w_sem, hid_sem, out_sem) = refs[6:11], refs[11:]
    chip, core, sib, left, right = line_place(n_seq)
    me = lax.axis_index("seq")
    d = lax.axis_index("dp")
    if not fetch:
        load = pltpu.make_async_copy(w_ref, wv, w_sem.at[0])
        load.start()
    for r in range(rows):
        x = x_ref[r].astype(F32)
        scale = lax.rsqrt(jnp.mean(x * x, axis=-1, keepdims=True) + EPS)
        buf[r, chip, pl.ds(pl.multiple_of(core * span, span), span)] = (x * scale * gain_ref[...]).astype(BF)
    if fetch:
        meet(all_peers("seq", n_seq) + all_peers("dp", n_dp))
    else:
        meet(line_peers(n))
        load.wait()

    def out_copies(j):
        return (
            pltpu.make_async_copy(buf.at[:, j], hid_ref.at[:, j], hid_sem.at[j]),
            pltpu.make_async_copy(po.at[j], proj_ref.at[:, pl.ds(j * CHUNK, CHUNK)], out_sem.at[j]),
        )

    def use(j):
        block = buf[:, j].reshape(rows * CHUNK, width)
        res = dot(block, wv[...].reshape(width, wv.shape[-1]))
        for r in range(rows):
            po[j, r] = res[r * CHUNK : (r + 1) * CHUNK]
        for copy in out_copies(j):
            copy.start()

    def done(j, _):
        for copy in out_copies(j):
            copy.wait()
        return 0

    if not fetch:
        line_gather(n, rows, span, buf, line, use)
        lax.fori_loop(0, n, done, 0)
        return

    spread = Spread(n_dp, lambda owner, i: wv.at[owner, i], n_seq, (p_s, p_r))
    half = wo_ref.shape[0] // 2

    def half_of(owner, i):
        return wout_ref.at[owner, pl.ds(pl.multiple_of(i * half, half), half)]

    outs = Spread(n_dp, half_of, 2, (o_s, o_r))

    def across(i):
        to = (me + i) % n_seq
        return remote(parts_ref.at[to], wv.at[d, me], a_s.at[to], a_r.at[me], {"seq": to})

    def arrival(i):
        source = (me - i + n_seq) % n_seq
        return remote(parts_ref.at[me], wv.at[d, source], a_s.at[me], a_r.at[source], {"seq": source})

    def marks_copy(i):
        to = (me + i) % n_seq
        return remote(marks_ref, mall.at[me], m_s.at[to], m_r.at[me], {"seq": to})

    def marks_in(i):
        source = (me - i + n_seq) % n_seq
        return remote(marks_ref, mall.at[source], m_s.at[me], m_r.at[source], {"seq": source})

    def place(i):
        return (me - i + n_seq) % n_seq

    def go(i, _):
        across(i).start()
        return 0

    lax.fori_loop(1, n_seq, go, 0)
    wv[d, me] = parts_ref[me]
    spread.hand(me)
    for i in range(1, n_seq):
        marks_copy(i).start()
    mall[me] = marks_ref[...]

    def begun():
        def one(i, _):
            arrival(i).wait_recv()
            spread.hand(place(i))

            @pl.when(i >= 2)
            def _():
                spread.relay(place(i - 2))

            return 0

        lax.fori_loop(1, n_seq, one, 0)
        wout_ref[d] = wo_ref[...]
        for i in range(2):
            outs.hand(i)
        spread.relay(place(n_seq - 2))
        spread.relay(place(n_seq - 1))

    line_gather(n, rows, span, buf, line, lambda j: None, begun)
    for i in range(1, n_seq):
        marks_in(i).wait_recv()
    for r in range(rows):
        for j in range(n):
            all_ref[r * n + j : r * n + j + 1] = mall[2 * j, r : r + 1] + mall[2 * j + 1, r : r + 1]
    for i in range(2):
        outs.relay(i)

    def ended(i, _):
        spread.end(i)
        return 0

    lax.fori_loop(0, n_seq, ended, 0)
    keep = pltpu.make_async_copy(wv, w_ref, w_sem.at[0])
    keep.start()

    def each(j, _):
        use(j)
        return 0

    lax.fori_loop(0, n, each, 0)
    for i in range(2):
        outs.end(i)

    def sent(i, _):
        across(i).wait_send()
        marks_copy(i).wait_send()
        return 0

    lax.fori_loop(1, n_seq, sent, 0)
    lax.fori_loop(0, n, done, 0)
    keep.wait()


def project(x, gain, w, n_seq):
    return project_call(x, gain, w.shape, (w,), None, n_seq)


def project_fetch(x, gain, parts, wo, marks, n_dp, n_seq):
    piece, cols = parts.shape[1:]
    return project_call(x, gain, (n_dp, n_seq, piece, cols), (parts, wo, marks), n_dp, n_seq)


def project_call(x, gain, w_shape, more, n_dp, n_seq):
    rows, span, width = x.shape
    n = n_seq // 2
    k = n * rows
    cols = w_shape[-1]
    outs = [
        jax.ShapeDtypeStruct((rows, n, CHUNK, width), BF),
        jax.ShapeDtypeStruct((rows, n * CHUNK, cols), F32),
    ]
    scratch = [
        pltpu.VMEM((rows, n, CHUNK, width), BF),
        pltpu.VMEM(w_shape, BF),
        pltpu.VMEM((n, rows, CHUNK, cols), F32),
    ] + dma(k, k, k, k, k, 1, n, n)
    in_specs = [VMEM_SPEC, VMEM_SPEC, ANY_SPEC]
    out_specs = [ANY_SPEC, ANY_SPEC]
    if n_dp is not None:
        parts, wo, marks = more
        in_specs = [VMEM_SPEC] * 5
        out_specs += [ANY_SPEC, VMEM_SPEC, VMEM_SPEC]
        outs += [
            jax.ShapeDtypeStruct(w_shape, BF),
            jax.ShapeDtypeStruct((n_dp,) + wo.shape, BF),
            jax.ShapeDtypeStruct((k, CHUNK), F32),
        ]
        scratch += dma(n_seq, n_seq) + Spread.scratch(n_dp, n_seq) + Spread.scratch(n_dp, 2) + dma(n_seq, n_seq)
        scratch += [pltpu.VMEM((n_seq,) + marks.shape, F32)]
    return pl.pallas_call(
        functools.partial(project_kernel, n, n_dp, n_dp is not None),
        in_specs=in_specs,
        out_specs=out_specs,
        out_shape=outs,
        scratch_shapes=scratch,
        compiler_params=comm_params(0 if n_dp is None else 7),
        cost_estimate=pl.CostEstimate(flops=6 * 10**9, bytes_accessed=20 * 2**20, transcendentals=0),
    )(x, gain, *more)


def branch_kernel(n, gated_ref, ss_ref, gain_ref, w_ref, x_ref, y_ref, mid_ref, scale_ref, own, so, si, lo, li, slots, *sems):
    rows, span, width = x_ref.shape
    line, (share_s, share_r) = sems[:6], sems[6:]
    chip, core, sib, left, right = line_place(2 * n)
    meet(all_peers("seq", 2 * n))
    copies = share_start("seq", 2 * n, lambda to: ss_ref, slots, share_s, share_r)
    total = share_sum(copies, ss_ref[...], slots)
    scale = lax.rsqrt(total / DI + EPS)
    scale_ref[...] = scale
    cols = jnp.transpose(scale)
    for r in range(rows):
        for k in range(n):
            at = r * n + k
            g = gated_ref[r, k * CHUNK : (k + 1) * CHUNK]
            mid_ref[r, k * CHUNK : (k + 1) * CHUNK] = (g * cols[:, at : at + 1] * gain_ref[...]).astype(BF)

    def emit(j):
        here = pl.ds(pl.multiple_of(j * CHUNK, CHUNK), CHUNK)
        block = jnp.concatenate([mid_ref[r, here] for r in range(rows)], axis=0)
        for at in range(0, width, 512):
            halves(own, so, j, core, at, dot(block, w_ref[:, at : at + 512]), rows, span)

    line_sum(n, rows, emit, lambda tau: None, own, so, si, lo, li, line)
    for r in range(rows):
        y_ref[r] = x_ref[r] + own[chip, r]
    share_end(copies)


def branch(gated, ss, gain, w, x, n_seq):
    rows, span, width = x.shape
    n = n_seq // 2
    k = n * rows
    return pl.pallas_call(
        functools.partial(branch_kernel, n),
        in_specs=[VMEM_SPEC] * 5,
        out_specs=[VMEM_SPEC] * 3,
        out_shape=[
            jax.ShapeDtypeStruct(x.shape, F32),
            jax.ShapeDtypeStruct(gated.shape, BF),
            jax.ShapeDtypeStruct(ss.shape, F32),
        ],
        scratch_shapes=line_scratch(n, rows, span, width)
        + [pltpu.VMEM((n_seq - 1,) + ss.shape, F32)]
        + dma(k, k, k, k, k, k, n_seq - 1, n_seq - 1),
        compiler_params=comm_params(1),
        cost_estimate=pl.CostEstimate(flops=3 * 10**9, bytes_accessed=10 * 2**20, transcendentals=0),
    )(gated, ss, gain, w, x)


def back_branch_kernel(n, n_dp, later, given, *refs):
    n_seq = 2 * n
    refs = list(refs)
    g_ref, w_ref, mid_ref, gated_ref, gain_ref, scale_ref = refs[:6]
    refs = refs[6:]
    if later:
        pbc_ref, hid_ref, term_ref = refs[:3]
        refs = refs[3:]
    dmid_ref, gw_ref, cube_ref = refs[:3]
    refs = refs[3:]
    if later:
        got_ref, bc_ref = refs[:2]
        refs = refs[2:]
    buf, acc, tot, slots = refs[:4]
    line, (share_s, share_r) = refs[4:9], refs[9:11]
    refs = refs[11:]
    rows, span, width = g_ref.shape[-3:]
    chip, core, sib, left, right = line_place(n_seq)
    here = pl.ds(pl.multiple_of(core * span, span), span)
    peers = all_peers("seq", n_seq)
    if later:
        shared = Shared(n, n_dp, hid_ref, *refs[:4], refs[4:7])
        refs = refs[7:]
        pieces = Pieces(n_dp, n_seq, term_ref, got_ref, refs[:6])
        shared.start()
        peers = peers + all_peers("dp", n_dp)
    for r in range(0 if given else rows):
        buf[r, chip, here, :width] = g_ref[r].astype(BF)
        if later:
            buf[r, chip, here, width:] = pbc_ref[r]
    acc[...] = jnp.zeros_like(acc)
    ones = jnp.ones((8, mid_ref.shape[2]), F32)
    meet(peers)
    if later:

        def send(i, _):
            pieces.each(i, pieces.sum.send)
            return 0

        lax.fori_loop(0, pieces.tiles, send, 0)
        shared.loaded()

    def use(j):
        chunk = pl.ds(pl.multiple_of(j * CHUNK, CHUNK), CHUNK)
        if given:
            block = jnp.concatenate([g_ref[2 * j + c, r] for r in range(rows) for c in range(2)], axis=0)
        else:
            block = buf[:, j, :, :width].reshape(rows * CHUNK, width)
        res = dot(block, w_ref[...], NT)
        left_side = jnp.concatenate([mid_ref[r, chunk] for r in range(rows)], axis=0)
        for k in range(0, width, 512):
            acc[:, k : k + 512] += dot(left_side, block[:, k : k + 512], TN)
        for r in range(rows):
            part = res[r * CHUNK : (r + 1) * CHUNK]
            dmid_ref[r, chunk] = part
            v = part * gain_ref[...] * gated_ref[r, chunk]
            tot[pl.ds(r * n + j, 1)] = dot(ones, v, NT, HIGH)[:1]
        if later:
            shared.add(j, buf[:, j, :, width:].reshape(rows * CHUNK, buf.shape[3] - width))

    def between(t):
        if later:
            pieces.stage(t, sent=True)

    if given:

        def each(j, _):
            use(j)
            return 0

        lax.fori_loop(0, n, each, 0)
    else:
        line_gather(n, rows, span, buf, line, use, None, between)
    copies = share_start("seq", n_seq, lambda to: tot, slots, share_s, share_r)
    if later:
        shared.send()
        for q in range(n, pieces.stages()):
            pieces.stage(q, sent=True)
    total = share_sum(copies, tot[...], slots)
    scale = scale_ref[...]
    cube_ref[...] = scale * scale * scale * (total / DI)
    gw_ref[...] = acc[...].astype(BF)
    if later:
        bc_ref[...] = shared.total()
        pieces.end()
        shared.end()
    share_end(copies)


def back_branch(g, w, mid, gated, gain, scale, later, n_dp, n_seq):
    rows, span, width = g.shape[-3:]
    given = len(g.shape) == 4
    n = n_seq // 2
    k = n * rows
    inner = gated.shape[2]
    extra = 0
    outs = [
        jax.ShapeDtypeStruct(gated.shape, F32),
        jax.ShapeDtypeStruct((inner, width), BF),
        jax.ShapeDtypeStruct(scale.shape, F32),
    ]
    more = []
    in_specs = [VMEM_SPEC] * 6
    if later is not None:
        p_bc, hidden, term = later
        extra = p_bc.shape[2]
        piece = width // (n_dp * n_seq)
        outs += [
            jax.ShapeDtypeStruct((n_seq, piece, term.shape[2]), BF),
            jax.ShapeDtypeStruct((piece, extra), F32),
        ]
        more = Shared.scratch(n, n_dp, n_seq, rows, width, extra)
        more += Pieces.scratch(n_dp, n_seq, term.shape[1], term.shape[2])
        in_specs += [VMEM_SPEC, ANY_SPEC, VMEM_SPEC]
    return pl.pallas_call(
        functools.partial(back_branch_kernel, n, n_dp, later is not None, given),
        in_specs=in_specs,
        out_specs=[VMEM_SPEC] * len(outs),
        out_shape=outs,
        scratch_shapes=[
            pltpu.VMEM((rows, 1 if given else n, CHUNK, width + extra), BF),
            pltpu.VMEM((inner, width), F32),
            pltpu.VMEM(scale.shape, F32),
            pltpu.VMEM((n_seq - 1,) + scale.shape, F32),
        ]
        + dma(k, k, k, k, k, n_seq - 1, n_seq - 1)
        + more,
        compiler_params=comm_params(2 if later is None else 4),
        cost_estimate=pl.CostEstimate(flops=6 * 10**9, bytes_accessed=16 * 2**20, transcendentals=0),
    )(g, w, mid, gated, gain, scale, *(later or ()))


def back_project_kernel(n, n_dp, final, with_out, dp_ref, dbc_ref, w_ref, x_ref, g_ref, gain_ref, hid_ref, *refs):
    n_seq = 2 * n
    refs = list(refs)
    if with_out:
        gw_ref = refs.pop(0)
    out_ref, dgain_ref, pbc_ref, term_ref = refs[:4]
    refs = refs[4:]
    if with_out:
        gout_ref = refs.pop(0)
    hid, own, so, si, lo, li, hid_sem = refs[:7]
    line = refs[7:13]
    refs = refs[13:]
    rows, span, width = x_ref.shape
    bc = dbc_ref.shape[2]
    part = dp_ref.shape[2]
    group = width // n_dp
    chip, core, sib, left, right = line_place(n_seq)
    load = pltpu.make_async_copy(hid_ref, hid, hid_sem.at[0])
    load.start()
    peers = line_peers(n)
    if with_out:
        outs = DpSum(n_dp, gw_ref, refs[0], gw_ref.shape[1] // 2, refs[1:3])
        refs = refs[3:]
    if final:
        term = refs.pop(0)
        pieces = Pieces(n_dp, n_seq, term, term_ref, refs[:6])
        peers = all_peers("seq", n_seq)
    else:
        term = term_ref
    if final or with_out:
        peers = peers + all_peers("dp", n_dp)
    meet(peers)
    if with_out:
        for i in range(2):
            outs.send(i)

    def emit(j):
        here = pl.ds(pl.multiple_of(j * CHUNK, CHUNK), CHUNK)
        block = jnp.concatenate([dp_ref[r, here] for r in range(rows)], axis=0)
        for at in range(0, width, 512):
            halves(own, so, j, core, at, dot(block, w_ref[at : at + 512, :part], NT), rows, span)
        halves(own, so, j, core, width, jnp.concatenate([dbc_ref[r, here] for r in range(rows)], axis=0), rows, span)

    def product(tile):
        right_side = dp_ref[...].reshape(rows * n * CHUNK, part)

        def one(owner, _):
            col = pl.ds(pl.multiple_of(owner * group + tile * LANES, LANES), LANES)
            h = hid[:, :, :, col].reshape(rows * n * CHUNK, LANES)
            term[owner, pl.ds(pl.multiple_of(tile * LANES, LANES), LANES)] = dot(h, right_side, TN).astype(BF)
            return 0

        lax.fori_loop(0, n_dp, one, 0)

    tiles = group // LANES

    def stage(q):
        if final:
            pieces.stage(q, product)
        else:

            def one(k, _):
                @pl.when(2 * q + k < tiles)
                def _():
                    product(2 * q + k)

                return 0

            lax.fori_loop(0, 2, one, 0)

    def between(tau):
        @pl.when(tau == 0)
        def _():
            load.wait()

        stage(tau)
        if with_out:

            @pl.when(tau == 1)
            def _():
                for i in range(2):
                    outs.middle(i)

    line_sum(n, rows, emit, between, own, so, si, lo, li, line)
    for q in range(n - 1, pieces.stages() if final else (tiles + 1) // 2):
        stage(q)
    d_gain = jnp.zeros((1, width), F32)
    for r in range(rows):
        p_bc = own[chip, r, :, width:].astype(BF)
        pbc_ref[r] = p_bc
        d_hid = own[chip, r, :, :width] + dot(p_bc, w_ref[:, part:], NT)
        x = x_ref[r]
        scale = lax.rsqrt(jnp.mean(x * x, axis=-1, keepdims=True) + EPS)
        m = d_hid * gain_ref[...]
        mean = jnp.mean(m * x, axis=-1, keepdims=True)
        out_ref[r] = g_ref[r] + scale * m - x * (scale * scale * scale * mean)
        d_gain = d_gain + jnp.sum(d_hid * x * scale, axis=0, keepdims=True)
    dgain_ref[...] = d_gain
    if with_out:
        for i in range(2):
            gout_ref[outs.rows_of(i)] = outs.total(i)
            outs.end(i)
    if final:
        pieces.end()


def back_project(dp, dbc, w, x, g, gain, hidden, gw, final, n_dp, n_seq):
    rows, span, width = x.shape
    n = n_seq // 2
    k = n * rows
    bc, part = dbc.shape[2], dp.shape[2]
    group = width // n_dp
    with_out = gw is not None
    whole_term = (n_dp, group, part)
    outs = [
        jax.ShapeDtypeStruct(x.shape, F32),
        jax.ShapeDtypeStruct((1, width), F32),
        jax.ShapeDtypeStruct((rows, span, bc), BF),
        jax.ShapeDtypeStruct((n_seq, group // n_seq, part) if final else whole_term, BF),
    ]
    more = []
    if with_out:
        outs.append(jax.ShapeDtypeStruct(gw.shape[1:], F32))
        more += DpSum.scratch(n_dp, gw.shape[1], gw.shape[2], gw.shape[1] // 2)
    if final:
        more += [pltpu.VMEM(whole_term, BF)] + Pieces.scratch(n_dp, n_seq, group, part)
    return pl.pallas_call(
        functools.partial(back_project_kernel, n, n_dp, final, with_out),
        in_specs=[VMEM_SPEC] * 6 + [ANY_SPEC] + [VMEM_SPEC] * with_out,
        out_specs=[VMEM_SPEC] * len(outs),
        out_shape=outs,
        scratch_shapes=[pltpu.VMEM(hidden.shape, BF)]
        + line_scratch(n, rows, span, width + bc)
        + dma(1, k, k, k, k, k, k)
        + more,
        compiler_params=comm_params(5 if final else 3),
        cost_estimate=pl.CostEstimate(flops=11 * 10**9, bytes_accessed=24 * 2**20, transcendentals=0),
    )(dp, dbc, w, x, g, gain, hidden, *([gw] if with_out else []))


def small_kernel(n, n_dp, vec_ref, pbc_ref, hid_ref, vall_ref, bc_ref, pall, vslots, *refs):
    n_seq = 2 * n
    rows, span, bc = pbc_ref.shape
    size = vec_ref.shape[0]
    chip, core, sib, left, right = line_place(n_seq)
    p_line, v_line, (v_s, v_r) = refs[:5], refs[5:10], refs[10:12]
    shared = Shared(n, n_dp, hid_ref, *refs[12:16], refs[16:19])
    shared.start()
    for r in range(rows):
        pall[r, chip, pl.ds(pl.multiple_of(core * span, span), span)] = pbc_ref[r]
    meet(line_peers(n) + all_peers("dp", n_dp))
    over_dp = share_start("dp", n_dp, lambda to: vec_ref, vslots, v_s, v_r)
    line_gather(
        n, rows, span, pall, p_line, lambda j: shared.add(j, pall[:, j].reshape(rows * CHUNK, bc)), shared.loaded
    )
    shared.send()
    vall_ref[0, chip, pl.ds(pl.multiple_of(core * size, size), size)] = share_sum(over_dp, vec_ref[...], vslots)
    line_gather(n, 1, size, vall_ref, v_line, lambda j: None)
    bc_ref[...] = shared.total()
    share_end(over_dp)
    shared.end()


def small_sums(vec, p_bc, hidden, n_dp, n_seq):
    rows, span, bc = p_bc.shape
    n = n_seq // 2
    k = n * rows
    width = hidden.shape[3]
    return pl.pallas_call(
        functools.partial(small_kernel, n, n_dp),
        in_specs=[VMEM_SPEC, VMEM_SPEC, ANY_SPEC],
        out_specs=[VMEM_SPEC] * 2,
        out_shape=[
            jax.ShapeDtypeStruct((1, n, 2 * vec.shape[0], LANES), F32),
            jax.ShapeDtypeStruct((width // (n_dp * n_seq), bc), F32),
        ],
        scratch_shapes=[
            pltpu.VMEM((rows, n, CHUNK, bc), BF),
            pltpu.VMEM((n_dp - 1,) + vec.shape, F32),
        ]
        + dma(k, k, k, k, k, n, n, n, n, n, n_dp - 1, n_dp - 1)
        + Shared.scratch(n, n_dp, n_seq, rows, width, bc),
        compiler_params=comm_params(6),
    )(vec, p_bc, hidden)


def arrange_kernel(groups, own_heads, got0, got1, bc0, bc1, vall_ref, gin_ref, gain_ref, mid_ref, cw_ref, cb_ref, dtb_ref, al_ref, ds_ref):
    n_seq = got0.shape[0]
    inner = DI // n_seq
    bc = CONV_CH - DI
    cols = inner // groups
    per = own_heads // groups
    for level, (got, bcs) in enumerate(((got0, bc0), (got1, bc1))):
        dts = jnp.zeros((got.shape[1], HEADS), F32)
        for s in range(n_seq):
            dts = dts + dot(got[s, :, :LANES].astype(F32), head_place(LANES, s, n_seq, own_heads, per), precision=HIGH)
            for g in range(groups):
                at = (g * n_seq + s) * cols
                for kind in range(2):
                    src = LANES + kind * inner + g * cols
                    gin_ref[level, :, kind * DI + at : kind * DI + at + cols] = got[s, :, src : src + cols].astype(F32)
        gin_ref[level, :, 2 * DI : 2 * DI + bc] = bcs[...]
        gin_ref[level, :, 2 * DI + bc :] = dts
    wide = (inner + bc) // LANES
    for level in range(2):
        base = level * (8 * wide + 16 + gain_ref.shape[1] // LANES)
        total = jnp.zeros((8, bc), F32)
        heads = [jnp.zeros((1, HEADS), F32)] * 3
        for s in range(n_seq):
            place = head_place(8, s, n_seq, own_heads, per)
            tiles = [vall_ref[s, base + 8 * t : base + 8 * t + 8] for t in range(wide)]
            for g in range(groups):
                for t in range(cols // LANES):
                    tile = tiles[g * cols // LANES + t]
                    at = (g * n_seq + s) * cols + t * LANES
                    cw_ref[level, :, at : at + LANES] = tile[:TAPS]
                    cb_ref[level : level + 1, at : at + LANES] = tile[4:5]
                    mid_ref[level : level + 1, at : at + LANES] = tile[6:7]
            total = total + jnp.concatenate(tiles[inner // LANES :], axis=1)
            skip = jnp.concatenate(tiles[: inner // LANES], axis=1)
            skip = dot(skip, head_matrix(inner), NT, HIGH)
            heads[2] = heads[2] + dot(skip, place, precision=HIGH)[5:6]
            for kind in range(2):
                at = base + 8 * wide + 8 * kind
                row = dot(jnp.ones((8, LANES), F32), vall_ref[s, at : at + 8], NT, HIGH)
                heads[kind] = heads[kind] + dot(row, place, precision=HIGH)[:1]
        cw_ref[level, :, DI:] = total[:TAPS]
        cb_ref[level : level + 1, DI:] = total[4:5]
        for ref, value in zip((dtb_ref, al_ref, ds_ref), heads):
            ref[level : level + 1] = value
        at = base + 8 * wide + 16
        tiles = gain_ref.shape[1] // LANES
        gains = vall_ref[0, at : at + tiles]
        for s in range(1, n_seq):
            gains = gains + vall_ref[s, at : at + tiles]
        for t in range(tiles):
            gain_ref[level : level + 1, t * LANES : (t + 1) * LANES] = gains[t : t + 1]


def head_place(size, s, n_seq, own_heads, per):
    i = lax.broadcasted_iota(jnp.int32, (size, HEADS), 0)
    h = lax.broadcasted_iota(jnp.int32, (size, HEADS), 1)
    return ((i < own_heads) & (h == (i // per * n_seq + s) * per + i % per)).astype(F32)


def arrange(gots, bcs, vall, groups, own_heads, width):
    piece = gots[0].shape[1]
    shapes = [
        (2, piece, 2 * DI + CONV_CH - DI + HEADS),
        (2, width),
        (2, DI),
        (2, TAPS, CONV_CH),
        (2, CONV_CH),
        (2, HEADS),
        (2, HEADS),
        (2, HEADS),
    ]
    return pl.pallas_call(
        functools.partial(arrange_kernel, groups, own_heads),
        in_specs=[VMEM_SPEC] * 5,
        out_specs=[VMEM_SPEC] * 8,
        out_shape=[jax.ShapeDtypeStruct(shape, F32) for shape in shapes],
        compiler_params=pltpu.CompilerParams(vmem_limit_bytes=40 * 2**20),
    )(*gots, *bcs, vall)


def split_cols(x, groups, size):
    cols = x.shape[-1] // (groups * size)
    x = x.reshape(x.shape[:-1] + (groups, size, cols))
    x = jnp.moveaxis(x, -2, 0)
    return x.reshape(x.shape[:-2] + (groups * cols,))


def shards(
    tokens, resets, cotangent, w_in, w_out, gain_in, gain_mid, conv_w, conv_b, dt_bias, a_log, d_skip
):
    rows, span, width = tokens.shape
    layers = w_in.shape[0]
    n_dp, n_seq = lax.axis_size("dp"), lax.axis_size("seq")
    place = lax.axis_index("seq")
    length = span * n_seq
    own_heads = HEADS // n_seq
    groups = n_dp if own_heads % n_dp == 0 else 1
    inner = DI // n_seq
    bc_all = CONV_CH - DI
    part = LANES + 2 * inner

    part_z = split_cols(w_in[..., :DI], groups, n_seq)
    part_x = split_cols(w_in[..., DI : 2 * DI], groups, n_seq)
    part_bc = jnp.broadcast_to(w_in[..., 2 * DI : DI + CONV_CH], (n_seq,) + w_in.shape[:2] + (bc_all,))
    part_dt = split_cols(w_in[..., DI + CONV_CH :], groups, n_seq)
    part_dt = jnp.pad(part_dt, ((0, 0),) * 3 + ((0, LANES - own_heads),))
    parts = jnp.concatenate([part_dt, part_z, part_x, part_bc], axis=-1)
    cols = parts.shape[-1]
    marks = jnp.pad(resets.astype(F32), ((0, 8 - rows), (0, CHUNK - span)))
    marks = jnp.where(place % 2 == 0, marks, jnp.roll(marks, span, axis=1))

    def columns(x, by_head):
        x = split_cols(x, groups, n_seq)
        x = lax.dynamic_index_in_dim(x, place, 0, False)
        return jnp.repeat(x, HEAD, axis=-1) if by_head else x

    taps = jnp.concatenate([conv_w, conv_b[:, None]], axis=1)
    rest = jnp.concatenate([d_skip[:, None], jnp.zeros((layers, 2, HEADS), F32)], axis=1)
    cws = jnp.concatenate([columns(taps[..., :DI], False), columns(rest, True)], axis=1)
    cws = jnp.concatenate([cws, jnp.pad(taps[..., DI:], ((0, 0), (0, 7 - TAPS), (0, 0)))], axis=2)
    hps = columns(jnp.stack([dt_bias, a_log], axis=1), False)
    hps = jnp.broadcast_to(jnp.pad(hps, ((0, 0), (0, 0), (0, 8 - own_heads)))[..., None], (layers, 2, 8, LANES))
    gains = columns(gain_mid[:, None], False)

    def swapped(pieces):
        out = [lax.dynamic_index_in_dim(pieces, place, 0, False)]
        for k in range(1, n_seq):
            away = lax.dynamic_index_in_dim(pieces, (place + k) % n_seq, 0, False)
            out.append(lax.ppermute(away, "seq", [(i, (i + k) % n_seq) for i in range(n_seq)]))
        return jnp.take(jnp.stack(out), (place - jnp.arange(n_seq)) % n_seq, axis=0)

    def whole_rows(w):
        return lax.dynamic_slice_in_dim(lax.all_gather(w, BOTH, axis=0, tiled=True), place * inner, inner, 0)

    resid = tokens.astype(F32)
    stored = []
    for level in range(layers):
        cw, hp, gain = cws[level], hps[level], gains[level]
        before = resid
        if level == 0:
            hidden, proj, w_all, wo_all, marks_all = project_fetch(
                before, gain_in[level][None], parts[:, level], w_out[level], marks, n_dp, n_seq
            )
            win = [w_all.reshape(width, cols)]
            wout = [wo_all.reshape(DI // n_seq, width) if groups == n_dp else whole_rows(w_out[level])]
            proj, later_parts, later_out, own_cot = lax.optimization_barrier(
                (proj, parts[:, 1:], w_out[1:], cotangent)
            )
            cot = lax.all_gather(own_cot, "seq")
            for k in range(layers - 1):
                win.append(lax.all_gather(swapped(later_parts[:, k]), "dp").reshape(width, cols))
                if groups == n_dp:
                    wout.append(lax.all_gather(later_out[k], "dp", axis=0, tiled=True))
                else:
                    wout.append(whole_rows(later_out[k]))
        else:
            hidden, proj = project(before, gain_in[level][None], win[level], n_seq)
        gated, squares, ys, sin = mix_fwd(proj, marks_all, cw, hp, inner)
        resid, mid, scale = branch(gated, squares, gain, wout[level], before, n_seq)
        stored.append((before, hidden, proj, cw, hp, gain, gated, ys, sin, mid, scale))
    outputs = resid.astype(BF)
    grad = cotangent.astype(F32)
    gots = [None] * layers
    bcs = [None] * layers
    grads_out = [None] * layers
    smalls = [None] * layers
    later = None
    for level in reversed(range(layers)):
        before, hidden, proj, cw, hp, gain, gated, ys, sin, mid, scale = stored[level]
        d_mid, out_term, cube, *rest = back_branch(
            cot if level == layers - 1 else grad, wout[level], mid, gated, gain, scale, later, n_dp, n_seq
        )
        if later is not None:
            gots[level + 1], bcs[level + 1] = rest
        gw = None
        if groups == n_dp:
            gw = out_term.reshape(n_dp, inner // n_dp, width)
        else:
            padded = jnp.zeros((DI, width), BF)
            padded = lax.dynamic_update_slice_in_dim(padded, out_term, place * inner, 0)
            grads_out[level] = lax.psum_scatter(padded, BOTH, scatter_dimension=0, tiled=True).astype(F32)
        d_proj, d_bc, gc, gh = mix_bwd(proj, marks_all, cw, hp, ys, sin, d_mid, scale, cube, gain, inner)
        grad, d_gain_in, p_bc, term, *rest = back_project(
            d_proj, d_bc, win[level], before, grad, gain_in[level][None], hidden, gw, level == 0, n_dp, n_seq
        )
        if gw is not None:
            grads_out[level] = rest[0]
        later = (p_bc, hidden, term)
        tiles = [jnp.moveaxis(gc.reshape(8, -1, LANES), 1, 0).reshape(-1, LANES), gh.reshape(-1, LANES)]
        smalls[level] = jnp.concatenate(tiles + [d_gain_in.reshape(-1, LANES)], axis=0)
    gots[0] = term
    vall, bcs[0] = small_sums(jnp.concatenate(smalls, axis=0), p_bc, hidden, n_dp, n_seq)
    vall = vall.reshape(n_seq, -1, LANES)
    grads_in, *ends = arrange(gots, bcs, vall, groups, own_heads, width)
    return (outputs, grad, grads_in, jnp.stack(grads_out), *ends)


def solution(mesh):
    placed = (
        P("dp", "seq", None),
        P("dp", "seq"),
        P("dp", "seq", None),
        P(None, BOTH, None),
        P(None, BOTH, None),
    ) + (P(),) * 7
    return jax.shard_map(
        shards,
        mesh=mesh,
        in_specs=placed,
        out_specs=(
            P("dp", "seq", None),
            P("dp", "seq", None),
            P(None, BOTH, None),
            P(None, BOTH, None),
        )
        + (P(),) * 7,
        check_vma=False,
    )
```

```python
import functools

import jax
import jax.numpy as jnp
from jax import lax
from jax.experimental import pallas as pl
from jax.experimental.pallas import tpu as pltpu
from jax.sharding import PartitionSpec as P

HEADS = 64
HEAD = 64
STATE = 128
DI = 4096
CONV_CH = 4352
CHUNK = 128
LANES = 128
TAPS = 4
EPS = 1e-05
HIGH = lax.Precision.HIGHEST
BF = jnp.bfloat16
F32 = jnp.float32
FAR = -1e30
BOTH = ("dp", "seq")


def dot(a, b, dims=((1,), (0,)), precision=None):
    return lax.dot_general(a, b, (dims, ((), ())), preferred_element_type=F32, precision=precision)


NT = ((1,), (1,))
TN = ((0,), (0,))


def head_matrix(inner):
    row = lax.broadcasted_iota(jnp.int32, (8, inner), 0)
    col = lax.broadcasted_iota(jnp.int32, (8, inner), 1)
    return (col // HEAD == row).astype(F32)


def parts_of(x, count):
    parts = []
    for _ in range(count - 1):
        part = x.astype(BF).astype(F32)
        parts.append(part)
        x = x - part
    parts.append(x)
    return jnp.concatenate(parts, axis=0)


def spread(rows, inner):
    heads = head_matrix(inner)
    return dot(parts_of(rows, 2).astype(BF), jnp.concatenate([heads, heads], axis=0).astype(BF), TN)


def by_head(heads, x):
    heads = heads.astype(BF)
    high = x.astype(BF)
    return dot(heads, high, NT) + dot(heads, (x - high.astype(F32)).astype(BF), NT)


def along(rows, ones):
    res = dot(parts_of(rows, 3).astype(BF), ones.astype(BF))
    return res[:8] + res[8:16] + res[16:]


def gaps_of(cum, heads):
    parts = parts_of(cum, 3)
    row = lax.broadcasted_iota(jnp.int32, (24, heads * CHUNK), 0)
    col = lax.broadcasted_iota(jnp.int32, (24, heads * CHUNK), 1)
    mine = (row % 8 == col // CHUNK).astype(F32)
    right = jnp.concatenate([mine, -mine * jnp.concatenate([parts] * heads, axis=1)], axis=0)
    left = jnp.concatenate([parts, jnp.ones_like(parts)], axis=0)
    return dot(left.astype(BF), right.astype(BF), TN)


def stacked_halves(x):
    lane = lax.broadcasted_iota(jnp.int32, x.shape, 1)
    zero = jnp.zeros_like(x)
    return jnp.concatenate([jnp.where(lane < HEAD, x, zero), jnp.where(lane < HEAD, zero, x)], axis=0)


def chunk_masks(marks_ref, at, first):
    here = marks_ref[pl.ds(at, 1)]
    past = marks_ref[pl.ds(jnp.maximum(at - 1, 0), 1)]
    same = 1.0 - jnp.concatenate([jnp.where(first, 1.0, past), here], axis=1)
    same = jnp.broadcast_to(same, (8, 2 * CHUNK))
    rows = [same]
    for back in range(1, TAPS - 1):
        rows.append(rows[-1] * pltpu.roll(same, back, 1))
    rows = [row[:1, CHUNK:] for row in rows]
    row = lax.broadcasted_iota(jnp.int32, (CHUNK, CHUNK), 0)
    col = lax.broadcasted_iota(jnp.int32, (CHUNK, CHUNK), 1)
    counts = dot(jnp.broadcast_to(here, (8, CHUNK)), (row <= col).astype(F32))[:1]
    return jnp.concatenate(rows + [counts] + [jnp.zeros_like(counts)] * (8 - TAPS), axis=0), counts


def chunk_rows(dt_block, hp, cr):
    raw = jnp.transpose(dt_block)[:8] + hp[0]
    dt = jnp.maximum(raw, 0.0) + jnp.log1p(jnp.exp(-jnp.abs(raw)))
    rate = jnp.exp(hp[1])
    row = lax.broadcasted_iota(jnp.int32, (CHUNK, CHUNK), 0)
    col = lax.broadcasted_iota(jnp.int32, (CHUNK, CHUNK), 1)
    cum = along(-dt * rate, (row <= col).astype(F32))
    end = cum[:, CHUNK - 1 :]
    last = cr[:, CHUNK - 1 :]
    reach = jnp.where(cr == 0.0, jnp.exp(cum), 0.0)
    to_end = jnp.where(cr == last, jnp.exp(end - cum), 0.0)
    passing = jnp.where(last == 0.0, jnp.exp(end), 0.0)
    return raw, dt, rate, cum, reach, to_end, passing


def conv_in(ext, xbc, mk, cw):
    total = cw[4:5] + cw[TAPS - 1 : TAPS] * xbc
    moved = []
    for back in range(1, TAPS):
        m = pltpu.roll(ext, back, 0)[8:] * mk[:, back - 1 : back]
        moved.append(m)
        total = total + cw[TAPS - 1 - back : TAPS - back] * m
    return total, moved


def decay_of(gaps, mask, head):
    return jnp.exp(gaps[:, head * CHUNK : (head + 1) * CHUNK] + mask)


def chunk_mask(mk, cr):
    row = lax.broadcasted_iota(jnp.int32, (CHUNK, CHUNK), 0)
    col = lax.broadcasted_iota(jnp.int32, (CHUNK, CHUNK), 1)
    return jnp.where((row >= col) & (mk[:, 3:4] == cr), 0.0, FAR)


def mix_fwd_kernel(inner, proj_ref, marks_ref, cw_ref, hp_ref, gated_ref, ss_ref, ys_ref, sin_ref, s_scr, tail_scr):
    bc = CONV_CH - DI

    @pl.when(pl.program_id(1) == 0)
    def _():
        s_scr[...] = jnp.zeros_like(s_scr)
        tail_scr[...] = jnp.zeros_like(tail_scr)

    at = pl.program_id(0) * pl.num_programs(1) + pl.program_id(1)
    masks, cr = chunk_masks(marks_ref, at, pl.program_id(1) == 0)
    mk = jnp.transpose(masks)
    cw = cw_ref[...]
    xbc = proj_ref[0, :, LANES + inner :]
    ext = jnp.concatenate([tail_scr[...], xbc], axis=0)
    tail_scr[...] = xbc[CHUNK - 8 :]
    conv, _ = conv_in(ext, xbc, mk, cw)
    act = conv * jax.nn.sigmoid(conv)
    xs = act[:, :inner]
    bmat = act[:, inner : inner + STATE].astype(BF)
    cmat = act[:, inner + STATE :].astype(BF)
    raw, dt, rate, cum, reach, to_end, passing = chunk_rows(proj_ref[0, :, :LANES], hp_ref, cr)
    gaps = gaps_of(cum, inner // HEAD)
    mask = chunk_mask(mk, cr)
    xd = xs * spread(dt, inner)
    xdb = xd.astype(BF)
    state = s_scr[...]
    sin_ref[0, 0] = state
    scores = dot(cmat, bmat, NT)
    y = spread(reach, inner) * dot(cmat, state.astype(BF))
    inner_parts = []
    for j in range(inner // LANES):
        w = [(scores * decay_of(gaps, mask, 2 * j + i)).astype(BF) for i in range(2)]
        inner_parts.append(dot(jnp.concatenate(w, axis=1), stacked_halves(xdb[:, j * LANES : (j + 1) * LANES])))
    y = y + jnp.concatenate(inner_parts, axis=1)
    ys_ref[0] = y
    keep = jnp.sum(passing * head_matrix(inner), axis=0, keepdims=True)
    s_scr[...] = keep * state + dot(bmat, (xd * spread(to_end, inner)).astype(BF), TN)
    z = proj_ref[0, :, LANES : LANES + inner]
    gated = (y + cw[5:6, :inner] * xs) * (z * jax.nn.sigmoid(z))
    gated_ref[0] = gated
    ss_ref[pl.ds(at, 1)] = by_head(jnp.ones((8, inner), F32), gated * gated)[:1]


def mix_fwd(proj, marks, cw, hp, inner):
    rows, length, cols = proj.shape
    chunks = length // CHUNK
    bc = CONV_CH - DI
    whole = lambda r, c: (0, 0)
    return pl.pallas_call(
        functools.partial(mix_fwd_kernel, inner),
        grid=(rows, chunks),
        in_specs=[
            pl.BlockSpec((1, CHUNK, cols), lambda r, c: (r, c, 0)),
            pl.BlockSpec(marks.shape, whole),
            pl.BlockSpec(cw.shape, whole),
            pl.BlockSpec(hp.shape, lambda r, c: (0, 0, 0)),
        ],
        out_specs=[
            pl.BlockSpec((1, CHUNK, inner), lambda r, c: (r, c, 0)),
            pl.BlockSpec((rows * chunks, CHUNK), whole),
            pl.BlockSpec((1, CHUNK, inner), lambda r, c: (r, c, 0)),
            pl.BlockSpec((1, 1, STATE, inner), lambda r, c: (r, c, 0, 0)),
        ],
        out_shape=[
            jax.ShapeDtypeStruct((rows, length, inner), F32),
            jax.ShapeDtypeStruct((rows * chunks, CHUNK), F32),
            jax.ShapeDtypeStruct((rows, length, inner), F32),
            jax.ShapeDtypeStruct((rows, chunks, STATE, inner), F32),
        ],
        scratch_shapes=[pltpu.VMEM((STATE, inner), F32), pltpu.VMEM((8, inner + bc), F32)],
        compiler_params=pltpu.CompilerParams(
            dimension_semantics=("arbitrary", "arbitrary"), vmem_limit_bytes=60 * 2**20
        ),
        cost_estimate=pl.CostEstimate(flops=3 * 10**9, bytes_accessed=18 * 2**20, transcendentals=10**6),
    )(proj, marks, cw, hp)


def silu_slope(v, s):
    return s * (1.0 + v * (1.0 - s))


def mix_bwd_step(
    inner, chunks, proj_ref, prev_ref, marks_ref, cw_ref, hp_ref, ys_ref, sin_ref, d_mid, scale_ref, cube_ref, gain_ref,
    dp_ref, gc_ref, ds_scr, gam_scr, head_scr, gh_ref,
):
    step = pl.program_id(1)

    @pl.when((step == 0) & (pl.program_id(0) == 0))
    def _():
        gc_ref[...] = jnp.zeros_like(gc_ref)
        gh_ref[...] = jnp.zeros_like(gh_ref)

    @pl.when(step == 0)
    def _():
        ds_scr[...] = jnp.zeros_like(ds_scr)
        gam_scr[...] = jnp.zeros_like(gam_scr)
        head_scr[...] = jnp.zeros_like(head_scr)

    at = pl.program_id(0) * chunks + chunks - 1 - step
    masks, cr = chunk_masks(marks_ref, at, step == chunks - 1)
    mk = jnp.transpose(masks)
    cw = cw_ref[...]
    heads = head_matrix(inner)
    xbc = proj_ref[0, :, LANES + inner :]
    ext = jnp.concatenate([prev_ref[0, :, LANES + inner :], xbc], axis=0)
    conv, moved = conv_in(ext, xbc, mk, cw)
    sig = jax.nn.sigmoid(conv)
    act = conv * sig
    xs = act[:, :inner]
    bmat = act[:, inner : inner + STATE].astype(BF)
    cmat = act[:, inner + STATE :].astype(BF)
    raw, dt, rate, cum, reach, to_end, passing = chunk_rows(proj_ref[0, :, :LANES], hp_ref, cr)
    norm = [scale_ref[pl.ds(at, 1)], cube_ref[pl.ds(at, 1)], jnp.zeros((6, CHUNK), F32)]
    cols = jnp.transpose(jnp.concatenate(norm, axis=0))
    gaps = gaps_of(cum, inner // HEAD)
    mask = chunk_mask(mk, cr)
    dt_e = spread(dt, inner)
    reach_e = spread(reach, inner)
    end_e = spread(to_end, inner)
    xd = xs * dt_e
    xdb = xd.astype(BF)

    z = proj_ref[0, :, LANES : LANES + inner]
    sz = jax.nn.sigmoid(z)
    silu_z = z * sz
    ys = ys_ref[0]
    skip = cw[5:6, :inner]
    y = ys + skip * xs
    gated = y * silu_z
    r_mid = d_mid * cols[:, :1]
    d_gated = r_mid * gain_ref[...] - gated * cols[:, 1:2]
    d_gain = jnp.sum(r_mid * gated, axis=0, keepdims=True)
    dy = d_gated * silu_z
    dyb = dy.astype(BF)
    dyr = dyb.astype(F32)
    dz = d_gated * y * silu_slope(z, sz)

    state = sin_ref[0, 0]
    d_state = ds_scr[...]
    dsb = d_state.astype(BF)
    scores = dot(cmat, bmat, NT)
    reached = (reach_e * dyr).astype(BF)
    ended = (end_e * xd).astype(BF)
    d_xd = end_e * dot(bmat, dsb)
    d_scores = jnp.zeros((CHUNK, CHUNK), F32)
    parts = []
    for j in range(inner // LANES):
        lanes = slice(j * LANES, (j + 1) * LANES)
        pair_dy = stacked_halves(dyb[:, lanes])
        d_w = dot(pair_dy, xdb[:, lanes], NT)
        ws = []
        for i in range(2):
            decay = decay_of(gaps, mask, 2 * j + i)
            ws.append((scores * decay).astype(BF))
            d_scores = d_scores + d_w[i * CHUNK : (i + 1) * CHUNK] * decay
        parts.append(dot(jnp.concatenate(ws, axis=0), pair_dy, TN))
    d_xd = d_xd + jnp.concatenate(parts, axis=1)
    dgb = d_scores.astype(BF)
    d_c = dot(reached, state.astype(BF), NT) + dot(dgb, bmat)
    d_b = dot(ended, dsb, NT) + dot(dgb, cmat, TN)
    keep = jnp.sum(passing * heads, axis=0, keepdims=True)
    new_ds = keep * d_state + dot(cmat, reached, TN)
    alpha = by_head(heads, dyr * ys)
    beta = by_head(heads, xs * d_xd)
    lane = lax.broadcasted_iota(jnp.int32, (8, CHUNK), 1)
    d_cum = alpha - dt * beta + jnp.where(lane == CHUNK - 1, gam_scr[...], 0.0)
    row = lax.broadcasted_iota(jnp.int32, (CHUNK, CHUNK), 0)
    col = lax.broadcasted_iota(jnp.int32, (CHUNK, CHUNK), 1)
    d_log = along(d_cum, (row >= col).astype(F32))
    d_dt = beta - rate * d_log
    d_raw = d_dt * jax.nn.sigmoid(raw)
    gh_ref[0] += d_raw
    gh_ref[1] += -rate * dt * d_log
    ds_scr[...] = new_ds
    gam_scr[...] = jnp.broadcast_to(
        jnp.sum(heads * jnp.sum(new_ds * state, axis=0, keepdims=True), axis=1, keepdims=True), gam_scr.shape
    )
    d_xs = dt_e * d_xd + skip * dy

    d_conv = jnp.concatenate([d_xs, d_b, d_c], axis=1) * silu_slope(conv, sig)
    d_xbc = cw[TAPS - 1 : TAPS] * d_conv
    gc_ref[TAPS - 1 : TAPS] += jnp.sum(d_conv * xbc, axis=0, keepdims=True)
    for back in range(1, TAPS):
        u = d_conv * mk[:, back - 1 : back]
        full = jnp.concatenate([u, head_scr[back - 1]], axis=0)
        head_scr[back - 1] = u[:8]
        d_xbc = d_xbc + cw[TAPS - 1 - back : TAPS - back] * pltpu.roll(full, CHUNK + 8 - back, 0)[:CHUNK]
        gc_ref[TAPS - 1 - back : TAPS - back] += jnp.sum(d_conv * moved[back - 1], axis=0, keepdims=True)
    gc_ref[4:5] += jnp.sum(d_conv, axis=0, keepdims=True)
    gc_ref[5:6, :inner] += jnp.sum(dy * xs, axis=0, keepdims=True)
    gc_ref[6:7, :inner] += d_gain
    dp_ref[0, :, LANES : LANES + inner] = dz.astype(BF)
    dp_ref[0, :, LANES + inner :] = d_xbc.astype(BF)

    @pl.when((step == chunks - 1) & (pl.program_id(0) == pl.num_programs(0) - 1))
    def _():
        for kind in range(2):
            sums = jnp.concatenate([gh_ref[kind], jnp.zeros((LANES - 8, CHUNK), F32)], axis=0)
            sums = dot(jnp.ones((8, CHUNK), F32), sums, NT, HIGH)
            gc_ref[7:8, kind * LANES : (kind + 1) * LANES] = sums[:1]

    d_rawt = jnp.transpose(jnp.concatenate([d_raw, jnp.zeros((LANES - 8, CHUNK), F32)], axis=0))
    dp_ref[0, :, :LANES] = d_rawt.astype(BF)


MESH = pl.DeviceIdType.MESH


def meet(peers):
    barrier = pltpu.get_barrier_semaphore()
    count = 0
    for here, peer in peers:
        if here is None:
            count = count + 1
            pl.semaphore_signal(barrier, inc=1, device_id=peer, device_id_type=MESH)
        else:
            count = count + here.astype(jnp.int32)

            @pl.when(here)
            def _():
                pl.semaphore_signal(barrier, inc=1, device_id=peer, device_id_type=MESH)

    pl.semaphore_wait(barrier, count)


def line_place(n_seq):
    me = lax.axis_index("seq")
    return me // 2, me % 2, {"seq": me + 1 - 2 * (me % 2)}, {"seq": me - 2}, {"seq": me + 2}


def line_peers(n):
    chip, core, sib, left, right = line_place(2 * n)
    return [(None, sib), (chip > 0, left), (chip < n - 1, right)]


def all_peers(axis, size):
    me = lax.axis_index(axis)
    return [(None, {axis: (me + k) % size}) for k in range(1, size)]


def remote(src, dst, send, recv, device):
    return pltpu.make_async_remote_copy(
        src_ref=src, dst_ref=dst, send_sem=send, recv_sem=recv, device_id=device, device_id_type=MESH
    )


def share_start(axis, size, source, slots, send, recv):
    me = lax.axis_index(axis)
    copies = []
    for k in range(1, size):
        to = (me + k) % size
        copy = remote(source(to), slots.at[k - 1], send.at[k - 1], recv.at[k - 1], {axis: to})
        copy.start()
        copies.append(copy)
    return copies


def share_sum(copies, own, slots):
    total = own.astype(F32)
    for k, copy in enumerate(copies):
        copy.wait_recv()
        total = total + slots[k].astype(F32)
    return total


def share_end(copies):
    for copy in copies:
        copy.wait_send()


def line_gather(n, rows, span, buf, sems, use, begun=None, between=None):
    right_s, left_s, sib_s, line_r, sib_r = sems
    chip, core, sib, left, right = line_place(2 * n)
    have_left, have_right = chip > 0, chip < n - 1

    def block(r, j, c):
        return buf.at[r, j, pl.ds(pl.multiple_of(c * span, span), span)]

    def to_sib(r, j, c):
        at = j * rows + r
        return remote(block(r, j, c), block(r, j, c), sib_s.at[at], sib_r.at[at], sib)

    def to_right(r, j):
        at = j * rows + r
        return remote(block(r, j, core), block(r, j, core), right_s.at[at], line_r.at[at], right)

    def to_left(r, j):
        at = j * rows + r
        return remote(block(r, j, core), block(r, j, core), left_s.at[at], line_r.at[at], left)

    def pass_on(r, j, way):
        if way >= 0:

            @pl.when(have_right)
            def _():
                to_right(r, j).start()

        if way <= 0:

            @pl.when(have_left)
            def _():
                to_left(r, j).start()

        to_sib(r, j, core).start()

    def finish(j):
        for r in range(rows):
            to_sib(r, j, 1 - core).wait_recv()
        use(j)

    for r in range(rows):
        pass_on(r, chip, 0)
    if begun is not None:
        begun()
    finish(chip)

    def step(t, _):
        low, high = chip - t, chip + t
        for r in range(rows):

            @pl.when(low >= 0)
            def _():
                to_right(r, low).wait_recv()
                pass_on(r, low, 1)

            @pl.when(high < n)
            def _():
                to_left(r, high).wait_recv()
                pass_on(r, high, -1)

        def one(k, _):
            j = jnp.where(k == 0, low, high)

            @pl.when((j >= 0) & (j < n))
            def _():
                finish(j)

            return 0

        lax.fori_loop(0, 2, one, 0)
        if between is not None:
            between(t)
        return 0

    lax.fori_loop(1, n, step, 0)

    def done(j, _):
        for r in range(rows):
            to_sib(r, j, core).wait_send()

            @pl.when(have_right & (j <= chip))
            def _():
                to_right(r, j).wait_send()

            @pl.when(have_left & (j >= chip))
            def _():
                to_left(r, j).wait_send()

        return 0

    lax.fori_loop(0, n, done, 0)


def dma(*counts):
    return [pltpu.SemaphoreType.DMA((count,)) for count in counts]


class LineSum:
    def __init__(self, n, rows, emit, own, sib_out, sib_in, out, into, sems):
        self.n, self.rows, self.emit = n, rows, emit
        self.own, self.sib_out, self.sib_in, self.out, self.into = own, sib_out, sib_in, out, into
        self.sib_s, self.right_s, self.left_s, self.sib_r, self.right_r, self.left_r = sems
        self.chip, self.core, self.sib, self.left, self.right = line_place(2 * n)

    @staticmethod
    def scratch(n, rows, span, wide):
        shape = (n, rows, span, wide)
        k = n * rows
        return (
            [pltpu.VMEM(shape, F32)]
            + [pltpu.VMEM(shape, BF)] * 3
            + [pltpu.VMEM((n + 1,) + shape[1:], BF)]
            + dma(k, k, k, k, k, k)
        )

    def to_sib(self, j, r):
        at = j * self.rows + r
        return remote(self.sib_out.at[j, r], self.sib_in.at[j, r], self.sib_s.at[at], self.sib_r.at[at], self.sib)

    def to_right(self, j, r):
        at = j * self.rows + r
        return remote(self.out.at[j, r], self.into.at[j, r], self.right_s.at[at], self.right_r.at[at], self.right)

    def left_copy(self, j, r, owner, device):
        at = j * self.rows + r
        slot = jnp.where(j == owner, self.n, j)
        return remote(self.out.at[j, r], self.into.at[slot, r], self.left_s.at[at], self.left_r.at[at], device)

    def to_left(self, j, r):
        return self.left_copy(j, r, self.chip - 1, self.left)

    def from_right(self, j, r):
        return self.left_copy(j, r, self.chip, self.right)

    def make(self, j):
        self.emit(j)
        for r in range(self.rows):
            self.to_sib(j, r).start()

    def right_j(self, tau):
        j = self.n - 1 - (tau - self.chip)
        return j, (tau >= self.chip) & (j > self.chip)

    def left_j(self, tau):
        j = tau - (self.n - 1 - self.chip)
        return j, (j >= 0) & (j < self.chip)

    def prepare(self, tau):
        def one(k, _):
            jr, on_r = self.right_j(tau)
            jl, on_l = self.left_j(tau)
            j = jnp.where(k == 0, jr, jl)

            @pl.when(((k == 0) & on_r) | ((k == 1) & on_l))
            def _():
                self.make(j)

            return 0

        lax.fori_loop(0, 2, one, 0)

    def step(self, tau):
        jr, on_r = self.right_j(tau)
        jl, on_l = self.left_j(tau)
        own, sib_in, out, into = self.own, self.sib_in, self.out, self.into
        for r in range(self.rows):

            @pl.when(on_r)
            def _():
                self.to_sib(jr, r).wait_recv()

                @pl.when(self.chip > 0)
                def _():
                    self.to_right(jr, r).wait_recv()
                    out[jr, r] = (own[jr, r] + sib_in[jr, r].astype(F32) + into[jr, r].astype(F32)).astype(BF)

                @pl.when(self.chip == 0)
                def _():
                    out[jr, r] = (own[jr, r] + sib_in[jr, r].astype(F32)).astype(BF)

                self.to_right(jr, r).start()

            @pl.when(on_l)
            def _():
                self.to_sib(jl, r).wait_recv()

                @pl.when(self.chip < self.n - 1)
                def _():
                    self.from_right(jl, r).wait_recv()
                    out[jl, r] = (own[jl, r] + sib_in[jl, r].astype(F32) + into[jl, r].astype(F32)).astype(BF)

                @pl.when(self.chip == self.n - 1)
                def _():
                    out[jl, r] = (own[jl, r] + sib_in[jl, r].astype(F32)).astype(BF)

                self.to_left(jl, r).start()

    def finish(self, r):
        chip, own, into = self.chip, self.own, self.into
        self.to_sib(chip, r).wait_recv()
        own[chip, r] = own[chip, r] + self.sib_in[chip, r].astype(F32)

        @pl.when(chip > 0)
        def _():
            self.to_right(chip, r).wait_recv()
            own[chip, r] = own[chip, r] + into[chip, r].astype(F32)

        @pl.when(chip < self.n - 1)
        def _():
            self.from_right(chip, r).wait_recv()
            own[chip, r] = own[chip, r] + into[self.n, r].astype(F32)

    def end(self):
        def done(j, _):
            for r in range(self.rows):
                self.to_sib(j, r).wait_send()

                @pl.when(j > self.chip)
                def _():
                    self.to_right(j, r).wait_send()

                @pl.when(j < self.chip)
                def _():
                    self.to_left(j, r).wait_send()

            return 0

        lax.fori_loop(0, self.n, done, 0)

    def run(self, between=None, before_end=None):
        self.prepare(0)

        def step(tau, _):
            self.step(tau)
            self.prepare(tau + 1)
            if between is not None:
                between(tau)
            return 0

        lax.fori_loop(0, self.n - 1, step, 0)
        self.make(self.chip)
        if before_end is not None:
            before_end()
        for r in range(self.rows):
            self.finish(r)
        self.end()


def halves(own, so, j, core, start, p, rows, span):
    stop = start + p.shape[1]
    for r in range(rows):
        low, high = p[r * CHUNK : r * CHUNK + span], p[r * CHUNK + span : (r + 1) * CHUNK]
        own[j, r, :, start:stop] = jnp.where(core == 0, low, high)
        so[j, r, :, start:stop] = jnp.where(core == 0, high, low).astype(BF)


def dp_neighbours():
    d = lax.axis_index("dp")
    return d, d + 1 - 2 * (d % 2), (d + 2) % 4, 3 - d


def either(even, yes, no):
    @pl.when(even)
    def _():
        yes()

    @pl.when(jnp.logical_not(even))
    def _():
        no()


class Spread:
    def __init__(self, n_dp, at, count, sems):
        self.n_dp, self.at, self.count = n_dp, at, count
        self.s, self.r = sems

    @staticmethod
    def scratch(n_dp, count):
        return dma((n_dp - 1) * count, (n_dp - 1) * count)

    def copy(self, kind, owner, i, to):
        where = self.at(owner, i)
        sem = kind * self.count + i
        return remote(where, where, self.s.at[sem], self.r.at[sem], {"dp": to})

    def hand(self, i):
        d = lax.axis_index("dp")
        if self.n_dp == 4:
            d, x, y, _ = dp_neighbours()
            self.copy(0, d, i, x).start()
            self.copy(1, d, i, y).start()
        else:
            for k in range(1, self.n_dp):
                self.copy(k - 1, d, i, (d + k) % self.n_dp).start()

    def relay(self, i):
        if self.n_dp == 4:
            d, x, y, _ = dp_neighbours()

            def by_x():
                self.copy(0, x, i, x).wait_recv()
                self.copy(2, x, i, y).start()

            def by_y():
                self.copy(1, y, i, y).wait_recv()
                self.copy(2, y, i, x).start()

            either(i % 2 == 0, by_x, by_y)

    def end(self, i):
        d = lax.axis_index("dp")
        if self.n_dp == 4:
            d, x, y, across = dp_neighbours()

            def by_x():
                self.copy(1, y, i, y).wait_recv()
                self.copy(2, across, i, y).wait_recv()
                self.copy(2, x, i, y).wait_send()

            def by_y():
                self.copy(0, x, i, x).wait_recv()
                self.copy(2, across, i, x).wait_recv()
                self.copy(2, y, i, x).wait_send()

            either(i % 2 == 0, by_x, by_y)
            self.copy(0, d, i, x).wait_send()
            self.copy(1, d, i, y).wait_send()
        else:
            for k in range(1, self.n_dp):
                source = (d - k + self.n_dp) % self.n_dp
                self.copy(k - 1, source, i, source).wait_recv()
                self.copy(k - 1, d, i, (d + k) % self.n_dp).wait_send()


class DpSum:
    def __init__(self, n_dp, term, slots, piece, sems):
        self.n_dp, self.term, self.slots, self.piece = n_dp, term, slots, piece
        self.count = term.shape[1] // piece
        self.s, self.r = sems

    @staticmethod
    def scratch(n_dp, rows, cols, piece):
        count = (n_dp - 1) * (rows // piece)
        return [pltpu.VMEM((n_dp - 1, rows, cols), BF)] + dma(count, count)

    def rows_of(self, i):
        return pl.ds(pl.multiple_of(i * self.piece, self.piece), self.piece)

    def copy(self, kind, source, i, to):
        sem = kind * self.count + i
        return remote(source, self.slots.at[kind, self.rows_of(i)], self.s.at[sem], self.r.at[sem], {"dp": to})

    def part(self, kind, owner, i, to):
        return self.copy(kind, self.term.at[owner, self.rows_of(i)], i, to)

    def on(self, i):
        return self.copy(2, self.slots.at[1, self.rows_of(i)], i, self.axes(i)[1])

    def axes(self, i):
        d, x, y, across = dp_neighbours()
        even = i % 2 == 0
        return jnp.where(even, x, y), jnp.where(even, y, x), across, d

    def send(self, i):
        if self.n_dp == 4:
            first, second, across, d = self.axes(i)
            self.part(1, across, i, first).start()
            self.part(0, first, i, first).start()
        else:
            d = lax.axis_index("dp")
            for k in range(1, self.n_dp):
                to = (d + k) % self.n_dp
                self.part(k - 1, to, i, to).start()

    def middle(self, i):
        if self.n_dp == 4:
            first, second, across, d = self.axes(i)
            here = self.rows_of(i)
            self.part(1, across, i, first).wait_recv()
            self.slots[1, here] = (self.term[second, here].astype(F32) + self.slots[1, here].astype(F32)).astype(BF)
            self.on(i).start()

    def total(self, i):
        d = lax.axis_index("dp")
        here = self.rows_of(i)
        total = self.term[d, here].astype(F32)
        if self.n_dp == 4:
            first, second, across, d = self.axes(i)
            self.part(0, first, i, first).wait_recv()
            self.on(i).wait_recv()
            return total + self.slots[0, here].astype(F32) + self.slots[2, here].astype(F32)
        for k in range(1, self.n_dp):
            to = (d + k) % self.n_dp
            self.part(k - 1, to, i, to).wait_recv()
            total = total + self.slots[k - 1, here].astype(F32)
        return total

    def end(self, i):
        if self.n_dp == 4:
            first, second, across, d = self.axes(i)
            self.part(1, across, i, first).wait_send()
            self.part(0, first, i, first).wait_send()
            self.on(i).wait_send()
        else:
            d = lax.axis_index("dp")
            for k in range(1, self.n_dp):
                to = (d + k) % self.n_dp
                self.part(k - 1, to, i, to).wait_send()


class Fetch:
    def __init__(self, n_dp, n_seq, parts, wv, refs):
        self.n_dp, self.n_seq, self.parts, self.wv = n_dp, n_seq, parts, wv
        self.a_s, self.a_r = refs[:2]
        self.spread = Spread(n_dp, lambda owner, i: wv.at[owner, i], n_seq, refs[2:4])

    @staticmethod
    def scratch(n_dp, n_seq):
        return dma(n_seq, n_seq) + Spread.scratch(n_dp, n_seq)

    def across(self, i):
        me, d = lax.axis_index("seq"), lax.axis_index("dp")
        to = (me + i) % self.n_seq
        return remote(self.parts.at[to], self.wv.at[d, me], self.a_s.at[to], self.a_r.at[me], {"seq": to})

    def place(self, i):
        return (lax.axis_index("seq") - i + self.n_seq) % self.n_seq

    def arrival(self, i):
        me, d = lax.axis_index("seq"), lax.axis_index("dp")
        source = self.place(i)
        return remote(self.parts.at[me], self.wv.at[d, source], self.a_s.at[me], self.a_r.at[source], {"seq": source})

    def start(self):
        def go(i, _):
            self.across(i).start()
            return 0

        lax.fori_loop(1, self.n_seq, go, 0)
        me, d = lax.axis_index("seq"), lax.axis_index("dp")
        self.wv[d, me] = self.parts[me]
        self.spread.hand(me)

    def pull(self, first, last):
        def one(i, _):
            @pl.when(i < self.n_seq)
            def _():
                self.arrival(i).wait_recv()
                self.spread.hand(self.place(i))

                @pl.when(i >= 2)
                def _():
                    self.spread.relay(self.place(i - 2))

            return 0

        lax.fori_loop(first, last, one, 0)

    def tail(self):
        self.spread.relay(self.place(self.n_seq - 2))
        self.spread.relay(self.place(self.n_seq - 1))

    def end(self):
        def ended(i, _):
            self.spread.end(i)
            return 0

        lax.fori_loop(0, self.n_seq, ended, 0)

    def sent(self):
        def one(i, _):
            self.across(i).wait_send()
            return 0

        lax.fori_loop(1, self.n_seq, one, 0)


class Pieces:
    def __init__(self, n_dp, n_seq, term, got, refs):
        self.n_seq, self.got = n_seq, got
        self.piece = got.shape[1]
        slots, dp_s, dp_r, self.sums, self.seq_s, self.seq_r = refs
        self.sum = DpSum(n_dp, term, slots, self.piece, (dp_s, dp_r))
        self.per = LANES // self.piece
        self.tiles = n_seq // self.per

    @staticmethod
    def scratch(n_dp, n_seq, rows, cols):
        piece = rows // n_seq
        return DpSum.scratch(n_dp, rows, cols, piece) + [pltpu.VMEM((n_seq, piece, cols), BF)] + dma(n_seq, n_seq)

    def tile(self, i):
        if 2 * self.tiles == self.n_seq:
            return (lax.axis_index("seq") // 2 + 1 + i) % self.tiles
        return i

    def each(self, i, act):
        def one(k, _):
            act(self.tile(i) * self.per + k)
            return 0

        lax.fori_loop(0, self.per, one, 0)

    def over_seq(self, s):
        me = lax.axis_index("seq")
        return remote(self.sums.at[s], self.got.at[me], self.seq_s.at[s], self.seq_r.at[me], {"seq": s})

    def from_seq(self, s):
        me = lax.axis_index("seq")
        return remote(self.sums.at[me], self.got.at[s], self.seq_s.at[me], self.seq_r.at[s], {"seq": s})

    def finish(self, s):
        me = lax.axis_index("seq")
        total = self.sum.total(s).astype(BF)

        def away():
            self.sums[s] = total
            self.over_seq(s).start()

        def stay():
            self.got[s] = total

        either(s != me, away, stay)

    def tiles_do(self, first, last, *acts):
        def one(i, _):
            @pl.when((i >= 0) & (i < self.tiles))
            def _():
                for act in acts:
                    act(i)

            return 0

        lax.fori_loop(first, last, one, 0)

    def send(self, i):
        self.each(i, self.sum.send)

    def middle(self, i):
        self.each(i, self.sum.middle)

    def last(self, i):
        self.each(i, self.finish)

    def end(self):
        def one(s, _):
            self.sum.end(s)

            @pl.when(s != lax.axis_index("seq"))
            def _():
                self.over_seq(s).wait_send()
                self.from_seq(s).wait_recv()

            return 0

        lax.fori_loop(0, self.n_seq, one, 0)


VMEM_SPEC = pl.BlockSpec(memory_space=pltpu.VMEM)
ANY_SPEC = pl.BlockSpec(memory_space=pl.ANY)


def comm_params(name):
    return pltpu.CompilerParams(collective_id=name, has_side_effects=True, vmem_limit_bytes=60 * 2**20)


def project_kernel(n, n_dp, fetch, x_ref, gain_ref, *refs):
    refs = list(refs)
    n_seq = 2 * n
    rows, span, width = x_ref.shape
    if fetch:
        parts_ref, wo_ref, marks_ref = refs[:3]
        hid_ref, proj_ref, w_ref, wout_ref, all_ref = refs[3:8]
        buf, wv, po = refs[8:11]
        line, (w_sem, hid_sem, out_sem) = refs[11:16], refs[16:19]
        get = Fetch(n_dp, n_seq, parts_ref, wv, refs[19:23])
        o_s, o_r, m_s, m_r, mall = refs[23:]
    else:
        w_ref, hid_ref, proj_ref, buf, wv, po = refs[:6]
        line, (w_sem, hid_sem, out_sem) = refs[6:11], refs[11:]
    chip, core, sib, left, right = line_place(n_seq)
    me = lax.axis_index("seq")
    d = lax.axis_index("dp")
    if not fetch:
        load = pltpu.make_async_copy(w_ref, wv, w_sem.at[0])
        load.start()
    for r in range(rows):
        x = x_ref[r].astype(F32)
        scale = lax.rsqrt(jnp.mean(x * x, axis=-1, keepdims=True) + EPS)
        buf[r, chip, pl.ds(pl.multiple_of(core * span, span), span)] = (x * scale * gain_ref[...]).astype(BF)
    if fetch:
        meet(all_peers("seq", n_seq) + all_peers("dp", n_dp))
    else:
        meet(line_peers(n))
        load.wait()

    def out_copies(j):
        return (
            pltpu.make_async_copy(buf.at[:, j], hid_ref.at[:, j], hid_sem.at[j]),
            pltpu.make_async_copy(po.at[j], proj_ref.at[:, pl.ds(j * CHUNK, CHUNK)], out_sem.at[j]),
        )

    def use(j):
        block = buf[:, j].reshape(rows * CHUNK, width)
        res = dot(block, wv[...].reshape(width, wv.shape[-1]))
        for r in range(rows):
            po[j, r] = res[r * CHUNK : (r + 1) * CHUNK]
        for copy in out_copies(j):
            copy.start()

    def done(j, _):
        for copy in out_copies(j):
            copy.wait()
        return 0

    if not fetch:
        line_gather(n, rows, span, buf, line, use)
        lax.fori_loop(0, n, done, 0)
        return

    half = wo_ref.shape[0] // 2

    def half_of(owner, i):
        return wout_ref.at[owner, pl.ds(pl.multiple_of(i * half, half), half)]

    outs = Spread(n_dp, half_of, 2, (o_s, o_r))

    def marks_copy(i):
        to = (me + i) % n_seq
        return remote(marks_ref, mall.at[me], m_s.at[to], m_r.at[me], {"seq": to})

    def marks_in(i):
        source = (me - i + n_seq) % n_seq
        return remote(marks_ref, mall.at[source], m_s.at[me], m_r.at[source], {"seq": source})

    get.start()
    for i in range(1, n_seq):
        marks_copy(i).start()
    mall[me] = marks_ref[...]

    def begun():
        get.pull(1, n_seq)
        wout_ref[d] = wo_ref[...]
        for i in range(2):
            outs.hand(i)
        get.tail()

    line_gather(n, rows, span, buf, line, lambda j: None, begun)
    for i in range(1, n_seq):
        marks_in(i).wait_recv()
    for r in range(rows):
        for j in range(n):
            all_ref[r * n + j : r * n + j + 1] = mall[2 * j, r : r + 1] + mall[2 * j + 1, r : r + 1]
    for i in range(2):
        outs.relay(i)

    get.end()
    keep = pltpu.make_async_copy(wv, w_ref, w_sem.at[0])
    keep.start()

    def each(j, _):
        use(j)
        return 0

    lax.fori_loop(0, n, each, 0)
    for i in range(2):
        outs.end(i)

    get.sent()
    for i in range(1, n_seq):
        marks_copy(i).wait_send()
    lax.fori_loop(0, n, done, 0)
    keep.wait()


def project(x, gain, w, n_seq):
    return project_call(x, gain, w.shape, (w,), None, n_seq)


def project_fetch(x, gain, parts, wo, marks, n_dp, n_seq):
    piece, cols = parts.shape[1:]
    return project_call(x, gain, (n_dp, n_seq, piece, cols), (parts, wo, marks), n_dp, n_seq)


def project_call(x, gain, w_shape, more, n_dp, n_seq):
    rows, span, width = x.shape
    n = n_seq // 2
    k = n * rows
    cols = w_shape[-1]
    outs = [
        jax.ShapeDtypeStruct((rows, n, CHUNK, width), BF),
        jax.ShapeDtypeStruct((rows, n * CHUNK, cols), F32),
    ]
    scratch = [
        pltpu.VMEM((rows, n, CHUNK, width), BF),
        pltpu.VMEM(w_shape, BF),
        pltpu.VMEM((n, rows, CHUNK, cols), F32),
    ] + dma(k, k, k, k, k, 1, n, n)
    in_specs = [VMEM_SPEC, VMEM_SPEC, ANY_SPEC]
    out_specs = [ANY_SPEC, ANY_SPEC]
    if n_dp is not None:
        parts, wo, marks = more
        in_specs = [VMEM_SPEC] * 5
        out_specs += [ANY_SPEC, VMEM_SPEC, VMEM_SPEC]
        outs += [
            jax.ShapeDtypeStruct(w_shape, BF),
            jax.ShapeDtypeStruct((n_dp,) + wo.shape, BF),
            jax.ShapeDtypeStruct((k, CHUNK), F32),
        ]
        scratch += Fetch.scratch(n_dp, n_seq) + Spread.scratch(n_dp, 2) + dma(n_seq, n_seq)
        scratch += [pltpu.VMEM((n_seq,) + marks.shape, F32)]
    return pl.pallas_call(
        functools.partial(project_kernel, n, n_dp, n_dp is not None),
        in_specs=in_specs,
        out_specs=out_specs,
        out_shape=outs,
        scratch_shapes=scratch,
        compiler_params=comm_params(0 if n_dp is None else 7),
        cost_estimate=pl.CostEstimate(flops=6 * 10**9, bytes_accessed=20 * 2**20, transcendentals=0),
    )(x, gain, *more)


def branch_kernel(
    n, n_dp, gated_ref, ss_ref, gain_ref, w_ref, x_ref, parts_ref, y_ref, mid_ref, scale_ref, next_ref,
    slots, share_s, share_r, own, so, *refs,
):
    rows, span, width = x_ref.shape
    n_seq = 2 * n
    line, (wv, w_sem), fetch_sems = refs[:9], refs[9:11], refs[11:]
    get = Fetch(n_dp, n_seq, parts_ref, wv, fetch_sems)
    chip, core, sib, left, right = line_place(n_seq)
    meet(all_peers("seq", n_seq) + all_peers("dp", n_dp))
    copies = share_start("seq", n_seq, lambda to: ss_ref, slots, share_s, share_r)
    total = share_sum(copies, ss_ref[...], slots)
    get.start()
    scale = lax.rsqrt(total / DI + EPS)
    scale_ref[...] = scale
    cols = jnp.transpose(scale)
    for r in range(rows):
        for k in range(n):
            at = r * n + k
            g = gated_ref[r, k * CHUNK : (k + 1) * CHUNK]
            mid_ref[r, k * CHUNK : (k + 1) * CHUNK] = (g * cols[:, at : at + 1] * gain_ref[...]).astype(BF)

    def emit(j):
        here = pl.ds(pl.multiple_of(j * CHUNK, CHUNK), CHUNK)
        block = jnp.concatenate([mid_ref[r, here] for r in range(rows)], axis=0)
        for at in range(0, width, 512):
            halves(own, so, j, core, at, dot(block, w_ref[:, at : at + 512]), rows, span)

    per = -(-(n_seq - 1) // (n - 1))
    LineSum(n, rows, emit, own, so, *line[:3], line[3:]).run(lambda tau: get.pull(1 + tau * per, 1 + tau * per + per))
    get.tail()
    for r in range(rows):
        y_ref[r] = x_ref[r] + own[chip, r]
    get.end()
    keep = pltpu.make_async_copy(wv, next_ref, w_sem.at[0])
    keep.start()
    get.sent()
    share_end(copies)
    keep.wait()


def branch(gated, ss, gain, w, x, parts, n_dp, n_seq):
    rows, span, width = x.shape
    n = n_seq // 2
    w_shape = (n_dp, n_seq) + parts.shape[1:]
    return pl.pallas_call(
        functools.partial(branch_kernel, n, n_dp),
        in_specs=[VMEM_SPEC] * 6,
        out_specs=[VMEM_SPEC] * 3 + [ANY_SPEC],
        out_shape=[
            jax.ShapeDtypeStruct(x.shape, F32),
            jax.ShapeDtypeStruct(gated.shape, BF),
            jax.ShapeDtypeStruct(ss.shape, F32),
            jax.ShapeDtypeStruct(w_shape, BF),
        ],
        scratch_shapes=[pltpu.VMEM((n_seq - 1,) + ss.shape, F32)]
        + dma(n_seq - 1, n_seq - 1)
        + LineSum.scratch(n, rows, span, width)
        + [pltpu.VMEM(w_shape, BF)]
        + dma(1)
        + Fetch.scratch(n_dp, n_seq),
        compiler_params=comm_params(1),
        cost_estimate=pl.CostEstimate(flops=3 * 10**9, bytes_accessed=10 * 2**20, transcendentals=0),
    )(gated, ss, gain, w, x, parts)


def back_mix_kernel(n, n_dp, top, with_out, *refs):
    n_seq = 2 * n
    refs = list(refs)
    take = lambda k: [refs.pop(0) for _ in range(k)]
    proj_ref, prev_ref, marks_ref, cw_ref, hp_ref, ys_ref, sin_ref, gain_ref, gated_ref, w_ref, g_ref = take(11)
    if top:
        ss_ref, x_ref = take(2)
    else:
        mid_ref, scale_ref, term_ref, vec_ref = take(4)
    dp_ref, gc_ref, gout_ref = take(3)
    if top:
        (y_ref,) = take(1)
    else:
        got_ref, vall_ref = take(2)
    mixer = take(4)
    dmid, acc, gwb, scale_scr, cube_scr, tot, slots = take(7)
    share_s, share_r = take(2)
    if with_out:
        outs = DpSum(n_dp, gwb, refs[0], gwb.shape[1] // 2, refs[1:3])
        take(3)
    rows, span, width = g_ref.shape[-3:]
    inner = gated_ref.shape[2]
    chip, core, sib, left, right = line_place(n_seq)
    step = pl.program_id(1)
    k = pl.program_id(0) * n + step
    last = rows * n - 1
    ones = jnp.ones((8, inner), F32)
    if top:
        own, so = refs[:2]
        line = LineSum(n, rows, None, own, so, *refs[2:5], refs[5:11])
        mids, turn = refs[11:13]
    else:
        buf, line_sems, got, vall = refs[0], refs[1:6], refs[6], refs[7]
        pieces = Pieces(n_dp, n_seq, term_ref, got, refs[8:14])
        small = Small(n_dp, n_seq, vec_ref, vall, *refs[14:20])

    def through(j, block, mid):
        chunk = pl.ds(pl.multiple_of(j * CHUNK, CHUNK), CHUNK)
        res = dot(block, w_ref[...], NT)
        for at in range(0, width, 512):
            acc[:, at : at + 512] += dot(mid, block[:, at : at + 512], TN)
        for r in range(rows):
            part = res[r * CHUNK : (r + 1) * CHUNK]
            dmid[r, chunk] = part
            v = part * gain_ref[...] * gated_ref[r, chunk]
            tot[pl.ds(r * n + j, 1)] = by_head(ones, v)[:1]

    @pl.when(k == 0)
    def _():
        if not top:
            acc[...] = jnp.zeros_like(acc)
        if top:
            meet(all_peers("seq", n_seq) + (all_peers("dp", n_dp) if with_out else []))
            first = share_start("seq", n_seq, lambda to: ss_ref, slots.at[0], share_s.at[0], share_r.at[0])
            scale = lax.rsqrt(share_sum(first, ss_ref[...], slots.at[0]) / DI + EPS)
            share_end(first)
            scale_scr[...] = scale
            cols = jnp.transpose(scale)
            for j in range(n):
                for r in range(rows):
                    at = r * n + j
                    part = gated_ref[r, j * CHUNK : (j + 1) * CHUNK] * cols[:, at : at + 1] * gain_ref[...]
                    turned = jnp.transpose(part).astype(BF)
                    part = part.astype(BF)
                    for c in range(2):
                        to = ((2 * j + c) * rows + r) * span
                        mids[to : to + span] = part[c * span : (c + 1) * span]
                        turn[:, to : to + span] = turned[:, c * span : (c + 1) * span]
            for at in range(0, width, 512):
                out = dot(mids[...], w_ref[:, at : at + 512])
                for j in range(n):
                    for r in range(rows):
                        low = out[(2 * j * rows + r) * span : (2 * j * rows + r + 1) * span]
                        high = out[((2 * j + 1) * rows + r) * span : ((2 * j + 1) * rows + r + 1) * span]
                        own[j, r, :, at : at + 512] = jnp.where(core == 0, low, high)
                        so[j, r, :, at : at + 512] = jnp.where(core == 0, high, low).astype(BF)
            for j in range(n):
                for r in range(rows):
                    line.to_sib(j, r).start()
            line.step(0)
            every = g_ref[...].reshape(n_seq * rows * span, width)
            res = dot(every, w_ref[...], NT)
            for j in range(n):
                for r in range(rows):
                    for c in range(2):
                        at = ((2 * j + c) * rows + r) * span
                        dmid[r, j * CHUNK + c * span : j * CHUNK + (c + 1) * span] = res[at : at + span]
                    chunk = slice(j * CHUNK, (j + 1) * CHUNK)
                    v = dmid[r, chunk] * gain_ref[...] * gated_ref[r, chunk]
                    tot[r * n + j : r * n + j + 1] = by_head(ones, v)[:1]
            second = share_start("seq", n_seq, lambda to: tot, slots.at[1], share_s.at[1], share_r.at[1])
            size = inner // n_dp
            for d in range(n_dp):
                for at in range(0, width, 512):
                    gwb[d, :, at : at + 512] = dot(
                        turn[d * size : (d + 1) * size], every[:, at : at + 512]
                    ).astype(BF)
            line.step(1)
        else:
            scale = scale_ref[...]
            scale_scr[...] = scale
            here = pl.ds(pl.multiple_of(core * span, span), span)
            for r in range(rows):
                buf[r, chip, here] = g_ref[r].astype(BF)
            meet(all_peers("seq", n_seq) + all_peers("dp", n_dp))

            small.start()
            pieces.tiles_do(0, pieces.tiles, pieces.send)

            def use(j):
                chunk = pl.ds(pl.multiple_of(j * CHUNK, CHUNK), CHUNK)
                mid = jnp.concatenate([mid_ref[r, chunk] for r in range(rows)], axis=0)
                through(j, buf[:, j].reshape(rows * CHUNK, width), mid)

            def between(t):
                at = jnp.maximum(2 * (t - 2), 0)
                pieces.tiles_do(at, jnp.where(t < 2, at, at + 2), pieces.middle)

            line_gather(n, rows, span, buf, line_sems, use, None, between)
            second = share_start("seq", n_seq, lambda to: tot, slots.at[1], share_s.at[1], share_r.at[1])
            for d in range(n_dp):
                size = inner // n_dp
                gwb[d] = acc[d * size : (d + 1) * size].astype(BF)
        if with_out:
            for i in range(2):
                outs.send(i)
        else:
            gout_ref[...] = gwb[...]
        cube_scr[...] = scale * scale * scale * (share_sum(second, tot[...], slots.at[1]) / DI)
        share_end(second)

    at = pl.multiple_of((n - 1 - step) * CHUNK, CHUNK)
    mix_bwd_step(
        inner, n, proj_ref, prev_ref, marks_ref, cw_ref, hp_ref, ys_ref, sin_ref,
        dmid[pl.program_id(0), pl.ds(at, CHUNK)], scale_scr, cube_scr, gain_ref, dp_ref, gc_ref, *mixer,
    )

    if top:

        @pl.when((k % 2 == 1) & (k < last - 1))
        def _():
            line.step((k + 3) // 2)
    else:

        @pl.when(k == 0)
        def _():
            small.middle()

        @pl.when(2 * k < pieces.tiles)
        def _():
            pieces.tiles_do(2 * k, 2 * k + 2, pieces.last)

    if with_out:

        @pl.when(k == last // 2)
        def _():
            for i in range(2):
                outs.middle(i)

    @pl.when(k == last)
    def _():
        if with_out:
            for i in range(2):
                gout_ref[outs.rows_of(i)] = outs.total(i)
                outs.end(i)
        if top:
            for r in range(rows):
                line.finish(r)
                y_ref[r] = (x_ref[r] + own[chip, r]).astype(BF)
            line.end()
        else:
            small.end()
            pieces.end()
            got_ref[...] = got[...]
            vall_ref[...] = vall[...]


def back_mix(proj, marks, cw, hp, ys, sin, gain, gated, w, g, more, n_dp, n_seq, with_out):
    top = len(more) == 2
    rows, length, cols = proj.shape
    span, width = g.shape[-2:]
    n = n_seq // 2
    inner = gated.shape[2]
    k = rows * n
    bc = CONV_CH - DI
    at = lambda r, c: (r, n - 1 - c, 0)

    def whole(x):
        zeros = (0,) * len(x.shape)
        return pl.BlockSpec(x.shape, lambda r, c: zeros, pipeline_mode=pl.Buffered(1))

    if with_out:
        gout = jax.ShapeDtypeStruct((inner // n_dp, width), F32)
    else:
        gout = jax.ShapeDtypeStruct((n_dp, inner // n_dp, width), BF)
    outs = [
        jax.ShapeDtypeStruct((rows, length, cols), BF),
        jax.ShapeDtypeStruct((8, inner + bc), F32),
        gout,
    ]
    scratch = [
        pltpu.VMEM((STATE, inner), F32),
        pltpu.VMEM((8, LANES), F32),
        pltpu.VMEM((TAPS - 1, 8, inner + bc), F32),
        pltpu.VMEM((2, 8, CHUNK), F32),
        pltpu.VMEM((rows, length, inner), F32),
        pltpu.VMEM((8, LANES) if top else (inner, width), F32),
        pltpu.VMEM((n_dp, inner // n_dp, width), BF),
        pltpu.VMEM((k, CHUNK), F32),
        pltpu.VMEM((k, CHUNK), F32),
        pltpu.VMEM((k, CHUNK), F32),
        pltpu.VMEM((2, n_seq - 1, k, CHUNK), F32),
        pltpu.SemaphoreType.DMA((2, n_seq - 1)),
        pltpu.SemaphoreType.DMA((2, n_seq - 1)),
    ]
    if with_out:
        scratch += DpSum.scratch(n_dp, inner // n_dp, width, inner // n_dp // 2)
    if top:
        outs.append(jax.ShapeDtypeStruct((rows, span, width), BF))
        scratch += LineSum.scratch(n, rows, span, width) + [pltpu.VMEM((length * rows, inner), BF), pltpu.VMEM((inner, length * rows), BF)]
    else:
        term, vec = more[2:]
        outs.append(jax.ShapeDtypeStruct((n_seq, term.shape[1] // n_seq, term.shape[2]), BF))
        outs.append(jax.ShapeDtypeStruct((n_seq,) + vec.shape, F32))
        scratch += [pltpu.VMEM((rows, n, CHUNK, width), BF)] + dma(k, k, k, k, k)
        scratch += [pltpu.VMEM(outs[-2].shape, BF), pltpu.VMEM(outs[-1].shape, F32)]
        scratch += Pieces.scratch(n_dp, n_seq, term.shape[1], term.shape[2])
        scratch += Small.scratch(n_dp, n_seq, vec)
    full = (marks, cw, hp)
    rest = (gain, gated, w, g) + tuple(more)
    return pl.pallas_call(
        functools.partial(back_mix_kernel, n, n_dp, top, with_out),
        grid=(rows, n),
        in_specs=[
            pl.BlockSpec((1, CHUNK, cols), at),
            pl.BlockSpec((1, 8, cols), lambda r, c: (r, jnp.maximum((n - 1 - c) * (CHUNK // 8) - 1, 0), 0)),
        ]
        + [whole(x) for x in full]
        + [
            pl.BlockSpec((1, CHUNK, inner), at),
            pl.BlockSpec((1, 1, STATE, inner), lambda r, c: (r, n - 1 - c, 0, 0)),
        ]
        + [whole(x) for x in rest],
        out_specs=[pl.BlockSpec((1, CHUNK, cols), at)] + [whole(x) for x in outs[1:]],
        out_shape=outs,
        scratch_shapes=scratch,
        compiler_params=pltpu.CompilerParams(
            dimension_semantics=("arbitrary", "arbitrary"),
            collective_id=2 if top else 4,
            has_side_effects=True,
            vmem_limit_bytes=60 * 2**20,
        ),
        cost_estimate=pl.CostEstimate(flops=14 * 10**9, bytes_accessed=40 * 2**20, transcendentals=2 * 10**6),
    )(proj, proj, *full, ys, sin, *rest)


def back_project_kernel(n, n_dp, final, dp_ref, w_ref, x_ref, g_ref, gain_ref, hid_ref, out_ref, dgain_ref, term_ref, hid, hid_sem, own, so, *refs):
    n_seq = 2 * n
    line, refs = refs[:9], refs[9:]
    rows, span, width = x_ref.shape
    part = dp_ref.shape[2]
    group = width // n_dp
    chip, core, sib, left, right = line_place(n_seq)
    load = pltpu.make_async_copy(hid_ref, hid, hid_sem.at[0])
    load.start()
    if final:
        term = refs[0]
        pieces = Pieces(n_dp, n_seq, term, term_ref, refs[1:])
        meet(all_peers("seq", n_seq) + all_peers("dp", n_dp))
    else:
        term = term_ref
        meet(line_peers(n))

    def emit(j):
        here = pl.ds(pl.multiple_of(j * CHUNK, CHUNK), CHUNK)
        block = jnp.concatenate([dp_ref[r, here] for r in range(rows)], axis=0)
        for at in range(0, width, 512):
            halves(own, so, j, core, at, dot(block, w_ref[at : at + 512], NT), rows, span)

    def product(tile):
        right_side = dp_ref[...].reshape(rows * n * CHUNK, part)

        def one(owner, _):
            col = pl.ds(pl.multiple_of(owner * group + tile * LANES, LANES), LANES)
            h = hid[:, :, :, col].reshape(rows * n * CHUNK, LANES)
            term[owner, pl.ds(pl.multiple_of(tile * LANES, LANES), LANES)] = dot(h, right_side, TN).astype(BF)
            return 0

        lax.fori_loop(0, n_dp, one, 0)

    tiles = group // LANES

    def between(tau):
        @pl.when(tau == 0)
        def _():
            load.wait()

        if final:
            pieces.tiles_do(tau - 1, jnp.maximum(tau, 0), pieces.middle)
            pieces.tiles_do(tau - 2, jnp.maximum(tau - 1, 0), pieces.last)
            first = jnp.where(tau == 0, 0, tau + 1)
            pieces.tiles_do(first, tau + 2, lambda i: product(pieces.tile(i)), pieces.send)
        else:

            def one(k, _):
                @pl.when(2 * tau + k < tiles)
                def _():
                    product(2 * tau + k)

                return 0

            lax.fori_loop(0, 2, one, 0)

    def before_end():
        if final:
            pieces.tiles_do(n, pieces.tiles, lambda i: product(pieces.tile(i)), pieces.send)
            pieces.tiles_do(n - 2, pieces.tiles, pieces.middle)
            pieces.tiles_do(n - 3, n - 2, pieces.last)

    LineSum(n, rows, emit, own, so, *line[:3], line[3:]).run(between, before_end)
    if final:
        pieces.tiles_do(n - 2, pieces.tiles, pieces.last)
    d_gain = jnp.zeros((1, width), F32)
    for r in range(rows):
        d_hid = own[chip, r]
        x = x_ref[r]
        scale = lax.rsqrt(jnp.mean(x * x, axis=-1, keepdims=True) + EPS)
        m = d_hid * gain_ref[...]
        mean = jnp.mean(m * x, axis=-1, keepdims=True)
        out_ref[r] = g_ref[r] + scale * m - x * (scale * scale * scale * mean)
        d_gain = d_gain + jnp.sum(d_hid * x * scale, axis=0, keepdims=True)
    dgain_ref[...] = d_gain
    if final:
        pieces.end()


def back_project(dp, w, x, g, gain, hidden, final, n_dp, n_seq):
    rows, span, width = x.shape
    n = n_seq // 2
    part = dp.shape[2]
    group = width // n_dp
    whole_term = (n_dp, group, part)
    more = []
    if final:
        more = [pltpu.VMEM(whole_term, BF)] + Pieces.scratch(n_dp, n_seq, group, part)
    return pl.pallas_call(
        functools.partial(back_project_kernel, n, n_dp, final),
        in_specs=[VMEM_SPEC] * 5 + [ANY_SPEC],
        out_specs=[VMEM_SPEC] * 3,
        out_shape=[
            jax.ShapeDtypeStruct(x.shape, F32),
            jax.ShapeDtypeStruct((1, width), F32),
            jax.ShapeDtypeStruct((n_seq, group // n_seq, part) if final else whole_term, BF),
        ],
        scratch_shapes=[pltpu.VMEM(hidden.shape, BF)]
        + dma(1)
        + LineSum.scratch(n, rows, span, width)
        + more,
        compiler_params=comm_params(5 if final else 3),
        cost_estimate=pl.CostEstimate(flops=11 * 10**9, bytes_accessed=24 * 2**20, transcendentals=0),
    )(dp, w, x, g, gain, hidden)


class Small:
    def __init__(self, n_dp, n_seq, vec, vall, vsum, vslots, v_s, v_r, a_s, a_r):
        self.n_dp, self.n_seq, self.vec, self.vall = n_dp, n_seq, vec, vall
        self.vsum, self.vslots, self.v_s, self.v_r, self.a_s, self.a_r = vsum, vslots, v_s, v_r, a_s, a_r

    @staticmethod
    def scratch(n_dp, n_seq, vec):
        return [pltpu.VMEM(vec.shape, F32), pltpu.VMEM((n_dp - 1,) + vec.shape, F32)] + dma(
            n_dp - 1, n_dp - 1, n_seq, n_seq
        )

    def over_dp(self, k):
        to = (lax.axis_index("dp") + k) % self.n_dp
        return remote(self.vec, self.vslots.at[k - 1], self.v_s.at[k - 1], self.v_r.at[k - 1], {"dp": to})

    def give(self, k):
        me = lax.axis_index("seq")
        to = (me + k) % self.n_seq
        return remote(self.vsum, self.vall.at[me], self.a_s.at[to], self.a_r.at[me], {"seq": to})

    def take(self, k):
        me = lax.axis_index("seq")
        source = (me + k) % self.n_seq
        return remote(self.vsum, self.vall.at[source], self.a_s.at[me], self.a_r.at[source], {"seq": source})

    def start(self):
        for k in range(1, self.n_dp):
            self.over_dp(k).start()

    def middle(self):
        total = self.vec[...]
        for k in range(1, self.n_dp):
            self.over_dp(k).wait_recv()
            total = total + self.vslots[k - 1]
        self.vsum[...] = total
        for k in range(1, self.n_seq):
            self.give(k).start()
        self.vall[lax.axis_index("seq")] = total

    def end(self):
        for k in range(1, self.n_seq):
            self.take(k).wait_recv()
        for k in range(1, self.n_seq):
            self.give(k).wait_send()
        for k in range(1, self.n_dp):
            self.over_dp(k).wait_send()


def small_kernel(n_dp, n_seq, vec_ref, vall_ref, *refs):
    small = Small(n_dp, n_seq, vec_ref, vall_ref, *refs)
    meet(all_peers("seq", n_seq) + all_peers("dp", n_dp))
    small.start()
    small.middle()
    small.end()


def small_sums(vec, n_dp, n_seq):
    return pl.pallas_call(
        functools.partial(small_kernel, n_dp, n_seq),
        in_specs=[VMEM_SPEC],
        out_specs=VMEM_SPEC,
        out_shape=jax.ShapeDtypeStruct((n_seq,) + vec.shape, F32),
        scratch_shapes=Small.scratch(n_dp, n_seq, vec),
        compiler_params=comm_params(6),
    )(vec)


def arrange_kernel(groups, own_heads, got0, got1, vec0, vec1, gin_ref, gain_ref, mid_ref, cw_ref, cb_ref, dtb_ref, al_ref, ds_ref):
    n_seq = got0.shape[0]
    inner = DI // n_seq
    bc = CONV_CH - DI
    cols = inner // groups
    per = own_heads // groups
    for level, got in enumerate((got0, got1)):
        dts = jnp.zeros((got.shape[1], HEADS), F32)
        shared = jnp.zeros((got.shape[1], bc), F32)
        for s in range(n_seq):
            dts = dts + dot(got[s, :, :LANES].astype(F32), head_place(LANES, s, n_seq, own_heads, per), precision=HIGH)
            shared = shared + got[s, :, LANES + 2 * inner :].astype(F32)
            for g in range(groups):
                at = (g * n_seq + s) * cols
                for kind in range(2):
                    src = LANES + kind * inner + g * cols
                    gin_ref[level, :, kind * DI + at : kind * DI + at + cols] = got[s, :, src : src + cols].astype(F32)
        gin_ref[level, :, 2 * DI : 2 * DI + bc] = shared
        gin_ref[level, :, 2 * DI + bc :] = dts
    wide = (inner + bc) // LANES
    for level, vec in enumerate((vec0, vec1)):
        total = jnp.zeros((8, bc), F32)
        heads = [jnp.zeros((1, HEADS), F32)] * 3
        for s in range(n_seq):
            tiles = [vec[s, 8 * t : 8 * t + 8] for t in range(wide)]
            for g in range(groups):
                for t in range(cols // LANES):
                    tile = tiles[g * cols // LANES + t]
                    at = (g * n_seq + s) * cols + t * LANES
                    cw_ref[level, :, at : at + LANES] = tile[:TAPS]
                    cb_ref[level : level + 1, at : at + LANES] = tile[4:5]
                    mid_ref[level : level + 1, at : at + LANES] = tile[6:7]
            total = total + jnp.concatenate(tiles[inner // LANES :], axis=1)
            skip = jnp.concatenate(tiles[: inner // LANES], axis=1)
            skip = dot(skip, head_matrix(inner), NT, HIGH)
            heads[2] = heads[2] + dot(skip, head_place(8, s, n_seq, own_heads, per), precision=HIGH)[5:6]
            place = head_place(LANES, s, n_seq, own_heads, per)
            for kind in range(2):
                heads[kind] = heads[kind] + dot(tiles[kind], place, precision=HIGH)[7:8]
        cw_ref[level, :, DI:] = total[:TAPS]
        cb_ref[level : level + 1, DI:] = total[4:5]
        for ref, value in zip((dtb_ref, al_ref, ds_ref), heads):
            ref[level : level + 1] = value
        gains = vec[0, 8 * wide :]
        for s in range(1, n_seq):
            gains = gains + vec[s, 8 * wide :]
        for t in range(gains.shape[0]):
            gain_ref[level : level + 1, t * LANES : (t + 1) * LANES] = gains[t : t + 1]


def head_place(size, s, n_seq, own_heads, per):
    i = lax.broadcasted_iota(jnp.int32, (size, HEADS), 0)
    h = lax.broadcasted_iota(jnp.int32, (size, HEADS), 1)
    return ((i < own_heads) & (h == (i // per * n_seq + s) * per + i % per)).astype(F32)


def arrange(gots, vecs, groups, own_heads, width):
    piece = gots[0].shape[1]
    shapes = [
        (2, piece, 2 * DI + CONV_CH - DI + HEADS),
        (2, width),
        (2, DI),
        (2, TAPS, CONV_CH),
        (2, CONV_CH),
        (2, HEADS),
        (2, HEADS),
        (2, HEADS),
    ]
    return pl.pallas_call(
        functools.partial(arrange_kernel, groups, own_heads),
        in_specs=[VMEM_SPEC] * 4,
        out_specs=[VMEM_SPEC] * 8,
        out_shape=[jax.ShapeDtypeStruct(shape, F32) for shape in shapes],
        compiler_params=pltpu.CompilerParams(vmem_limit_bytes=40 * 2**20),
    )(*gots, *vecs)


def split_cols(x, groups, size):
    cols = x.shape[-1] // (groups * size)
    x = x.reshape(x.shape[:-1] + (groups, size, cols))
    x = jnp.moveaxis(x, -2, 0)
    return x.reshape(x.shape[:-2] + (groups * cols,))


def shards(
    tokens, resets, cotangent, w_in, w_out, gain_in, gain_mid, conv_w, conv_b, dt_bias, a_log, d_skip
):
    rows, span, width = tokens.shape
    layers = w_in.shape[0]
    n_dp, n_seq = lax.axis_size("dp"), lax.axis_size("seq")
    place = lax.axis_index("seq")
    length = span * n_seq
    own_heads = HEADS // n_seq
    groups = n_dp if own_heads % n_dp == 0 else 1
    inner = DI // n_seq
    bc_all = CONV_CH - DI

    part_z = split_cols(w_in[..., :DI], groups, n_seq)
    part_x = split_cols(w_in[..., DI : 2 * DI], groups, n_seq)
    part_bc = jnp.broadcast_to(w_in[..., 2 * DI : DI + CONV_CH], (n_seq,) + w_in.shape[:2] + (bc_all,))
    part_dt = split_cols(w_in[..., DI + CONV_CH :], groups, n_seq)
    part_dt = jnp.pad(part_dt, ((0, 0),) * 3 + ((0, LANES - own_heads),))
    parts = jnp.concatenate([part_dt, part_z, part_x, part_bc], axis=-1)
    cols = parts.shape[-1]
    marks = jnp.pad(resets.astype(F32), ((0, 8 - rows), (0, CHUNK - span)))
    marks = jnp.where(place % 2 == 0, marks, jnp.roll(marks, span, axis=1))

    def columns(x, by_head):
        x = split_cols(x, groups, n_seq)
        x = lax.dynamic_index_in_dim(x, place, 0, False)
        return jnp.repeat(x, HEAD, axis=-1) if by_head else x

    taps = jnp.concatenate([conv_w, conv_b[:, None]], axis=1)
    rest = jnp.concatenate([d_skip[:, None], jnp.zeros((layers, 2, HEADS), F32)], axis=1)
    cws = jnp.concatenate([columns(taps[..., :DI], False), columns(rest, True)], axis=1)
    cws = jnp.concatenate([cws, jnp.pad(taps[..., DI:], ((0, 0), (0, 7 - TAPS), (0, 0)))], axis=2)
    hps = columns(jnp.stack([dt_bias, a_log], axis=1), False)
    hps = jnp.broadcast_to(jnp.pad(hps, ((0, 0), (0, 0), (0, 8 - own_heads)))[..., None], (layers, 2, 8, LANES))
    gains = columns(gain_mid[:, None], False)

    def whole_rows(w):
        return lax.dynamic_slice_in_dim(lax.all_gather(w, BOTH, axis=0, tiled=True), place * inner, inner, 0)

    resid = tokens.astype(F32)
    stored = []
    for level in range(layers):
        cw, hp, gain = cws[level], hps[level], gains[level]
        before = resid
        if level == 0:
            hidden, proj, w_all, wo_all, marks_all = project_fetch(
                before, gain_in[level][None], parts[:, level], w_out[level], marks, n_dp, n_seq
            )
            win = [w_all.reshape(width, cols)]
            wout = [wo_all.reshape(DI // n_seq, width) if groups == n_dp else whole_rows(w_out[level])]
            proj, later_out, own_cot = lax.optimization_barrier((proj, w_out[1:], cotangent))
            cot = lax.all_gather(own_cot, "seq")
            for k in range(layers - 1):
                if groups == n_dp:
                    wout.append(lax.all_gather(later_out[k], "dp", axis=0, tiled=True))
                else:
                    wout.append(whole_rows(later_out[k]))
        else:
            hidden, proj = project(before, gain_in[level][None], win[level], n_seq)
        gated, squares, ys, sin = mix_fwd(proj, marks_all, cw, hp, inner)
        if level < layers - 1:
            resid, mid, scale, w_all = branch(
                gated, squares, gain, wout[level], before, parts[:, level + 1], n_dp, n_seq
            )
            win.append(w_all.reshape(width, cols))
            stored.append((before, hidden, proj, cw, hp, gain, gated, ys, sin, mid, scale))
    grad = cotangent.astype(F32)
    gots = [None] * layers
    grads_out = [None] * layers
    vecs = [None] * layers
    with_out = groups == n_dp
    for level in reversed(range(layers)):
        if level == layers - 1:
            given, more = cot, (squares, before)
        else:
            before, hidden, proj, cw, hp, gain, gated, ys, sin, mid, scale = stored[level]
            given, more = grad, (mid, scale, term, vec)
        d_proj, gc, out_term, *rest = back_mix(
            proj, marks_all, cw, hp, ys, sin, gain, gated, wout[level], given, more, n_dp, n_seq, with_out
        )
        if level == layers - 1:
            (outputs,) = rest
        else:
            gots[level + 1], vecs[level + 1] = rest
        if with_out:
            grads_out[level] = out_term
        else:
            padded = jnp.zeros((DI, width), BF)
            padded = lax.dynamic_update_slice_in_dim(padded, out_term.reshape(inner, width), place * inner, 0)
            grads_out[level] = lax.psum_scatter(padded, BOTH, scatter_dimension=0, tiled=True).astype(F32)
        grad, d_gain_in, term = back_project(
            d_proj, win[level], before, grad, gain_in[level][None], hidden, level == 0, n_dp, n_seq
        )
        tiles = jnp.moveaxis(gc.reshape(8, -1, LANES), 1, 0).reshape(-1, LANES)
        vec = jnp.concatenate([tiles, d_gain_in.reshape(-1, LANES)], axis=0)
    vecs[0] = small_sums(vec, n_dp, n_seq)
    gots[0] = term
    grads_in, *ends = arrange(gots, vecs, groups, own_heads, width)
    return (outputs, grad, grads_in, jnp.stack(grads_out), *ends)


def solution(mesh):
    placed = (
        P("dp", "seq", None),
        P("dp", "seq"),
        P("dp", "seq", None),
        P(None, BOTH, None),
        P(None, BOTH, None),
    ) + (P(),) * 7
    return jax.shard_map(
        shards,
        mesh=mesh,
        in_specs=placed,
        out_specs=(
            P("dp", "seq", None),
            P("dp", "seq", None),
            P(None, BOTH, None),
            P(None, BOTH, None),
        )
        + (P(),) * 7,
        check_vma=False,
    )
```

```python
import functools

import jax
import jax.numpy as jnp
from jax import lax
from jax.experimental import pallas as pl
from jax.experimental.pallas import tpu as pltpu
from jax.sharding import PartitionSpec as P

HEADS = 64
HEAD = 64
STATE = 128
DI = 4096
CONV_CH = 4352
CHUNK = 128
LANES = 128
TAPS = 4
EPS = 1e-05
HIGH = lax.Precision.HIGHEST
BF = jnp.bfloat16
F32 = jnp.float32
FAR = -1e30
BOTH = ("dp", "seq")


def dot(a, b, dims=((1,), (0,)), precision=None):
    return lax.dot_general(a, b, (dims, ((), ())), preferred_element_type=F32, precision=precision)


NT = ((1,), (1,))
TN = ((0,), (0,))


def head_matrix(inner):
    row = lax.broadcasted_iota(jnp.int32, (8, inner), 0)
    col = lax.broadcasted_iota(jnp.int32, (8, inner), 1)
    return (col // HEAD == row).astype(F32)


def parts_of(x, count):
    parts = []
    for _ in range(count - 1):
        part = x.astype(BF).astype(F32)
        parts.append(part)
        x = x - part
    parts.append(x)
    return jnp.concatenate(parts, axis=0)


def spread(rows, inner):
    heads = head_matrix(inner)
    return dot(parts_of(rows, 2).astype(BF), jnp.concatenate([heads, heads], axis=0).astype(BF), TN)


def by_head(heads, x):
    heads = heads.astype(BF)
    high = x.astype(BF)
    return dot(heads, high, NT) + dot(heads, (x - high.astype(F32)).astype(BF), NT)


def along(rows, ones):
    res = dot(parts_of(rows, 3).astype(BF), ones.astype(BF))
    return res[:8] + res[8:16] + res[16:]


def gaps_of(cum, heads):
    parts = parts_of(cum, 3)
    row = lax.broadcasted_iota(jnp.int32, (24, heads * CHUNK), 0)
    col = lax.broadcasted_iota(jnp.int32, (24, heads * CHUNK), 1)
    mine = (row % 8 == col // CHUNK).astype(F32)
    right = jnp.concatenate([mine, -mine * jnp.concatenate([parts] * heads, axis=1)], axis=0)
    left = jnp.concatenate([parts, jnp.ones_like(parts)], axis=0)
    return dot(left.astype(BF), right.astype(BF), TN)


def stacked_halves(x):
    lane = lax.broadcasted_iota(jnp.int32, x.shape, 1)
    zero = jnp.zeros_like(x)
    return jnp.concatenate([jnp.where(lane < HEAD, x, zero), jnp.where(lane < HEAD, zero, x)], axis=0)


def chunk_masks(marks_ref, at, first):
    here = marks_ref[pl.ds(at, 1)]
    past = marks_ref[pl.ds(jnp.maximum(at - 1, 0), 1)]
    same = 1.0 - jnp.concatenate([jnp.where(first, 1.0, past), here], axis=1)
    same = jnp.broadcast_to(same, (8, 2 * CHUNK))
    rows = [same]
    for back in range(1, TAPS - 1):
        rows.append(rows[-1] * pltpu.roll(same, back, 1))
    rows = [row[:1, CHUNK:] for row in rows]
    row = lax.broadcasted_iota(jnp.int32, (CHUNK, CHUNK), 0)
    col = lax.broadcasted_iota(jnp.int32, (CHUNK, CHUNK), 1)
    counts = dot(jnp.broadcast_to(here, (8, CHUNK)), (row <= col).astype(F32))[:1]
    return jnp.concatenate(rows + [counts] + [jnp.zeros_like(counts)] * (8 - TAPS), axis=0), counts


def chunk_rows(dt_block, hp, cr):
    raw = jnp.transpose(dt_block)[:8] + hp[0]
    dt = jnp.maximum(raw, 0.0) + jnp.log1p(jnp.exp(-jnp.abs(raw)))
    rate = jnp.exp(hp[1])
    row = lax.broadcasted_iota(jnp.int32, (CHUNK, CHUNK), 0)
    col = lax.broadcasted_iota(jnp.int32, (CHUNK, CHUNK), 1)
    cum = along(-dt * rate, (row <= col).astype(F32))
    end = cum[:, CHUNK - 1 :]
    last = cr[:, CHUNK - 1 :]
    reach = jnp.where(cr == 0.0, jnp.exp(cum), 0.0)
    to_end = jnp.where(cr == last, jnp.exp(end - cum), 0.0)
    passing = jnp.where(last == 0.0, jnp.exp(end), 0.0)
    return raw, dt, rate, cum, reach, to_end, passing


def conv_in(ext, xbc, mk, cw):
    total = cw[4:5] + cw[TAPS - 1 : TAPS] * xbc
    moved = []
    for back in range(1, TAPS):
        m = pltpu.roll(ext, back, 0)[8:] * mk[:, back - 1 : back]
        moved.append(m)
        total = total + cw[TAPS - 1 - back : TAPS - back] * m
    return total, moved


def decay_of(gaps, mask, head):
    return jnp.exp(gaps[:, head * CHUNK : (head + 1) * CHUNK] + mask)


def halved(x):
    high = x.astype(BF)
    return high, (x - high.astype(F32)).astype(BF)


def dot_parts(a, b, dims=((1,), (0,))):
    return dot(a[0], b[0], dims) + (dot(a[0], b[1], dims) + dot(a[1], b[0], dims))


def scores_of(act, inner):
    return dot_parts(halved(act[:, inner + STATE :]), halved(act[:, inner : inner + STATE]), NT)


def chunk_mask(mk, cr):
    row = lax.broadcasted_iota(jnp.int32, (CHUNK, CHUNK), 0)
    col = lax.broadcasted_iota(jnp.int32, (CHUNK, CHUNK), 1)
    return jnp.where((row >= col) & (mk[:, 3:4] == cr), 0.0, FAR)


def mix_fwd_kernel(inner, proj_ref, marks_ref, cw_ref, hp_ref, gated_ref, ss_ref, ys_ref, sin_ref, s_scr, tail_scr):
    bc = CONV_CH - DI

    @pl.when(pl.program_id(1) == 0)
    def _():
        s_scr[...] = jnp.zeros_like(s_scr)
        tail_scr[...] = jnp.zeros_like(tail_scr)

    at = pl.program_id(0) * pl.num_programs(1) + pl.program_id(1)
    masks, cr = chunk_masks(marks_ref, at, pl.program_id(1) == 0)
    mk = jnp.transpose(masks)
    cw = cw_ref[0]
    xbc = proj_ref[0, :, LANES + inner :]
    ext = jnp.concatenate([tail_scr[...], xbc], axis=0)
    tail_scr[...] = xbc[CHUNK - 8 :]
    conv, _ = conv_in(ext, xbc, mk, cw)
    act = conv * jax.nn.sigmoid(conv)
    xs = act[:, :inner]
    bmat = halved(act[:, inner : inner + STATE])
    cmat = halved(act[:, inner + STATE :])
    raw, dt, rate, cum, reach, to_end, passing = chunk_rows(proj_ref[0, :, :LANES], hp_ref[0], cr)
    gaps = gaps_of(cum, inner // HEAD)
    mask = chunk_mask(mk, cr)
    xd = xs * spread(dt, inner)
    xdb = halved(xd)
    state = s_scr[...]
    sin_ref[0, 0] = state
    scores = dot_parts(cmat, bmat, NT)
    y = spread(reach, inner) * dot_parts(cmat, halved(state))
    inner_parts = []
    for j in range(inner // LANES):
        w = [scores * decay_of(gaps, mask, 2 * j + i) for i in range(2)]
        x = [stacked_halves(part[:, j * LANES : (j + 1) * LANES]) for part in xdb]
        inner_parts.append(dot_parts(halved(jnp.concatenate(w, axis=1)), x))
    y = y + jnp.concatenate(inner_parts, axis=1)
    ys_ref[0] = y
    keep = jnp.sum(passing * head_matrix(inner), axis=0, keepdims=True)
    s_scr[...] = keep * state + dot_parts(bmat, halved(xd * spread(to_end, inner)), TN)
    z = proj_ref[0, :, LANES : LANES + inner]
    gated = (y + cw[5:6, :inner] * xs) * (z * jax.nn.sigmoid(z))
    gated_ref[0] = gated
    ss_ref[pl.ds(at, 1)] = by_head(jnp.ones((8, inner), F32), gated * gated)[:1]


def mix_fwd(proj, marks, cws, hps, level, inner):
    rows, length, cols = proj.shape
    chunks = length // CHUNK
    bc = CONV_CH - DI
    whole = lambda r, c: (0, 0)
    return pl.pallas_call(
        functools.partial(mix_fwd_kernel, inner),
        grid=(rows, chunks),
        in_specs=[
            pl.BlockSpec((1, CHUNK, cols), lambda r, c: (r, c, 0)),
            pl.BlockSpec(marks.shape, whole),
            pl.BlockSpec((1,) + cws.shape[1:], lambda r, c: (level, 0, 0)),
            pl.BlockSpec((1,) + hps.shape[1:], lambda r, c: (level, 0, 0, 0)),
        ],
        out_specs=[
            pl.BlockSpec((1, CHUNK, inner), lambda r, c: (r, c, 0)),
            pl.BlockSpec((rows * chunks, CHUNK), whole),
            pl.BlockSpec((1, CHUNK, inner), lambda r, c: (r, c, 0)),
            pl.BlockSpec((1, 1, STATE, inner), lambda r, c: (r, c, 0, 0)),
        ],
        out_shape=[
            jax.ShapeDtypeStruct((rows, length, inner), F32),
            jax.ShapeDtypeStruct((rows * chunks, CHUNK), F32),
            jax.ShapeDtypeStruct((rows, length, inner), F32),
            jax.ShapeDtypeStruct((rows, chunks, STATE, inner), F32),
        ],
        scratch_shapes=[pltpu.VMEM((STATE, inner), F32), pltpu.VMEM((8, inner + bc), F32)],
        compiler_params=pltpu.CompilerParams(
            dimension_semantics=("arbitrary", "arbitrary"), vmem_limit_bytes=60 * 2**20
        ),
        cost_estimate=pl.CostEstimate(flops=3 * 10**9, bytes_accessed=18 * 2**20, transcendentals=10**6),
    )(proj, marks, cws, hps)


def silu_slope(v, s):
    return s * (1.0 + v * (1.0 - s))


def mix_bwd_step(
    inner, chunks, proj_ref, prev_ref, marks_ref, cw_ref, hp_ref, ys_ref, sin_ref, d_mid, scale_ref, cube_ref, gain_ref,
    dp_ref, gc_ref, ds_scr, gam_scr, head_scr, gh_ref,
):
    step = pl.program_id(1)

    @pl.when((step == 0) & (pl.program_id(0) == 0))
    def _():
        gc_ref[...] = jnp.zeros_like(gc_ref)
        gh_ref[...] = jnp.zeros_like(gh_ref)

    @pl.when(step == 0)
    def _():
        ds_scr[...] = jnp.zeros_like(ds_scr)
        gam_scr[...] = jnp.zeros_like(gam_scr)
        head_scr[...] = jnp.zeros_like(head_scr)

    at = pl.program_id(0) * chunks + chunks - 1 - step
    masks, cr = chunk_masks(marks_ref, at, step == chunks - 1)
    mk = jnp.transpose(masks)
    cw = cw_ref[0]
    heads = head_matrix(inner)
    xbc = proj_ref[0, :, LANES + inner :]
    ext = jnp.concatenate([prev_ref[0, :, LANES + inner :], xbc], axis=0)
    conv, moved = conv_in(ext, xbc, mk, cw)
    sig = jax.nn.sigmoid(conv)
    act = conv * sig
    xs = act[:, :inner]
    bmat = act[:, inner : inner + STATE].astype(BF)
    cmat = act[:, inner + STATE :].astype(BF)
    raw, dt, rate, cum, reach, to_end, passing = chunk_rows(proj_ref[0, :, :LANES], hp_ref[0], cr)
    norm = [scale_ref[pl.ds(at, 1)], cube_ref[pl.ds(at, 1)], jnp.zeros((6, CHUNK), F32)]
    cols = jnp.transpose(jnp.concatenate(norm, axis=0))
    gaps = gaps_of(cum, inner // HEAD)
    mask = chunk_mask(mk, cr)
    dt_e = spread(dt, inner)
    reach_e = spread(reach, inner)
    end_e = spread(to_end, inner)
    xd = xs * dt_e
    xdb = xd.astype(BF)

    z = proj_ref[0, :, LANES : LANES + inner]
    sz = jax.nn.sigmoid(z)
    silu_z = z * sz
    ys = ys_ref[0]
    skip = cw[5:6, :inner]
    y = ys + skip * xs
    gated = y * silu_z
    r_mid = d_mid * cols[:, :1]
    d_gated = r_mid * gain_ref[...] - gated * cols[:, 1:2]
    d_gain = jnp.sum(r_mid * gated, axis=0, keepdims=True)
    dy = d_gated * silu_z
    dyb = halved(dy)
    dz = d_gated * y * silu_slope(z, sz)

    state = sin_ref[0, 0]
    d_state = ds_scr[...]
    dsb = d_state.astype(BF)
    scores = scores_of(act, inner)
    reached = (reach_e * dy).astype(BF)
    ended = (end_e * xd).astype(BF)
    d_xd = end_e * dot_parts(halved(act[:, inner : inner + STATE]), halved(d_state))
    d_scores = jnp.zeros((CHUNK, CHUNK), F32)
    parts = []
    for j in range(inner // LANES):
        lanes = slice(j * LANES, (j + 1) * LANES)
        pair_dy = [stacked_halves(part[:, lanes]) for part in dyb]
        d_w = dot(pair_dy[0], xdb[:, lanes], NT)
        ws = []
        for i in range(2):
            decay = decay_of(gaps, mask, 2 * j + i)
            ws.append(scores * decay)
            d_scores = d_scores + d_w[i * CHUNK : (i + 1) * CHUNK] * decay
        parts.append(dot_parts(halved(jnp.concatenate(ws, axis=0)), pair_dy, TN))
    d_xd = d_xd + jnp.concatenate(parts, axis=1)
    dgb = d_scores.astype(BF)
    d_c = dot(reached, state.astype(BF), NT) + dot(dgb, bmat)
    d_b = dot(ended, dsb, NT) + dot(dgb, cmat, TN)
    keep = jnp.sum(passing * heads, axis=0, keepdims=True)
    new_ds = keep * d_state + dot(cmat, reached, TN)
    alpha = by_head(heads, dy * ys)
    beta = by_head(heads, xs * d_xd)
    lane = lax.broadcasted_iota(jnp.int32, (8, CHUNK), 1)
    d_cum = alpha - dt * beta + jnp.where(lane == CHUNK - 1, gam_scr[...], 0.0)
    row = lax.broadcasted_iota(jnp.int32, (CHUNK, CHUNK), 0)
    col = lax.broadcasted_iota(jnp.int32, (CHUNK, CHUNK), 1)
    d_log = along(d_cum, (row >= col).astype(F32))
    d_dt = beta - rate * d_log
    d_raw = d_dt * jax.nn.sigmoid(raw)
    gh_ref[0] += d_raw
    gh_ref[1] += -rate * dt * d_log
    ds_scr[...] = new_ds
    gam_scr[...] = jnp.broadcast_to(
        jnp.sum(heads * jnp.sum(new_ds * state, axis=0, keepdims=True), axis=1, keepdims=True), gam_scr.shape
    )
    d_xs = dt_e * d_xd + skip * dy

    d_conv = jnp.concatenate([d_xs, d_b, d_c], axis=1) * silu_slope(conv, sig)
    d_xbc = cw[TAPS - 1 : TAPS] * d_conv
    gc_ref[TAPS - 1 : TAPS] += jnp.sum(d_conv * xbc, axis=0, keepdims=True)
    for back in range(1, TAPS):
        u = d_conv * mk[:, back - 1 : back]
        full = jnp.concatenate([u, head_scr[back - 1]], axis=0)
        head_scr[back - 1] = u[:8]
        d_xbc = d_xbc + cw[TAPS - 1 - back : TAPS - back] * pltpu.roll(full, CHUNK + 8 - back, 0)[:CHUNK]
        gc_ref[TAPS - 1 - back : TAPS - back] += jnp.sum(d_conv * moved[back - 1], axis=0, keepdims=True)
    gc_ref[4:5] += jnp.sum(d_conv, axis=0, keepdims=True)
    gc_ref[5:6, :inner] += jnp.sum(dy * xs, axis=0, keepdims=True)
    gc_ref[6:7, :inner] += d_gain
    dp_ref[0, :, LANES : LANES + inner] = dz.astype(BF)
    dp_ref[0, :, LANES + inner :] = d_xbc.astype(BF)

    @pl.when((step == chunks - 1) & (pl.program_id(0) == pl.num_programs(0) - 1))
    def _():
        for kind in range(2):
            sums = jnp.concatenate([gh_ref[kind], jnp.zeros((LANES - 8, CHUNK), F32)], axis=0)
            sums = dot(jnp.ones((8, CHUNK), F32), sums, NT, HIGH)
            gc_ref[7:8, kind * LANES : (kind + 1) * LANES] = sums[:1]

    d_rawt = jnp.transpose(jnp.concatenate([d_raw, jnp.zeros((LANES - 8, CHUNK), F32)], axis=0))
    dp_ref[0, :, :LANES] = d_rawt.astype(BF)


MESH = pl.DeviceIdType.MESH


def meet(peers):
    barrier = pltpu.get_barrier_semaphore()
    count = 0
    for here, peer in peers:
        if here is None:
            count = count + 1
            pl.semaphore_signal(barrier, inc=1, device_id=peer, device_id_type=MESH)
        else:
            count = count + here.astype(jnp.int32)

            @pl.when(here)
            def _():
                pl.semaphore_signal(barrier, inc=1, device_id=peer, device_id_type=MESH)

    pl.semaphore_wait(barrier, count)


def line_place(n_seq):
    me = lax.axis_index("seq")
    return me // 2, me % 2, {"seq": me + 1 - 2 * (me % 2)}, {"seq": me - 2}, {"seq": me + 2}


def line_peers(n):
    chip, core, sib, left, right = line_place(2 * n)
    return [(None, sib), (chip > 0, left), (chip < n - 1, right)]


def all_peers(axis, size):
    me = lax.axis_index(axis)
    return [(None, {axis: (me + k) % size}) for k in range(1, size)]


def remote(src, dst, send, recv, device):
    return pltpu.make_async_remote_copy(
        src_ref=src, dst_ref=dst, send_sem=send, recv_sem=recv, device_id=device, device_id_type=MESH
    )


def share_start(axis, size, source, slots, send, recv):
    me = lax.axis_index(axis)
    copies = []
    for k in range(1, size):
        to = (me + k) % size
        copy = remote(source(to), slots.at[k - 1], send.at[k - 1], recv.at[k - 1], {axis: to})
        copy.start()
        copies.append(copy)
    return copies


def share_sum(copies, own, slots):
    total = own.astype(F32)
    for k, copy in enumerate(copies):
        copy.wait_recv()
        total = total + slots[k].astype(F32)
    return total


def share_end(copies):
    for copy in copies:
        copy.wait_send()


def line_gather(n, rows, span, buf, sems, use, begun=None, between=None, ready=None):
    right_s, left_s, sib_s, line_r, sib_r = sems
    chip, core, sib, left, right = line_place(2 * n)
    have_left, have_right = chip > 0, chip < n - 1

    def block(r, j, c):
        return buf.at[r, j, pl.ds(pl.multiple_of(c * span, span), span)]

    def to_sib(r, j, c):
        at = j * rows + r
        return remote(block(r, j, c), block(r, j, c), sib_s.at[at], sib_r.at[at], sib)

    def to_right(r, j):
        at = j * rows + r
        return remote(block(r, j, core), block(r, j, core), right_s.at[at], line_r.at[at], right)

    def to_left(r, j):
        at = j * rows + r
        return remote(block(r, j, core), block(r, j, core), left_s.at[at], line_r.at[at], left)

    def pass_on(r, j, way):
        if way >= 0:

            @pl.when(have_right)
            def _():
                to_right(r, j).start()

        if way <= 0:

            @pl.when(have_left)
            def _():
                to_left(r, j).start()

        to_sib(r, j, core).start()

    def finish(j):
        for r in range(rows):
            to_sib(r, j, 1 - core).wait_recv()
        use(j)

    for r in range(rows):
        if ready is not None:
            ready(r)
        pass_on(r, chip, 0)
    if begun is not None:
        begun()
    finish(chip)

    def step(t, _):
        low, high = chip - t, chip + t
        for r in range(rows):

            @pl.when(low >= 0)
            def _():
                to_right(r, low).wait_recv()
                pass_on(r, low, 1)

            @pl.when(high < n)
            def _():
                to_left(r, high).wait_recv()
                pass_on(r, high, -1)

        def one(k, _):
            j = jnp.where(k == 0, low, high)

            @pl.when((j >= 0) & (j < n))
            def _():
                finish(j)

            return 0

        lax.fori_loop(0, 2, one, 0)
        if between is not None:
            between(t)
        return 0

    lax.fori_loop(1, n, step, 0)

    def done(j, _):
        for r in range(rows):
            to_sib(r, j, core).wait_send()

            @pl.when(have_right & (j <= chip))
            def _():
                to_right(r, j).wait_send()

            @pl.when(have_left & (j >= chip))
            def _():
                to_left(r, j).wait_send()

        return 0

    lax.fori_loop(0, n, done, 0)


def dma(*counts):
    return [pltpu.SemaphoreType.DMA((count,)) for count in counts]


class LineSum:
    def __init__(self, n, rows, emit, own, sib_out, sib_in, out, into, sems):
        self.n, self.rows, self.emit = n, rows, emit
        self.own, self.sib_out, self.sib_in, self.out, self.into = own, sib_out, sib_in, out, into
        self.sib_s, self.right_s, self.left_s, self.sib_r, self.right_r, self.left_r = sems
        self.chip, self.core, self.sib, self.left, self.right = line_place(2 * n)

    @staticmethod
    def scratch(n, rows, span, wide):
        shape = (n, rows, span, wide)
        k = n * rows
        return (
            [pltpu.VMEM(shape, F32)]
            + [pltpu.VMEM(shape, BF)] * 3
            + [pltpu.VMEM((n + 1,) + shape[1:], BF)]
            + dma(k, k, k, k, k, k)
        )

    def to_sib(self, j, r):
        at = j * self.rows + r
        return remote(self.sib_out.at[j, r], self.sib_in.at[j, r], self.sib_s.at[at], self.sib_r.at[at], self.sib)

    def to_right(self, j, r):
        at = j * self.rows + r
        return remote(self.out.at[j, r], self.into.at[j, r], self.right_s.at[at], self.right_r.at[at], self.right)

    def left_copy(self, j, r, owner, device):
        at = j * self.rows + r
        slot = jnp.where(j == owner, self.n, j)
        return remote(self.out.at[j, r], self.into.at[slot, r], self.left_s.at[at], self.left_r.at[at], device)

    def to_left(self, j, r):
        return self.left_copy(j, r, self.chip - 1, self.left)

    def from_right(self, j, r):
        return self.left_copy(j, r, self.chip, self.right)

    def make(self, j):
        self.emit(j)
        for r in range(self.rows):
            self.to_sib(j, r).start()

    def right_j(self, tau):
        j = self.n - 1 - (tau - self.chip)
        return j, (tau >= self.chip) & (j > self.chip)

    def left_j(self, tau):
        j = tau - (self.n - 1 - self.chip)
        return j, (j >= 0) & (j < self.chip)

    def prepare(self, tau):
        def one(k, _):
            jr, on_r = self.right_j(tau)
            jl, on_l = self.left_j(tau)
            j = jnp.where(k == 0, jr, jl)

            @pl.when(((k == 0) & on_r) | ((k == 1) & on_l))
            def _():
                self.make(j)

            return 0

        lax.fori_loop(0, 2, one, 0)

    def step(self, tau):
        jr, on_r = self.right_j(tau)
        jl, on_l = self.left_j(tau)
        own, sib_in, out, into = self.own, self.sib_in, self.out, self.into
        for r in range(self.rows):

            @pl.when(on_r)
            def _():
                self.to_sib(jr, r).wait_recv()

                @pl.when(self.chip > 0)
                def _():
                    self.to_right(jr, r).wait_recv()
                    out[jr, r] = (own[jr, r] + sib_in[jr, r].astype(F32) + into[jr, r].astype(F32)).astype(BF)

                @pl.when(self.chip == 0)
                def _():
                    out[jr, r] = (own[jr, r] + sib_in[jr, r].astype(F32)).astype(BF)

                self.to_right(jr, r).start()

            @pl.when(on_l)
            def _():
                self.to_sib(jl, r).wait_recv()

                @pl.when(self.chip < self.n - 1)
                def _():
                    self.from_right(jl, r).wait_recv()
                    out[jl, r] = (own[jl, r] + sib_in[jl, r].astype(F32) + into[jl, r].astype(F32)).astype(BF)

                @pl.when(self.chip == self.n - 1)
                def _():
                    out[jl, r] = (own[jl, r] + sib_in[jl, r].astype(F32)).astype(BF)

                self.to_left(jl, r).start()

    def finish(self, r):
        chip, own, into = self.chip, self.own, self.into
        self.to_sib(chip, r).wait_recv()
        own[chip, r] = own[chip, r] + self.sib_in[chip, r].astype(F32)

        @pl.when(chip > 0)
        def _():
            self.to_right(chip, r).wait_recv()
            own[chip, r] = own[chip, r] + into[chip, r].astype(F32)

        @pl.when(chip < self.n - 1)
        def _():
            self.from_right(chip, r).wait_recv()
            own[chip, r] = own[chip, r] + into[self.n, r].astype(F32)

    def end(self):
        def done(j, _):
            for r in range(self.rows):
                self.to_sib(j, r).wait_send()

                @pl.when(j > self.chip)
                def _():
                    self.to_right(j, r).wait_send()

                @pl.when(j < self.chip)
                def _():
                    self.to_left(j, r).wait_send()

            return 0

        lax.fori_loop(0, self.n, done, 0)

    def run(self, between=None, before_end=None, to_end=True):
        self.prepare(0)

        def step(tau, _):
            self.step(tau)
            self.prepare(tau + 1)
            if between is not None:
                between(tau)
            return 0

        lax.fori_loop(0, self.n - 1, step, 0)
        self.make(self.chip)
        if before_end is not None:
            before_end()
        if to_end:
            for r in range(self.rows):
                self.finish(r)
            self.end()


def halves(own, so, j, core, start, p, rows, span):
    stop = start + p.shape[1]
    for r in range(rows):
        low, high = p[r * CHUNK : r * CHUNK + span], p[r * CHUNK + span : (r + 1) * CHUNK]
        own[j, r, :, start:stop] = jnp.where(core == 0, low, high)
        so[j, r, :, start:stop] = jnp.where(core == 0, high, low).astype(BF)


def dp_neighbours():
    d = lax.axis_index("dp")
    return d, d + 1 - 2 * (d % 2), (d + 2) % 4, 3 - d


def either(even, yes, no):
    @pl.when(even)
    def _():
        yes()

    @pl.when(jnp.logical_not(even))
    def _():
        no()


class Spread:
    def __init__(self, n_dp, at, count, sems):
        self.n_dp, self.at, self.count = n_dp, at, count
        self.s, self.r = sems

    @staticmethod
    def scratch(n_dp, count):
        return dma((n_dp - 1) * count, (n_dp - 1) * count)

    def copy(self, kind, owner, i, to):
        where = self.at(owner, i)
        sem = kind * self.count + i
        return remote(where, where, self.s.at[sem], self.r.at[sem], {"dp": to})

    def hand(self, i):
        d = lax.axis_index("dp")
        if self.n_dp == 4:
            d, x, y, _ = dp_neighbours()
            self.copy(0, d, i, x).start()
            self.copy(1, d, i, y).start()
        else:
            for k in range(1, self.n_dp):
                self.copy(k - 1, d, i, (d + k) % self.n_dp).start()

    def relay(self, i):
        if self.n_dp == 4:
            d, x, y, _ = dp_neighbours()

            def by_x():
                self.copy(0, x, i, x).wait_recv()
                self.copy(2, x, i, y).start()

            def by_y():
                self.copy(1, y, i, y).wait_recv()
                self.copy(2, y, i, x).start()

            either(i % 2 == 0, by_x, by_y)

    def end(self, i):
        d = lax.axis_index("dp")
        if self.n_dp == 4:
            d, x, y, across = dp_neighbours()

            def by_x():
                self.copy(1, y, i, y).wait_recv()
                self.copy(2, across, i, y).wait_recv()
                self.copy(2, x, i, y).wait_send()

            def by_y():
                self.copy(0, x, i, x).wait_recv()
                self.copy(2, across, i, x).wait_recv()
                self.copy(2, y, i, x).wait_send()

            either(i % 2 == 0, by_x, by_y)
            self.copy(0, d, i, x).wait_send()
            self.copy(1, d, i, y).wait_send()
        else:
            for k in range(1, self.n_dp):
                source = (d - k + self.n_dp) % self.n_dp
                self.copy(k - 1, source, i, source).wait_recv()
                self.copy(k - 1, d, i, (d + k) % self.n_dp).wait_send()


def spread_halves(n_dp, place, own, sems):
    half = own.shape[0] // 2
    return Spread(n_dp, lambda owner, i: place.at[owner, pl.ds(pl.multiple_of(i * half, half), half)], 2, sems)


class DpSum:
    def __init__(self, n_dp, term, slots, piece, sems):
        self.n_dp, self.term, self.slots, self.piece = n_dp, term, slots, piece
        self.count = term.shape[1] // piece
        self.s, self.r = sems

    @staticmethod
    def scratch(n_dp, rows, cols, piece):
        count = (n_dp - 1) * (rows // piece)
        return [pltpu.VMEM((n_dp - 1, rows, cols), BF)] + dma(count, count)

    def rows_of(self, i):
        return pl.ds(pl.multiple_of(i * self.piece, self.piece), self.piece)

    def copy(self, kind, source, i, to):
        sem = kind * self.count + i
        return remote(source, self.slots.at[kind, self.rows_of(i)], self.s.at[sem], self.r.at[sem], {"dp": to})

    def part(self, kind, owner, i, to):
        return self.copy(kind, self.term.at[owner, self.rows_of(i)], i, to)

    def on(self, i):
        return self.copy(2, self.slots.at[1, self.rows_of(i)], i, self.axes(i)[1])

    def axes(self, i):
        d, x, y, across = dp_neighbours()
        even = i % 2 == 0
        return jnp.where(even, x, y), jnp.where(even, y, x), across, d

    def send(self, i):
        if self.n_dp == 4:
            first, second, across, d = self.axes(i)
            self.part(1, across, i, first).start()
            self.part(0, first, i, first).start()
        else:
            d = lax.axis_index("dp")
            for k in range(1, self.n_dp):
                to = (d + k) % self.n_dp
                self.part(k - 1, to, i, to).start()

    def middle(self, i):
        if self.n_dp == 4:
            first, second, across, d = self.axes(i)
            here = self.rows_of(i)
            self.part(1, across, i, first).wait_recv()
            self.slots[1, here] = (self.term[second, here].astype(F32) + self.slots[1, here].astype(F32)).astype(BF)
            self.on(i).start()

    def total(self, i):
        d = lax.axis_index("dp")
        here = self.rows_of(i)
        total = self.term[d, here].astype(F32)
        if self.n_dp == 4:
            first, second, across, d = self.axes(i)
            self.part(0, first, i, first).wait_recv()
            self.on(i).wait_recv()
            return total + self.slots[0, here].astype(F32) + self.slots[2, here].astype(F32)
        for k in range(1, self.n_dp):
            to = (d + k) % self.n_dp
            self.part(k - 1, to, i, to).wait_recv()
            total = total + self.slots[k - 1, here].astype(F32)
        return total

    def end(self, i):
        if self.n_dp == 4:
            first, second, across, d = self.axes(i)
            self.part(1, across, i, first).wait_send()
            self.part(0, first, i, first).wait_send()
            self.on(i).wait_send()
        else:
            d = lax.axis_index("dp")
            for k in range(1, self.n_dp):
                to = (d + k) % self.n_dp
                self.part(k - 1, to, i, to).wait_send()


class Cut:
    def __init__(self, level, w_ref, dts_ref, parts, sems):
        n_seq, _, cols = parts.shape
        inner = DI // n_seq
        groups = self.groups(n_seq, sems.shape[0])
        size = inner // groups
        bc = CONV_CH - DI
        pairs = [(dts_ref, parts.at[:, :, pl.ds(0, LANES)])]
        for s in range(n_seq):
            for kind in range(2):
                for g in range(groups):
                    source = w_ref.at[level, :, pl.ds(kind * DI + (g * n_seq + s) * size, size)]
                    pairs.append((source, parts.at[s, :, pl.ds(LANES + kind * inner + g * size, size)]))
            pairs.append((w_ref.at[level, :, pl.ds(2 * DI, bc)], parts.at[s, :, pl.ds(cols - bc, bc)]))
        self.copies = [pltpu.make_async_copy(a, b, sems.at[i]) for i, (a, b) in enumerate(pairs)]

    @staticmethod
    def count(n_seq, groups):
        return 1 + n_seq * (2 * groups + 1)

    @staticmethod
    def groups(n_seq, count):
        return ((count - 1) // n_seq - 1) // 2

    def start(self):
        for copy in self.copies:
            copy.start()

    def wait(self):
        for copy in self.copies:
            copy.wait()


class Fetch:
    def __init__(self, n_dp, n_seq, parts, wv, refs):
        self.n_dp, self.n_seq, self.parts, self.wv = n_dp, n_seq, parts, wv
        self.a_s, self.a_r = refs[:2]
        self.spread = Spread(n_dp, lambda owner, i: wv.at[owner, i], n_seq, refs[2:4])

    @staticmethod
    def scratch(n_dp, n_seq):
        return dma(n_seq, n_seq) + Spread.scratch(n_dp, n_seq)

    def across(self, i):
        me, d = lax.axis_index("seq"), lax.axis_index("dp")
        to = (me + i) % self.n_seq
        return remote(self.parts.at[to], self.wv.at[d, me], self.a_s.at[to], self.a_r.at[me], {"seq": to})

    def place(self, i):
        return (lax.axis_index("seq") - i + self.n_seq) % self.n_seq

    def arrival(self, i):
        me, d = lax.axis_index("seq"), lax.axis_index("dp")
        source = self.place(i)
        return remote(self.parts.at[me], self.wv.at[d, source], self.a_s.at[me], self.a_r.at[source], {"seq": source})

    def start(self):
        def go(i, _):
            self.across(i).start()
            return 0

        lax.fori_loop(1, self.n_seq, go, 0)
        me, d = lax.axis_index("seq"), lax.axis_index("dp")
        self.wv[d, me] = self.parts[me]
        self.spread.hand(me)

    def pull(self, first, last):
        def one(i, _):
            @pl.when(i < self.n_seq)
            def _():
                self.arrival(i).wait_recv()
                self.spread.hand(self.place(i))

                @pl.when(i >= 2)
                def _():
                    self.spread.relay(self.place(i - 2))

            return 0

        lax.fori_loop(first, last, one, 0)

    def tail(self):
        self.spread.relay(self.place(self.n_seq - 2))
        self.spread.relay(self.place(self.n_seq - 1))

    def end(self):
        def ended(i, _):
            self.spread.end(i)
            return 0

        lax.fori_loop(0, self.n_seq, ended, 0)

    def sent(self):
        def one(i, _):
            self.across(i).wait_send()
            return 0

        lax.fori_loop(1, self.n_seq, one, 0)


class Pieces:
    def __init__(self, n_dp, n_seq, term, got, refs):
        self.n_seq, self.got = n_seq, got
        self.piece = got.shape[1]
        slots, dp_s, dp_r, self.sums, self.seq_s, self.seq_r = refs
        self.sum = DpSum(n_dp, term, slots, self.piece, (dp_s, dp_r))
        self.per = LANES // self.piece
        self.tiles = term.shape[1] // LANES

    @staticmethod
    def scratch(n_dp, n_seq, rows, cols):
        piece = rows // n_seq
        return DpSum.scratch(n_dp, rows, cols, piece) + [pltpu.VMEM((n_seq, piece, cols), BF)] + dma(n_seq, n_seq)

    def tile(self, i):
        if 2 * self.tiles == self.n_seq:
            return (lax.axis_index("seq") // 2 + 1 + i) % self.tiles
        return i

    def each(self, i, act):
        def one(k, _):
            act(i * self.per + k, self.tile(i) * self.per + k)
            return 0

        lax.fori_loop(0, self.per, one, 0)

    def tiles_do(self, first, last, *acts):
        def one(i, _):
            @pl.when((i >= 0) & (i < self.tiles))
            def _():
                for act in acts:
                    act(i)

            return 0

        lax.fori_loop(first, last, one, 0)

    def over_seq(self, s):
        me = lax.axis_index("seq")
        return remote(self.sums.at[s], self.got.at[me], self.seq_s.at[s], self.seq_r.at[me], {"seq": s})

    def from_seq(self, s):
        me = lax.axis_index("seq")
        return remote(self.sums.at[me], self.got.at[s], self.seq_s.at[me], self.seq_r.at[s], {"seq": s})

    def send(self, i):
        self.each(i, lambda p, s: self.sum.send(p))

    def middle(self, i):
        self.each(i, lambda p, s: self.sum.middle(p))

    def last(self, i):
        me = lax.axis_index("seq")

        def finish(p, s):
            total = self.sum.total(p).astype(BF)

            def away():
                self.sums[s] = total
                self.over_seq(s).start()

            def stay():
                self.got[s] = total

            either(s != me, away, stay)

        self.each(i, finish)

    def end(self):
        me = lax.axis_index("seq")

        def sent(p, s):
            self.sum.end(p)

        self.tiles_do(0, self.tiles, lambda i: self.each(i, sent))

        def one(s, _):
            @pl.when(s != me)
            def _():
                self.over_seq(s).wait_send()
                self.from_seq(s).wait_recv()

            return 0

        lax.fori_loop(0, self.n_seq, one, 0)


class Loads:
    def __init__(self, sources, places, sems):
        self.copies = [pltpu.make_async_copy(s, p, sems.at[i]) for i, (s, p) in enumerate(zip(sources, places))]

    @staticmethod
    def scratch(*arrays):
        return [pltpu.VMEM(x.shape, x.dtype) for x in arrays] + dma(len(arrays))

    def start(self):
        for copy in self.copies:
            copy.start()

    def wait(self, *which):
        for i in which:
            self.copies[i].wait()


VMEM_SPEC = pl.BlockSpec(memory_space=pltpu.VMEM)
ANY_SPEC = pl.BlockSpec(memory_space=pl.ANY)


def comm_params(name):
    return pltpu.CompilerParams(collective_id=name, has_side_effects=True, vmem_limit_bytes=60 * 2**20)


def project_kernel(n, n_dp, level, x_ref, gain_ref, *refs):
    n_seq = 2 * n
    rows, span, width = x_ref.shape
    wo_ref, marks_ref, win_ref, dts_ref = refs[:4]
    hid_ref, proj_ref, w_ref, wout_ref, all_ref = refs[4:9]
    cut = Cut(level, win_ref, dts_ref, *refs[9:11])
    cut.start()
    buf, wv, po = refs[11:14]
    line, (w_sem, hid_sem, out_sem) = refs[14:19], refs[19:22]
    get = Fetch(n_dp, n_seq, refs[9], wv, refs[22:26])
    o_s, o_r, m_s, m_r, mall = refs[26:]
    chip, core, sib, left, right = line_place(n_seq)
    me = lax.axis_index("seq")
    d = lax.axis_index("dp")
    for r in range(rows):
        x = x_ref[r].astype(F32)
        scale = lax.rsqrt(jnp.mean(x * x, axis=-1, keepdims=True) + EPS)
        buf[r, chip, pl.ds(pl.multiple_of(core * span, span), span)] = (x * scale * gain_ref[...]).astype(BF)
    meet(all_peers("seq", n_seq) + all_peers("dp", n_dp))
    cut.wait()

    def out_copies(j):
        return (
            pltpu.make_async_copy(buf.at[:, j], hid_ref.at[:, j], hid_sem.at[j]),
            pltpu.make_async_copy(po.at[j], proj_ref.at[:, pl.ds(j * CHUNK, CHUNK)], out_sem.at[j]),
        )

    def use(j):
        block = buf[:, j].reshape(rows * CHUNK, width)
        res = dot(block, wv[...].reshape(width, wv.shape[-1]))
        for r in range(rows):
            po[j, r] = res[r * CHUNK : (r + 1) * CHUNK]
        for copy in out_copies(j):
            copy.start()

    def done(j, _):
        for copy in out_copies(j):
            copy.wait()
        return 0

    outs = spread_halves(n_dp, wout_ref, wo_ref, (o_s, o_r))

    def marks_copy(i):
        to = (me + i) % n_seq
        return remote(marks_ref, mall.at[me], m_s.at[to], m_r.at[me], {"seq": to})

    def marks_in(i):
        source = (me - i + n_seq) % n_seq
        return remote(marks_ref, mall.at[source], m_s.at[me], m_r.at[source], {"seq": source})

    get.start()
    for i in range(1, n_seq):
        marks_copy(i).start()
    mall[me] = marks_ref[...]

    def begun():
        get.pull(1, n_seq)
        wout_ref[d] = wo_ref[...]
        for i in range(2):
            outs.hand(i)
        get.tail()

    line_gather(n, rows, span, buf, line, lambda j: None, begun)
    for i in range(1, n_seq):
        marks_in(i).wait_recv()
    for r in range(rows):
        for j in range(n):
            all_ref[r * n + j : r * n + j + 1] = mall[2 * j, r : r + 1] + mall[2 * j + 1, r : r + 1]
    for i in range(2):
        outs.relay(i)

    get.end()
    keep = pltpu.make_async_copy(wv, w_ref, w_sem.at[0])
    keep.start()

    def each(j, _):
        use(j)
        return 0

    lax.fori_loop(0, n, each, 0)
    for i in range(2):
        outs.end(i)

    get.sent()
    for i in range(1, n_seq):
        marks_copy(i).wait_send()
    lax.fori_loop(0, n, done, 0)
    keep.wait()


def parts_shape(w_in, n_seq):
    cols = LANES + 2 * (DI // n_seq) + CONV_CH - DI
    return jax.ShapeDtypeStruct((n_seq, w_in.shape[1], cols), BF)


def project(x, gain, wo, marks, w_in, dts, level, groups, n_dp, n_seq):
    rows, span, width = x.shape
    n = n_seq // 2
    k = n * rows
    parts = parts_shape(w_in, n_seq)
    cols = parts.shape[2]
    w_shape = (n_dp, n_seq) + parts.shape[1:]
    return pl.pallas_call(
        functools.partial(project_kernel, n, n_dp, level),
        in_specs=[VMEM_SPEC] * 4 + [ANY_SPEC] * 2,
        out_specs=[ANY_SPEC] * 3 + [VMEM_SPEC] * 2,
        out_shape=[
            jax.ShapeDtypeStruct((rows, n, CHUNK, width), BF),
            jax.ShapeDtypeStruct((rows, n * CHUNK, cols), F32),
            jax.ShapeDtypeStruct(w_shape, BF),
            jax.ShapeDtypeStruct((n_dp,) + wo.shape, BF),
            jax.ShapeDtypeStruct((k, CHUNK), F32),
        ],
        scratch_shapes=[pltpu.VMEM(parts.shape, BF)]
        + dma(Cut.count(n_seq, groups))
        + [
            pltpu.VMEM((rows, n, CHUNK, width), BF),
            pltpu.VMEM(w_shape, BF),
            pltpu.VMEM((n, rows, CHUNK, cols), F32),
        ]
        + dma(k, k, k, k, k, 1, n, n)
        + Fetch.scratch(n_dp, n_seq)
        + Spread.scratch(n_dp, 2)
        + dma(n_seq, n_seq)
        + [pltpu.VMEM((n_seq,) + marks.shape, F32)],
        compiler_params=comm_params(0),
        cost_estimate=pl.CostEstimate(flops=6 * 10**9, bytes_accessed=20 * 2**20, transcendentals=0),
    )(x, gain, wo, marks, w_in, dts)


def turn_kernel(
    n, n_dp, level, ss_ref, gain_ref, gain_in_ref, wo_ref, win_ref, dts_ref, *refs,
):
    n_seq = 2 * n
    y_ref, mid_ref, scale_ref, wout_ref, next_ref, hid_ref, proj_ref = refs[3:10]
    gated_ref, w_ref, x_ref = refs[10:13]
    loads = Loads(refs[:3], refs[10:13], refs[13])
    loads.start()
    parts_ref, cut_sems, slots, share_s, share_r, own, so, *refs = refs[14:]
    cut = Cut(level, win_ref, dts_ref, parts_ref, cut_sems)
    cut.start()
    rows, span, width = x_ref.shape
    line, (wv, w_sem, buf, po, hid_sem, out_sem) = refs[:9], refs[9:15]
    get = Fetch(n_dp, n_seq, parts_ref, wv, refs[15:19])
    outs = spread_halves(n_dp, wout_ref, wo_ref, refs[19:21])
    gather = refs[21:]
    chip, core, sib, left, right = line_place(n_seq)
    meet(all_peers("seq", n_seq) + all_peers("dp", n_dp))
    copies = share_start("seq", n_seq, lambda to: ss_ref, slots, share_s, share_r)
    total = share_sum(copies, ss_ref[...], slots)
    cut.wait()
    get.start()
    loads.wait(0, 1, 2)
    scale = lax.rsqrt(total / DI + EPS)
    scale_ref[...] = scale
    cols = jnp.transpose(scale)
    for r in range(rows):
        for k in range(n):
            at = r * n + k
            g = gated_ref[r, k * CHUNK : (k + 1) * CHUNK]
            mid_ref[r, k * CHUNK : (k + 1) * CHUNK] = (g * cols[:, at : at + 1] * gain_ref[...]).astype(BF)

    def emit(j):
        here = pl.ds(pl.multiple_of(j * CHUNK, CHUNK), CHUNK)
        block = jnp.concatenate([mid_ref[r, here] for r in range(rows)], axis=0)
        for at in range(0, width, 512):
            halves(own, so, j, core, at, dot(block, w_ref[:, at : at + 512]), rows, span)

    per = -(-(n_seq - 1) // (n - 1))
    sums = LineSum(n, rows, emit, own, so, *line[:3], line[3:])
    sums.run(lambda tau: get.pull(1 + tau * per, 1 + tau * per + per), to_end=False)

    def ready(r):
        sums.finish(r)
        y = x_ref[r].astype(F32) + own[chip, r]
        y_ref[r] = y
        norm = lax.rsqrt(jnp.mean(y * y, axis=-1, keepdims=True) + EPS)
        buf[r, chip, pl.ds(pl.multiple_of(core * span, span), span)] = (y * norm * gain_in_ref[...]).astype(BF)
    keep = pltpu.make_async_copy(wv, next_ref, w_sem.at[0])

    def begun():
        get.tail()
        get.end()
        wout_ref[lax.axis_index("dp")] = wo_ref[...]
        for i in range(2):
            outs.hand(i)
        keep.start()

    def out_copies(j):
        return (
            pltpu.make_async_copy(buf.at[:, j], hid_ref.at[:, j], hid_sem.at[j]),
            pltpu.make_async_copy(po.at[j], proj_ref.at[:, pl.ds(j * CHUNK, CHUNK)], out_sem.at[j]),
        )

    def use(j):
        block = buf[:, j].reshape(rows * CHUNK, width)
        res = dot(block, wv[...].reshape(width, wv.shape[-1]))
        for r in range(rows):
            po[j, r] = res[r * CHUNK : (r + 1) * CHUNK]
        for copy in out_copies(j):
            copy.start()

    def done(j, _):
        for copy in out_copies(j):
            copy.wait()
        return 0

    def between(t):
        @pl.when(t == n - 2)
        def _():
            for i in range(2):
                outs.relay(i)

    line_gather(n, rows, span, buf, gather, use, begun, between, ready)
    sums.end()
    for i in range(2):
        outs.end(i)
    get.sent()
    share_end(copies)
    lax.fori_loop(0, n, done, 0)
    keep.wait()


def turn(gated, ss, gain, w, x, gain_in, wo, w_in, dts, level, groups, n_dp, n_seq):
    rows, span, width = x.shape
    n = n_seq // 2
    k = n * rows
    parts = parts_shape(w_in, n_seq)
    cols = parts.shape[2]
    w_shape = (n_dp, n_seq) + parts.shape[1:]
    return pl.pallas_call(
        functools.partial(turn_kernel, n, n_dp, level),
        in_specs=[VMEM_SPEC] * 4 + [ANY_SPEC] * 5,
        out_specs=[VMEM_SPEC] * 4 + [ANY_SPEC] * 3,
        out_shape=[
            jax.ShapeDtypeStruct(x.shape, F32),
            jax.ShapeDtypeStruct(gated.shape, BF),
            jax.ShapeDtypeStruct(ss.shape, F32),
            jax.ShapeDtypeStruct((n_dp,) + wo.shape, BF),
            jax.ShapeDtypeStruct(w_shape, BF),
            jax.ShapeDtypeStruct((rows, n, CHUNK, width), BF),
            jax.ShapeDtypeStruct((rows, n * CHUNK, cols), F32),
        ],
        scratch_shapes=Loads.scratch(gated, w, x)
        + [pltpu.VMEM(parts.shape, BF)]
        + dma(Cut.count(n_seq, groups))
        + [pltpu.VMEM((n_seq - 1,) + ss.shape, F32)]
        + dma(n_seq - 1, n_seq - 1)
        + LineSum.scratch(n, rows, span, width)
        + [pltpu.VMEM(w_shape, BF)]
        + dma(1)
        + [pltpu.VMEM((rows, n, CHUNK, width), BF), pltpu.VMEM((n, rows, CHUNK, cols), F32)]
        + dma(n, n)
        + Fetch.scratch(n_dp, n_seq)
        + Spread.scratch(n_dp, 2)
        + dma(k, k, k, k, k),
        compiler_params=comm_params(1),
        cost_estimate=pl.CostEstimate(flops=9 * 10**9, bytes_accessed=30 * 2**20, transcendentals=0),
    )(ss, gain, gain_in, wo, w_in, dts, gated, w, x)


def back_mix_kernel(n, n_dp, top, with_out, *refs):
    n_seq = 2 * n
    refs = list(refs)
    take = lambda k: [refs.pop(0) for _ in range(k)]
    proj_ref, prev_ref, marks_ref, cw_ref, hp_ref, ys_ref, sin_ref, gain_ref = take(8)
    if top:
        (ss_ref,) = take(1)
        sources = take(5)
    else:
        scale_ref, cols_ref, gains_ref = take(3)
        sources = take(5)
    dp_ref, gc_ref, gout_ref = take(3)
    if top:
        (y_ref,) = take(1)
    else:
        got_ref, cols_all, gains_all = take(3)
    places = take(len(sources))
    loads = Loads(sources, places, *take(1))
    gated_ref, w_ref, g_ref = places[:3]
    if top:
        x_ref, mine_ref = places[3:]
    else:
        mid_ref, term_ref = places[3:]
    mixer = take(4)
    dmid, acc, gwb, scale_scr, cube_scr, tot, slots = take(7)
    share_s, share_r = take(2)
    if with_out:
        outs = DpSum(n_dp, gwb, refs[0], gwb.shape[1] // 2, refs[1:3])
        take(3)
    rows, span, width = (x_ref if top else g_ref).shape
    inner = gated_ref.shape[2]
    chip, core, sib, left, right = line_place(n_seq)
    step = pl.program_id(1)
    k = pl.program_id(0) * n + step
    last = rows * n - 1
    ones = jnp.ones((8, inner), F32)
    if top:
        own, so = refs[:2]
        line = LineSum(n, rows, None, own, so, *refs[2:5], refs[5:11])
        mids, turn, buf = refs[11:14]
        line_sems = refs[14:19]
        span_rows = pl.ds(pl.multiple_of(core * span, span), span)
    else:
        buf, line_sems, got, cols_in, gains_in = refs[0], refs[1:6], refs[6], refs[7], refs[8]
        pieces = Pieces(n_dp, n_seq, term_ref, got, refs[9:15])
        smalls = [
            Small(n_dp, n_seq, cols_ref, cols_in, *refs[15:21]),
            Small(n_dp, n_seq, gains_ref, gains_in, *refs[21:27]),
        ]

    def through(j, block, mid):
        chunk = pl.ds(pl.multiple_of(j * CHUNK, CHUNK), CHUNK)
        res = dot(block, w_ref[...], NT)
        for at in range(0, width, 512):
            acc[:, at : at + 512] += dot(mid, block[:, at : at + 512], TN)
        for r in range(rows):
            part = res[r * CHUNK : (r + 1) * CHUNK]
            dmid[r, chunk] = part
            v = part * gain_ref[...] * gated_ref[r, chunk]
            tot[pl.ds(r * n + j, 1)] = by_head(ones, v)[:1]

    @pl.when(k == 0)
    def _():
        loads.start()
        if not top:
            acc[...] = jnp.zeros_like(acc)
        if top:
            meet(all_peers("seq", n_seq) + (all_peers("dp", n_dp) if with_out else []))
            first = share_start("seq", n_seq, lambda to: ss_ref, slots.at[0], share_s.at[0], share_r.at[0])
            scale = lax.rsqrt(share_sum(first, ss_ref[...], slots.at[0]) / DI + EPS)
            share_end(first)
            scale_scr[...] = scale
            cols = jnp.transpose(scale)
            loads.wait(0, 1)
            for r in range(rows):
                for j in range(n):
                    at = r * n + j
                    part = gated_ref[r, j * CHUNK : (j + 1) * CHUNK] * cols[:, at : at + 1] * gain_ref[...]
                    mids[at * CHUNK : (at + 1) * CHUNK] = part.astype(BF)
                    turn[:, at * CHUNK : (at + 1) * CHUNK] = jnp.transpose(part).astype(BF)

            def back(r, every, first):
                dmid[r] = dot(every, w_ref[...], NT)
                for j in range(n):
                    chunk = slice(j * CHUNK, (j + 1) * CHUNK)
                    v = dmid[r, chunk] * gain_ref[...] * gated_ref[r, chunk]
                    tot[r * n + j : r * n + j + 1] = by_head(ones, v)[:1]
                for at in range(0, width, 512):
                    value = dot(turn[:, r * n * CHUNK : (r + 1) * n * CHUNK], every[:, at : at + 512])
                    acc[:, at : at + 512] = value if first else acc[:, at : at + 512] + value

            def begun():
                for at in range(0, width, 512):
                    out = dot(mids[...], w_ref[:, at : at + 512])
                    for j in range(n):
                        for r in range(rows):
                            low = (r * n + j) * CHUNK
                            p, q = out[low : low + span], out[low + span : low + CHUNK]
                            own[j, r, :, at : at + 512] = jnp.where(core == 0, p, q)
                            so[j, r, :, at : at + 512] = jnp.where(core == 0, q, p).astype(BF)
                for j in range(n):
                    for r in range(rows):
                        line.to_sib(j, r).start()
                line.step(0)
                loads.wait(2)
                back(0, g_ref[...].reshape(n * CHUNK, width), True)

            def between(t):
                @pl.when(t == n - 2)
                def _():
                    line.step(1)

            loads.wait(4)
            for r in range(1, rows):
                buf[r - 1, chip, span_rows] = mine_ref[r]
            line_gather(n, rows - 1, span, buf, line_sems, lambda j: None, begun, between)
            for r in range(1, rows):
                back(r, buf[r - 1].reshape(n * CHUNK, width), False)
            second = share_start("seq", n_seq, lambda to: tot, slots.at[1], share_s.at[1], share_r.at[1])
        else:
            scale = scale_ref[...]
            scale_scr[...] = scale
            here = pl.ds(pl.multiple_of(core * span, span), span)
            loads.wait(2)
            for r in range(rows):
                buf[r, chip, here] = g_ref[r].astype(BF)
            meet(all_peers("seq", n_seq) + all_peers("dp", n_dp))
            loads.wait(4)

            for small in smalls:
                small.start()
            pieces.tiles_do(0, pieces.tiles, pieces.send)

            def use(j):
                chunk = pl.ds(pl.multiple_of(j * CHUNK, CHUNK), CHUNK)
                mid = jnp.concatenate([mid_ref[r, chunk] for r in range(rows)], axis=0)
                through(j, buf[:, j].reshape(rows * CHUNK, width), mid)

            def between(t):
                at = jnp.maximum(2 * (t - 2), 0)
                pieces.tiles_do(at, jnp.where(t < 2, at, at + 2), pieces.middle)

            line_gather(n, rows, span, buf, line_sems, use, lambda: loads.wait(0, 1, 3), between)
            second = share_start("seq", n_seq, lambda to: tot, slots.at[1], share_s.at[1], share_r.at[1])
        for d in range(n_dp):
            size = inner // n_dp
            gwb[d] = acc[d * size : (d + 1) * size].astype(BF)
        if with_out:
            for i in range(2):
                outs.send(i)
        else:
            gout_ref[...] = gwb[...]
        cube_scr[...] = scale * scale * scale * (share_sum(second, tot[...], slots.at[1]) / DI)
        share_end(second)

    at = pl.multiple_of((n - 1 - step) * CHUNK, CHUNK)
    mix_bwd_step(
        inner, n, proj_ref, prev_ref, marks_ref, cw_ref, hp_ref, ys_ref, sin_ref,
        dmid[pl.program_id(0), pl.ds(at, CHUNK)], scale_scr, cube_scr, gain_ref, dp_ref, gc_ref, *mixer,
    )

    if top:

        @pl.when((k % 2 == 1) & (k < last - 1))
        def _():
            line.step((k + 3) // 2)
    else:

        @pl.when(k == 0)
        def _():
            for small in smalls:
                small.middle()

        @pl.when(2 * k < pieces.tiles)
        def _():
            pieces.tiles_do(2 * k, 2 * k + 2, pieces.last)

    if with_out:

        @pl.when(k == last // 2)
        def _():
            for i in range(2):
                outs.middle(i)

    @pl.when(k == last)
    def _():
        if with_out:
            for i in range(2):
                gout_ref[outs.rows_of(i)] = outs.total(i)
                outs.end(i)
        if top:
            loads.wait(3)
            for r in range(rows):
                line.finish(r)
                y_ref[r] = (x_ref[r] + own[chip, r]).astype(BF)
            line.end()
        else:
            for small in smalls:
                small.end()
            pieces.end()

            got_ref[...] = got[...]
            cols_all[...] = cols_in[...]
            gains_all[...] = gains_in[...]


def back_mix(proj, marks, cws, hps, level, ys, sin, gain, gated, w, g, more, n_dp, n_seq, with_out):
    small, big = more
    top = len(small) == 1
    rows, length, cols = proj.shape
    span, width = g.shape[-2:]
    n = n_seq // 2
    inner = gated.shape[2]
    k = rows * n
    bc = CONV_CH - DI
    at = lambda r, c: (r, n - 1 - c, 0)

    def whole(x):
        zeros = (0,) * len(x.shape)
        return pl.BlockSpec(x.shape, lambda r, c: zeros, pipeline_mode=pl.Buffered(1))

    if with_out:
        gout = jax.ShapeDtypeStruct((inner // n_dp, width), F32)
    else:
        gout = jax.ShapeDtypeStruct((n_dp, inner // n_dp, width), BF)
    outs = [
        jax.ShapeDtypeStruct((rows, length, cols), BF),
        jax.ShapeDtypeStruct((8, inner + bc), F32),
        gout,
    ]
    big = (gated, w, g) + tuple(big)
    scratch = Loads.scratch(*big) + [
        pltpu.VMEM((STATE, inner), F32),
        pltpu.VMEM((8, LANES), F32),
        pltpu.VMEM((TAPS - 1, 8, inner + bc), F32),
        pltpu.VMEM((2, 8, CHUNK), F32),
        pltpu.VMEM((rows, length, inner), F32),
        pltpu.VMEM((inner, width), F32),
        pltpu.VMEM((n_dp, inner // n_dp, width), BF),
        pltpu.VMEM((k, CHUNK), F32),
        pltpu.VMEM((k, CHUNK), F32),
        pltpu.VMEM((k, CHUNK), F32),
        pltpu.VMEM((2, n_seq - 1, k, CHUNK), F32),
        pltpu.SemaphoreType.DMA((2, n_seq - 1)),
        pltpu.SemaphoreType.DMA((2, n_seq - 1)),
    ]
    if with_out:
        scratch += DpSum.scratch(n_dp, inner // n_dp, width, inner // n_dp // 2)
    if top:
        outs.append(jax.ShapeDtypeStruct((rows, span, width), BF))
        scratch += LineSum.scratch(n, rows, span, width)
        scratch += [pltpu.VMEM((length * rows, inner), BF), pltpu.VMEM((inner, length * rows), BF)]
        scratch += [pltpu.VMEM((rows - 1, n, CHUNK, width), BF)] + dma(*[k - n] * 5)
    else:
        (_, *vecs), (_, term) = more
        outs.append(jax.ShapeDtypeStruct((n_seq, width // (n_dp * n_seq), term.shape[2]), BF))
        outs += [jax.ShapeDtypeStruct((n_seq,) + vec.shape, F32) for vec in vecs]
        scratch += [pltpu.VMEM((rows, n, CHUNK, width), BF)] + dma(k, k, k, k, k)
        scratch += [pltpu.VMEM(out.shape, out.dtype) for out in outs[-3:]]
        scratch += Pieces.scratch(n_dp, n_seq, term.shape[1], term.shape[2])
        for vec in vecs:
            scratch += Small.scratch(n_dp, n_seq, vec)
    def of_level(x):
        zeros = (0,) * (len(x.shape) - 1)
        return pl.BlockSpec((1,) + x.shape[1:], lambda r, c: (level,) + zeros)

    rest = (gain,) + tuple(small)
    return pl.pallas_call(
        functools.partial(back_mix_kernel, n, n_dp, top, with_out),
        grid=(rows, n),
        in_specs=[
            pl.BlockSpec((1, CHUNK, cols), at),
            pl.BlockSpec((1, 8, cols), lambda r, c: (r, jnp.maximum((n - 1 - c) * (CHUNK // 8) - 1, 0), 0)),
        ]
        + [whole(marks), of_level(cws), of_level(hps)]
        + [
            pl.BlockSpec((1, CHUNK, inner), at),
            pl.BlockSpec((1, 1, STATE, inner), lambda r, c: (r, n - 1 - c, 0, 0)),
        ]
        + [whole(x) for x in rest]
        + [ANY_SPEC] * len(big),
        out_specs=[pl.BlockSpec((1, CHUNK, cols), at)] + [whole(x) for x in outs[1:]],
        out_shape=outs,
        scratch_shapes=scratch,
        compiler_params=pltpu.CompilerParams(
            dimension_semantics=("arbitrary", "arbitrary"),
            collective_id=2 if top else 4,
            has_side_effects=True,
            vmem_limit_bytes=60 * 2**20,
        ),
        cost_estimate=pl.CostEstimate(flops=14 * 10**9, bytes_accessed=40 * 2**20, transcendentals=2 * 10**6),
    )(proj, proj, marks, cws, hps, ys, sin, *rest, *big)


def back_project_kernel(n, n_dp, final, gain_ref, *refs):
    n_seq = 2 * n
    refs = list(refs)
    take = lambda k: [refs.pop(0) for _ in range(k)]
    if final:
        (cols_ref,) = take(1)
    sources = take(5)
    if final:
        out_ref, got_ref, cols_all, gains_all = take(4)
    else:
        out_ref, gains_ref, term_ref = take(3)
    dp_ref, w_ref, x_ref, g_ref, hid = places = take(5)
    loads = Loads(sources, places, *take(1))
    loads.start()
    own, so = take(2)
    line = take(9)
    rows, span, width = x_ref.shape
    part = dp_ref.shape[2]
    group = width // n_dp
    tiles = group // LANES
    chip, core, sib, left, right = line_place(n_seq)
    (term,) = take(1)
    if not final:
        (term_sem,) = take(1)
    if final:
        pieces = Pieces(n_dp, n_seq, term, got_ref, take(6))
        (gains_ref,) = take(1)
        small = Small(n_dp, n_seq, cols_ref, cols_all, *take(6))
        gain_sum = Small(n_dp, n_seq, gains_ref, gains_all, *take(6))
        meet(all_peers("seq", n_seq) + all_peers("dp", n_dp))
        small.start()
    else:
        meet(line_peers(n))
    loads.wait(0, 1)

    def term_copy(i):
        here = pl.ds(pl.multiple_of(i * LANES, LANES), LANES)
        return pltpu.make_async_copy(term.at[:, here], term_ref.at[:, here], term_sem.at[i])

    def emit(j):
        here = pl.ds(pl.multiple_of(j * CHUNK, CHUNK), CHUNK)
        block = jnp.concatenate([dp_ref[r, here] for r in range(rows)], axis=0)
        for at in range(0, width, 512):
            halves(own, so, j, core, at, dot(block, w_ref[at : at + 512], NT), rows, span)

    def product(i):
        right_side = dp_ref[...].reshape(rows * n * CHUNK, part)
        tile = (chip + 1 + i) % tiles if 2 * tiles == n_seq else i

        def one(owner, _):
            col = pl.ds(pl.multiple_of(owner * group + tile * LANES, LANES), LANES)
            h = hid[:, :, :, col].reshape(rows * n * CHUNK, LANES)
            term[owner, pl.ds(pl.multiple_of(i * LANES, LANES), LANES)] = dot(h, right_side, TN).astype(BF)
            return 0

        lax.fori_loop(0, n_dp, one, 0)

    def products(first, last):
        def one(i, _):
            @pl.when(i < tiles)
            def _():
                product(i)
                if final:
                    pieces.send(i)
                else:
                    term_copy(i).start()

            return 0

        lax.fori_loop(first, last, one, 0)

    def between(tau):
        @pl.when(tau == 0)
        def _():
            loads.wait(4)

        if final:
            pieces.tiles_do(tau - 1, tau, pieces.middle)
            pieces.tiles_do(tau - 2, tau - 1, pieces.last)
        products(jnp.where(tau == 0, 0, tau + 1), tau + 2)
        if final:

            @pl.when(tau == 1)
            def _():
                small.middle()

    def before_end():
        products(n, tiles)
        if final:
            pieces.tiles_do(n - 2, tiles, pieces.middle)
            pieces.tiles_do(n - 3, n - 2, pieces.last)

    LineSum(n, rows, emit, own, so, *line[:3], line[3:]).run(between, before_end)
    if final:
        pieces.tiles_do(n - 2, tiles, pieces.last)
    loads.wait(2, 3)
    d_gain = jnp.zeros((1, width), F32)
    for r in range(rows):
        d_hid = own[chip, r]
        x = x_ref[r].astype(F32)
        scale = lax.rsqrt(jnp.mean(x * x, axis=-1, keepdims=True) + EPS)
        m = d_hid * gain_ref[...]
        mean = jnp.mean(m * x, axis=-1, keepdims=True)
        out_ref[r] = g_ref[r].astype(F32) + scale * m - x * (scale * scale * scale * mean)
        d_gain = d_gain + jnp.sum(d_hid * x * scale, axis=0, keepdims=True)
    for t in range(width // LANES):
        gains_ref[t : t + 1] = d_gain[:, t * LANES : (t + 1) * LANES]
    if final:
        gain_sum.start()
        gain_sum.middle()
        small.end()
        gain_sum.end()
        pieces.end()
    else:
        for i in range(tiles):
            term_copy(i).wait()


def back_project(dp, w, x, g, gain, hidden, cols, n_dp, n_seq):
    rows, span, width = x.shape
    n = n_seq // 2
    part = dp.shape[2]
    group = width // n_dp
    final = cols is not None
    gains = jax.ShapeDtypeStruct((width // LANES, LANES), F32)
    outs = [jax.ShapeDtypeStruct(x.shape, F32)]
    scratch = Loads.scratch(dp, w, x, g, hidden) + LineSum.scratch(n, rows, span, width)
    scratch += [pltpu.VMEM((n_dp, group, part), BF)]
    out_specs = [VMEM_SPEC] * (4 if final else 2) + [ANY_SPEC] * (not final)
    if final:
        outs += [jax.ShapeDtypeStruct((n_seq, group // n_seq, part), BF)]
        outs += [jax.ShapeDtypeStruct((n_seq,) + x.shape, F32) for x in (cols, gains)]
        scratch += Pieces.scratch(n_dp, n_seq, group, part)
        scratch += [pltpu.VMEM(gains.shape, F32)]
        scratch += Small.scratch(n_dp, n_seq, cols) + Small.scratch(n_dp, n_seq, gains)
    else:
        outs += [gains, jax.ShapeDtypeStruct((n_dp, group, part), BF)]
        scratch += dma(group // LANES)
    return pl.pallas_call(
        functools.partial(back_project_kernel, n, n_dp, final),
        in_specs=[VMEM_SPEC] * (1 + final) + [ANY_SPEC] * 5,
        out_specs=out_specs,
        out_shape=outs,
        scratch_shapes=scratch,
        compiler_params=comm_params(5 if final else 3),
        cost_estimate=pl.CostEstimate(flops=11 * 10**9, bytes_accessed=24 * 2**20, transcendentals=0),
    )(gain, *([cols] if final else []), dp, w, x, g, hidden)


class Small:
    def __init__(self, n_dp, n_seq, vec, vall, vsum, vslots, v_s, v_r, a_s, a_r):
        self.n_dp, self.n_seq, self.vec, self.vall = n_dp, n_seq, vec, vall
        self.vsum, self.vslots, self.v_s, self.v_r, self.a_s, self.a_r = vsum, vslots, v_s, v_r, a_s, a_r

    @staticmethod
    def scratch(n_dp, n_seq, vec):
        return [pltpu.VMEM(vec.shape, F32), pltpu.VMEM((n_dp - 1,) + vec.shape, F32)] + dma(
            n_dp - 1, n_dp - 1, n_seq, n_seq
        )

    def over_dp(self, k):
        to = (lax.axis_index("dp") + k) % self.n_dp
        return remote(self.vec, self.vslots.at[k - 1], self.v_s.at[k - 1], self.v_r.at[k - 1], {"dp": to})

    def give(self, k):
        me = lax.axis_index("seq")
        to = (me + k) % self.n_seq
        return remote(self.vsum, self.vall.at[me], self.a_s.at[to], self.a_r.at[me], {"seq": to})

    def take(self, k):
        me = lax.axis_index("seq")
        source = (me + k) % self.n_seq
        return remote(self.vsum, self.vall.at[source], self.a_s.at[me], self.a_r.at[source], {"seq": source})

    def start(self):
        for k in range(1, self.n_dp):
            self.over_dp(k).start()

    def middle(self):
        total = self.vec[...]
        for k in range(1, self.n_dp):
            self.over_dp(k).wait_recv()
            total = total + self.vslots[k - 1]
        self.vsum[...] = total
        for k in range(1, self.n_seq):
            self.give(k).start()
        self.vall[lax.axis_index("seq")] = total

    def end(self):
        for k in range(1, self.n_seq):
            self.take(k).wait_recv()
        for k in range(1, self.n_seq):
            self.give(k).wait_send()
        for k in range(1, self.n_dp):
            self.over_dp(k).wait_send()


def arrange_kernel(
    groups, own_heads, got0, got1, vec0, vec1, gains0, gains1,
    *refs,
):
    gout0, gout1, gin_ref, gout_ref, gain_ref, mid_ref, cw_ref, cb_ref, dtb_ref, al_ref, ds_ref, sem = refs
    copies = [pltpu.make_async_copy(g, gout_ref.at[i], sem.at[i]) for i, g in enumerate((gout0, gout1))]
    for copy in copies:
        copy.start()
    n_seq = got0.shape[0]
    inner = DI // n_seq
    bc = CONV_CH - DI
    cols = inner // groups
    per = own_heads // groups
    for level, got in enumerate((got0, got1)):
        dts = jnp.zeros((got.shape[1], HEADS), F32)
        shared = jnp.zeros((got.shape[1], bc), F32)
        for s in range(n_seq):
            dts = dts + dot(got[s, :, :LANES].astype(F32), head_place(LANES, s, n_seq, own_heads, per), precision=HIGH)
            shared = shared + got[s, :, LANES + 2 * inner :].astype(F32)
            for g in range(groups):
                at = (g * n_seq + s) * cols
                for kind in range(2):
                    src = LANES + kind * inner + g * cols
                    gin_ref[level, :, kind * DI + at : kind * DI + at + cols] = got[s, :, src : src + cols].astype(F32)
        gin_ref[level, :, 2 * DI : 2 * DI + bc] = shared
        gin_ref[level, :, 2 * DI + bc :] = dts
    wide = (inner + bc) // LANES
    for level, (vec, gains_all) in enumerate(((vec0, gains0), (vec1, gains1))):
        total = jnp.zeros((8, bc), F32)
        heads = [jnp.zeros((1, HEADS), F32)] * 3
        for s in range(n_seq):
            tiles = [vec[s, :, t * LANES : (t + 1) * LANES] for t in range(wide)]
            for g in range(groups):
                for t in range(cols // LANES):
                    tile = tiles[g * cols // LANES + t]
                    at = (g * n_seq + s) * cols + t * LANES
                    cw_ref[level, :, at : at + LANES] = tile[:TAPS]
                    cb_ref[level : level + 1, at : at + LANES] = tile[4:5]
                    mid_ref[level : level + 1, at : at + LANES] = tile[6:7]
            total = total + jnp.concatenate(tiles[inner // LANES :], axis=1)
            skip = jnp.concatenate(tiles[: inner // LANES], axis=1)
            skip = dot(skip, head_matrix(inner), NT, HIGH)
            heads[2] = heads[2] + dot(skip, head_place(8, s, n_seq, own_heads, per), precision=HIGH)[5:6]
            place = head_place(LANES, s, n_seq, own_heads, per)
            for kind in range(2):
                heads[kind] = heads[kind] + dot(tiles[kind], place, precision=HIGH)[7:8]
        cw_ref[level, :, DI:] = total[:TAPS]
        cb_ref[level : level + 1, DI:] = total[4:5]
        for ref, value in zip((dtb_ref, al_ref, ds_ref), heads):
            ref[level : level + 1] = value
        gains = gains_all[0]
        for s in range(1, n_seq):
            gains = gains + gains_all[s]
        for t in range(gains.shape[0]):
            gain_ref[level : level + 1, t * LANES : (t + 1) * LANES] = gains[t : t + 1]
    for copy in copies:
        copy.wait()


def head_place(size, s, n_seq, own_heads, per):
    i = lax.broadcasted_iota(jnp.int32, (size, HEADS), 0)
    h = lax.broadcasted_iota(jnp.int32, (size, HEADS), 1)
    return ((i < own_heads) & (h == (i // per * n_seq + s) * per + i % per)).astype(F32)


def arrange(gots, vecs, gains, gouts, groups, own_heads, width):
    piece = gots[0].shape[1]
    shapes = [
        (2, piece, 2 * DI + CONV_CH - DI + HEADS),
        (2,) + gouts[0].shape,
        (2, width),
        (2, DI),
        (2, TAPS, CONV_CH),
        (2, CONV_CH),
        (2, HEADS),
        (2, HEADS),
        (2, HEADS),
    ]
    return pl.pallas_call(
        functools.partial(arrange_kernel, groups, own_heads),
        in_specs=[VMEM_SPEC] * 6 + [ANY_SPEC] * 2,
        out_specs=[VMEM_SPEC, ANY_SPEC] + [VMEM_SPEC] * 7,
        out_shape=[jax.ShapeDtypeStruct(shape, F32) for shape in shapes],
        scratch_shapes=dma(2),
        compiler_params=pltpu.CompilerParams(vmem_limit_bytes=60 * 2**20),
    )(*gots, *vecs, *gains, *gouts)


def split_cols(x, groups, size):
    cols = x.shape[-1] // (groups * size)
    x = x.reshape(x.shape[:-1] + (groups, size, cols))
    x = jnp.moveaxis(x, -2, 0)
    return x.reshape(x.shape[:-2] + (groups * cols,))


def shards(
    tokens, resets, cotangent, w_in, w_out, gain_in, gain_mid, conv_w, conv_b, dt_bias, a_log, d_skip
):
    rows, span, width = tokens.shape
    layers = w_in.shape[0]
    n_dp, n_seq = lax.axis_size("dp"), lax.axis_size("seq")
    place = lax.axis_index("seq")
    length = span * n_seq
    own_heads = HEADS // n_seq
    groups = n_dp if own_heads % n_dp == 0 else 1
    inner = DI // n_seq
    bc_all = CONV_CH - DI

    dts = split_cols(w_in[..., DI + CONV_CH :], groups, n_seq)
    dts = jnp.pad(dts, ((0, 0),) * 3 + ((0, LANES - own_heads),))
    cols = LANES + 2 * inner + bc_all

    marks = jnp.pad(resets.astype(F32), ((0, 8 - rows), (0, CHUNK - span)))
    marks = jnp.where(place % 2 == 0, marks, jnp.roll(marks, span, axis=1))

    def columns(x, by_head):
        x = split_cols(x, groups, n_seq)
        x = lax.dynamic_index_in_dim(x, place, 0, False)
        return jnp.repeat(x, HEAD, axis=-1) if by_head else x

    taps = jnp.concatenate([conv_w, conv_b[:, None]], axis=1)
    rest = jnp.concatenate([d_skip[:, None], jnp.zeros((layers, 2, HEADS), F32)], axis=1)
    cws = jnp.concatenate([columns(taps[..., :DI], False), columns(rest, True)], axis=1)
    cws = jnp.concatenate([cws, jnp.pad(taps[..., DI:], ((0, 0), (0, 7 - TAPS), (0, 0)))], axis=2)
    hps = columns(jnp.stack([dt_bias, a_log], axis=1), False)
    hps = jnp.broadcast_to(jnp.pad(hps, ((0, 0), (0, 0), (0, 8 - own_heads)))[..., None], (layers, 2, 8, LANES))
    gains = columns(gain_mid[:, None], False)

    def whole_rows(w):
        return lax.dynamic_slice_in_dim(lax.all_gather(w, BOTH, axis=0, tiled=True), place * inner, inner, 0)

    resid = tokens
    stored = []
    for level in range(layers):
        gain = gains[level]
        before = resid
        if level == 0:
            hidden, proj, w_all, wo_all, marks_all = project(
                before, gain_in[level][None], w_out[level], marks, w_in, dts[:, level], level, groups, n_dp, n_seq
            )
            win = [w_all.reshape(width, cols)]
            wout = [wo_all.reshape(DI // n_seq, width) if groups == n_dp else whole_rows(w_out[level])]
            proj, own_cot = lax.optimization_barrier((proj, cotangent[0]))
            cot = lax.all_gather(own_cot, "seq")
        gated, squares, ys, sin = mix_fwd(proj, marks_all, cws, hps, level, inner)
        if level < layers - 1:
            resid, mid, scale, wo_all, w_all, next_hidden, next_proj = turn(
                gated, squares, gain, wout[level], before, gain_in[level + 1][None],
                w_out[level + 1], w_in, dts[:, level + 1], level + 1, groups, n_dp, n_seq,
            )
            wout.append(wo_all.reshape(inner, width) if groups == n_dp else whole_rows(w_out[level + 1]))
            win.append(w_all.reshape(width, cols))
            stored.append((before, hidden, proj, gain, gated, ys, sin, mid, scale))
            hidden, proj = next_hidden, next_proj
    grad = cotangent
    gots = [None] * layers
    grads_out = [None] * layers
    vecs = [None] * layers
    gain_sums = [None] * layers
    with_out = groups == n_dp
    for level in reversed(range(layers)):
        if level == layers - 1:
            given, more = cot, ((squares,), (before, cotangent))
        else:
            before, hidden, proj, gain, gated, ys, sin, mid, scale = stored[level]
            given, more = grad, ((scale, gc, gain_rows), (mid, term))
        d_proj, gc, out_term, *rest = back_mix(
            proj, marks_all, cws, hps, level, ys, sin, gain, gated, wout[level], given, more, n_dp, n_seq, with_out
        )
        if level == layers - 1:
            (outputs,) = rest
        else:
            gots[level + 1], vecs[level + 1], gain_sums[level + 1] = rest
        if with_out:
            grads_out[level] = out_term
        else:
            padded = jnp.zeros((DI, width), BF)
            padded = lax.dynamic_update_slice_in_dim(padded, out_term.reshape(inner, width), place * inner, 0)
            grads_out[level] = lax.psum_scatter(padded, BOTH, scatter_dimension=0, tiled=True).astype(F32)
        grad, *rest = back_project(
            d_proj, win[level], before, grad, gain_in[level][None], hidden, gc if level == 0 else None, n_dp, n_seq
        )
        if level == 0:
            gots[0], vecs[0], gain_sums[0] = rest
        else:
            gain_rows, term = rest
    grads = arrange(gots, vecs, gain_sums, grads_out, groups, own_heads, width)
    return (outputs, grad, *grads)


def solution(mesh):
    placed = (
        P("dp", "seq", None),
        P("dp", "seq"),
        P("dp", "seq", None),
        P(None, BOTH, None),
        P(None, BOTH, None),
    ) + (P(),) * 7
    return jax.shard_map(
        shards,
        mesh=mesh,
        in_specs=placed,
        out_specs=(
            P("dp", "seq", None),
            P("dp", "seq", None),
            P(None, BOTH, None),
            P(None, BOTH, None),
        )
        + (P(),) * 7,
        check_vma=False,
    )
```

```python
import functools

import jax
import jax.numpy as jnp
from jax import lax
from jax.experimental import pallas as pl
from jax.experimental.pallas import tpu as pltpu
from jax.sharding import PartitionSpec as P

HEADS = 64
HEAD = 64
STATE = 128
DI = 4096
CONV_CH = 4352
CHUNK = 128
LANES = 128
TAPS = 4
EPS = 1e-05
HIGH = lax.Precision.HIGHEST
BF = jnp.bfloat16
F32 = jnp.float32
FAR = -1e30
BOTH = ("dp", "seq")


def dot(a, b, dims=((1,), (0,)), precision=None):
    return lax.dot_general(a, b, (dims, ((), ())), preferred_element_type=F32, precision=precision)


NT = ((1,), (1,))
TN = ((0,), (0,))


def head_matrix(inner):
    row = lax.broadcasted_iota(jnp.int32, (8, inner), 0)
    col = lax.broadcasted_iota(jnp.int32, (8, inner), 1)
    return (col // HEAD == row).astype(F32)


def parts_of(x, count):
    parts = []
    for _ in range(count - 1):
        part = x.astype(BF).astype(F32)
        parts.append(part)
        x = x - part
    parts.append(x)
    return jnp.concatenate(parts, axis=0)


def spread(rows, inner):
    heads = head_matrix(inner)
    return dot(parts_of(rows, 2).astype(BF), jnp.concatenate([heads, heads], axis=0).astype(BF), TN)


def by_head(heads, x):
    heads = heads.astype(BF)
    high = x.astype(BF)
    return dot(heads, high, NT) + dot(heads, (x - high.astype(F32)).astype(BF), NT)


def along(rows, ones):
    res = dot(parts_of(rows, 3).astype(BF), ones.astype(BF))
    return res[:8] + res[8:16] + res[16:]


def gaps_of(cum, heads):
    parts = parts_of(cum, 3)
    row = lax.broadcasted_iota(jnp.int32, (24, heads * CHUNK), 0)
    col = lax.broadcasted_iota(jnp.int32, (24, heads * CHUNK), 1)
    mine = (row % 8 == col // CHUNK).astype(F32)
    right = jnp.concatenate([mine, -mine * jnp.concatenate([parts] * heads, axis=1)], axis=0)
    left = jnp.concatenate([parts, jnp.ones_like(parts)], axis=0)
    return dot(left.astype(BF), right.astype(BF), TN)


def stacked_halves(x):
    lane = lax.broadcasted_iota(jnp.int32, x.shape, 1)
    zero = jnp.zeros_like(x)
    return jnp.concatenate([jnp.where(lane < HEAD, x, zero), jnp.where(lane < HEAD, zero, x)], axis=0)


def chunk_masks(marks_ref, at, first):
    here = marks_ref[pl.ds(at, 1)]
    past = marks_ref[pl.ds(jnp.maximum(at - 1, 0), 1)]
    same = 1.0 - jnp.concatenate([jnp.where(first, 1.0, past), here], axis=1)
    same = jnp.broadcast_to(same, (8, 2 * CHUNK))
    rows = [same]
    for back in range(1, TAPS - 1):
        rows.append(rows[-1] * pltpu.roll(same, back, 1))
    rows = [row[:1, CHUNK:] for row in rows]
    row = lax.broadcasted_iota(jnp.int32, (CHUNK, CHUNK), 0)
    col = lax.broadcasted_iota(jnp.int32, (CHUNK, CHUNK), 1)
    counts = dot(jnp.broadcast_to(here, (8, CHUNK)), (row <= col).astype(F32))[:1]
    return jnp.concatenate(rows + [counts] + [jnp.zeros_like(counts)] * (8 - TAPS), axis=0), counts


def chunk_rows(dt_block, hp, cr):
    raw = jnp.transpose(dt_block)[:8] + hp[0]
    dt = jnp.maximum(raw, 0.0) + jnp.log1p(jnp.exp(-jnp.abs(raw)))
    rate = jnp.exp(hp[1])
    row = lax.broadcasted_iota(jnp.int32, (CHUNK, CHUNK), 0)
    col = lax.broadcasted_iota(jnp.int32, (CHUNK, CHUNK), 1)
    cum = along(-dt * rate, (row <= col).astype(F32))
    end = cum[:, CHUNK - 1 :]
    last = cr[:, CHUNK - 1 :]
    reach = jnp.where(cr == 0.0, jnp.exp(cum), 0.0)
    to_end = jnp.where(cr == last, jnp.exp(end - cum), 0.0)
    passing = jnp.where(last == 0.0, jnp.exp(end), 0.0)
    return raw, dt, rate, cum, reach, to_end, passing


def conv_in(ext, xbc, mk, cw):
    total = cw[4:5] + cw[TAPS - 1 : TAPS] * xbc
    moved = []
    for back in range(1, TAPS):
        m = pltpu.roll(ext, back, 0)[8:] * mk[:, back - 1 : back]
        moved.append(m)
        total = total + cw[TAPS - 1 - back : TAPS - back] * m
    return total, moved


def decay_of(gaps, mask, head):
    return jnp.exp(gaps[:, head * CHUNK : (head + 1) * CHUNK] + mask)


def halved(x):
    high = x.astype(BF)
    return high, (x - high.astype(F32)).astype(BF)


def dot_parts(a, b, dims=((1,), (0,))):
    return dot(a[0], b[0], dims) + (dot(a[0], b[1], dims) + dot(a[1], b[0], dims))


def scores_of(act, inner):
    return dot_parts(halved(act[:, inner + STATE :]), halved(act[:, inner : inner + STATE]), NT)


def chunk_mask(mk, cr):
    row = lax.broadcasted_iota(jnp.int32, (CHUNK, CHUNK), 0)
    col = lax.broadcasted_iota(jnp.int32, (CHUNK, CHUNK), 1)
    return jnp.where((row >= col) & (mk[:, 3:4] == cr), 0.0, FAR)


def mix_fwd_kernel(inner, proj_ref, marks_ref, cw_ref, hp_ref, gated_ref, ss_ref, ys_ref, sin_ref, s_scr, tail_scr):
    bc = CONV_CH - DI

    @pl.when(pl.program_id(1) == 0)
    def _():
        s_scr[...] = jnp.zeros_like(s_scr)
        tail_scr[...] = jnp.zeros_like(tail_scr)

    at = pl.program_id(0) * pl.num_programs(1) + pl.program_id(1)
    masks, cr = chunk_masks(marks_ref, at, pl.program_id(1) == 0)
    mk = jnp.transpose(masks)
    cw = cw_ref[0]
    xbc = proj_ref[0, :, LANES + inner :]
    ext = jnp.concatenate([tail_scr[...], xbc], axis=0)
    tail_scr[...] = xbc[CHUNK - 8 :]
    conv, _ = conv_in(ext, xbc, mk, cw)
    act = conv * jax.nn.sigmoid(conv)
    xs = act[:, :inner]
    bmat = halved(act[:, inner : inner + STATE])
    cmat = halved(act[:, inner + STATE :])
    raw, dt, rate, cum, reach, to_end, passing = chunk_rows(proj_ref[0, :, :LANES], hp_ref[0], cr)
    gaps = gaps_of(cum, inner // HEAD)
    mask = chunk_mask(mk, cr)
    xd = xs * spread(dt, inner)
    xdb = halved(xd)
    state = s_scr[...]
    sin_ref[0, 0] = state
    scores = dot_parts(cmat, bmat, NT)
    y = spread(reach, inner) * dot_parts(cmat, halved(state))
    inner_parts = []
    for j in range(inner // LANES):
        w = [scores * decay_of(gaps, mask, 2 * j + i) for i in range(2)]
        x = [stacked_halves(part[:, j * LANES : (j + 1) * LANES]) for part in xdb]
        inner_parts.append(dot_parts(halved(jnp.concatenate(w, axis=1)), x))
    y = y + jnp.concatenate(inner_parts, axis=1)
    ys_ref[0] = y
    keep = jnp.sum(passing * head_matrix(inner), axis=0, keepdims=True)
    s_scr[...] = keep * state + dot_parts(bmat, halved(xd * spread(to_end, inner)), TN)
    z = proj_ref[0, :, LANES : LANES + inner]
    gated = (y + cw[5:6, :inner] * xs) * (z * jax.nn.sigmoid(z))
    gated_ref[0] = gated
    ss_ref[pl.ds(at, 1)] = by_head(jnp.ones((8, inner), F32), gated * gated)[:1]


def mix_fwd(proj, marks, cws, hps, level, inner):
    rows, length, cols = proj.shape
    chunks = length // CHUNK
    bc = CONV_CH - DI
    whole = lambda r, c: (0, 0)
    return pl.pallas_call(
        functools.partial(mix_fwd_kernel, inner),
        grid=(rows, chunks),
        in_specs=[
            pl.BlockSpec((1, CHUNK, cols), lambda r, c: (r, c, 0)),
            pl.BlockSpec(marks.shape, whole),
            pl.BlockSpec((1,) + cws.shape[1:], lambda r, c: (level, 0, 0)),
            pl.BlockSpec((1,) + hps.shape[1:], lambda r, c: (level, 0, 0, 0)),
        ],
        out_specs=[
            pl.BlockSpec((1, CHUNK, inner), lambda r, c: (r, c, 0)),
            pl.BlockSpec((rows * chunks, CHUNK), whole),
            pl.BlockSpec((1, CHUNK, inner), lambda r, c: (r, c, 0)),
            pl.BlockSpec((1, 1, STATE, inner), lambda r, c: (r, c, 0, 0)),
        ],
        out_shape=[
            jax.ShapeDtypeStruct((rows, length, inner), F32),
            jax.ShapeDtypeStruct((rows * chunks, CHUNK), F32),
            jax.ShapeDtypeStruct((rows, length, inner), F32),
            jax.ShapeDtypeStruct((rows, chunks, STATE, inner), F32),
        ],
        scratch_shapes=[pltpu.VMEM((STATE, inner), F32), pltpu.VMEM((8, inner + bc), F32)],
        compiler_params=pltpu.CompilerParams(
            dimension_semantics=("arbitrary", "arbitrary"), vmem_limit_bytes=60 * 2**20
        ),
        cost_estimate=pl.CostEstimate(flops=3 * 10**9, bytes_accessed=18 * 2**20, transcendentals=10**6),
    )(proj, marks, cws, hps)


def silu_slope(v, s):
    return s * (1.0 + v * (1.0 - s))


def mix_bwd_step(
    inner, chunks, proj_ref, prev_ref, marks_ref, cw_ref, hp_ref, ys_ref, sin_ref, d_mid, scale_ref, cube_ref, gain_ref,
    dp_ref, gc_ref, ds_scr, gam_scr, head_scr, gh_ref,
):
    step = pl.program_id(1)

    @pl.when((step == 0) & (pl.program_id(0) == 0))
    def _():
        gc_ref[...] = jnp.zeros_like(gc_ref)
        gh_ref[...] = jnp.zeros_like(gh_ref)

    @pl.when(step == 0)
    def _():
        ds_scr[...] = jnp.zeros_like(ds_scr)
        gam_scr[...] = jnp.zeros_like(gam_scr)
        head_scr[...] = jnp.zeros_like(head_scr)

    at = pl.program_id(0) * chunks + chunks - 1 - step
    masks, cr = chunk_masks(marks_ref, at, step == chunks - 1)
    mk = jnp.transpose(masks)
    cw = cw_ref[0]
    heads = head_matrix(inner)
    xbc = proj_ref[0, :, LANES + inner :]
    ext = jnp.concatenate([prev_ref[0, :, LANES + inner :], xbc], axis=0)
    conv, moved = conv_in(ext, xbc, mk, cw)
    sig = jax.nn.sigmoid(conv)
    act = conv * sig
    xs = act[:, :inner]
    bmat = act[:, inner : inner + STATE].astype(BF)
    cmat = act[:, inner + STATE :].astype(BF)
    raw, dt, rate, cum, reach, to_end, passing = chunk_rows(proj_ref[0, :, :LANES], hp_ref[0], cr)
    norm = [scale_ref[pl.ds(at, 1)], cube_ref[pl.ds(at, 1)], jnp.zeros((6, CHUNK), F32)]
    cols = jnp.transpose(jnp.concatenate(norm, axis=0))
    gaps = gaps_of(cum, inner // HEAD)
    mask = chunk_mask(mk, cr)
    dt_e = spread(dt, inner)
    reach_e = spread(reach, inner)
    end_e = spread(to_end, inner)
    xd = xs * dt_e
    xdb = xd.astype(BF)

    z = proj_ref[0, :, LANES : LANES + inner]
    sz = jax.nn.sigmoid(z)
    silu_z = z * sz
    ys = ys_ref[0]
    skip = cw[5:6, :inner]
    y = ys + skip * xs
    gated = y * silu_z
    r_mid = d_mid * cols[:, :1]
    d_gated = r_mid * gain_ref[...] - gated * cols[:, 1:2]
    d_gain = jnp.sum(r_mid * gated, axis=0, keepdims=True)
    dy = d_gated * silu_z
    dyb = halved(dy)
    dz = d_gated * y * silu_slope(z, sz)

    state = sin_ref[0, 0]
    d_state = ds_scr[...]
    dsb = d_state.astype(BF)
    scores = scores_of(act, inner)
    reached = (reach_e * dy).astype(BF)
    ended = (end_e * xd).astype(BF)
    d_xd = end_e * dot_parts(halved(act[:, inner : inner + STATE]), halved(d_state))
    d_scores = jnp.zeros((CHUNK, CHUNK), F32)
    parts = []
    for j in range(inner // LANES):
        lanes = slice(j * LANES, (j + 1) * LANES)
        pair_dy = [stacked_halves(part[:, lanes]) for part in dyb]
        d_w = dot(pair_dy[0], xdb[:, lanes], NT)
        ws = []
        for i in range(2):
            decay = decay_of(gaps, mask, 2 * j + i)
            ws.append(scores * decay)
            d_scores = d_scores + d_w[i * CHUNK : (i + 1) * CHUNK] * decay
        parts.append(dot_parts(halved(jnp.concatenate(ws, axis=0)), pair_dy, TN))
    d_xd = d_xd + jnp.concatenate(parts, axis=1)
    dgb = d_scores.astype(BF)
    d_c = dot(reached, state.astype(BF), NT) + dot(dgb, bmat)
    d_b = dot(ended, dsb, NT) + dot(dgb, cmat, TN)
    keep = jnp.sum(passing * heads, axis=0, keepdims=True)
    new_ds = keep * d_state + dot(cmat, reached, TN)
    alpha = by_head(heads, dy * ys)
    beta = by_head(heads, xs * d_xd)
    lane = lax.broadcasted_iota(jnp.int32, (8, CHUNK), 1)
    d_cum = alpha - dt * beta + jnp.where(lane == CHUNK - 1, gam_scr[...], 0.0)
    row = lax.broadcasted_iota(jnp.int32, (CHUNK, CHUNK), 0)
    col = lax.broadcasted_iota(jnp.int32, (CHUNK, CHUNK), 1)
    d_log = along(d_cum, (row >= col).astype(F32))
    d_dt = beta - rate * d_log
    d_raw = d_dt * jax.nn.sigmoid(raw)
    gh_ref[0] += d_raw
    gh_ref[1] += -rate * dt * d_log
    ds_scr[...] = new_ds
    gam_scr[...] = jnp.broadcast_to(
        jnp.sum(heads * jnp.sum(new_ds * state, axis=0, keepdims=True), axis=1, keepdims=True), gam_scr.shape
    )
    d_xs = dt_e * d_xd + skip * dy

    d_conv = jnp.concatenate([d_xs, d_b, d_c], axis=1) * silu_slope(conv, sig)
    d_xbc = cw[TAPS - 1 : TAPS] * d_conv
    gc_ref[TAPS - 1 : TAPS] += jnp.sum(d_conv * xbc, axis=0, keepdims=True)
    for back in range(1, TAPS):
        u = d_conv * mk[:, back - 1 : back]
        full = jnp.concatenate([u, head_scr[back - 1]], axis=0)
        head_scr[back - 1] = u[:8]
        d_xbc = d_xbc + cw[TAPS - 1 - back : TAPS - back] * pltpu.roll(full, CHUNK + 8 - back, 0)[:CHUNK]
        gc_ref[TAPS - 1 - back : TAPS - back] += jnp.sum(d_conv * moved[back - 1], axis=0, keepdims=True)
    gc_ref[4:5] += jnp.sum(d_conv, axis=0, keepdims=True)
    gc_ref[5:6, :inner] += jnp.sum(dy * xs, axis=0, keepdims=True)
    gc_ref[6:7, :inner] += d_gain
    dp_ref[0, :, LANES : LANES + inner] = dz.astype(BF)
    dp_ref[0, :, LANES + inner :] = d_xbc.astype(BF)

    @pl.when((step == chunks - 1) & (pl.program_id(0) == pl.num_programs(0) - 1))
    def _():
        for kind in range(2):
            sums = jnp.concatenate([gh_ref[kind], jnp.zeros((LANES - 8, CHUNK), F32)], axis=0)
            sums = dot(jnp.ones((8, CHUNK), F32), sums, NT, HIGH)
            gc_ref[7:8, kind * LANES : (kind + 1) * LANES] = sums[:1]

    d_rawt = jnp.transpose(jnp.concatenate([d_raw, jnp.zeros((LANES - 8, CHUNK), F32)], axis=0))
    dp_ref[0, :, :LANES] = d_rawt.astype(BF)


MESH = pl.DeviceIdType.MESH


def meet(peers):
    barrier = pltpu.get_barrier_semaphore()
    count = 0
    for here, peer in peers:
        if here is None:
            count = count + 1
            pl.semaphore_signal(barrier, inc=1, device_id=peer, device_id_type=MESH)
        else:
            count = count + here.astype(jnp.int32)

            @pl.when(here)
            def _():
                pl.semaphore_signal(barrier, inc=1, device_id=peer, device_id_type=MESH)

    pl.semaphore_wait(barrier, count)


def line_place(n_seq):
    me = lax.axis_index("seq")
    return me // 2, me % 2, {"seq": me + 1 - 2 * (me % 2)}, {"seq": me - 2}, {"seq": me + 2}


def line_peers(n):
    chip, core, sib, left, right = line_place(2 * n)
    return [(None, sib), (chip > 0, left), (chip < n - 1, right)]


def all_peers(axis, size):
    me = lax.axis_index(axis)
    return [(None, {axis: (me + k) % size}) for k in range(1, size)]


def remote(src, dst, send, recv, device):
    return pltpu.make_async_remote_copy(
        src_ref=src, dst_ref=dst, send_sem=send, recv_sem=recv, device_id=device, device_id_type=MESH
    )


def share_start(axis, size, source, slots, send, recv):
    me = lax.axis_index(axis)
    copies = []
    for k in range(1, size):
        to = (me + k) % size
        copy = remote(source(to), slots.at[k - 1], send.at[k - 1], recv.at[k - 1], {axis: to})
        copy.start()
        copies.append(copy)
    return copies


def share_sum(copies, own, slots):
    total = own.astype(F32)
    for k, copy in enumerate(copies):
        copy.wait_recv()
        total = total + slots[k].astype(F32)
    return total


def share_end(copies):
    for copy in copies:
        copy.wait_send()


def line_gather(n, rows, span, buf, sems, use, begun=None, between=None, ready=None):
    right_s, left_s, sib_s, line_r, sib_r = sems
    chip, core, sib, left, right = line_place(2 * n)
    have_left, have_right = chip > 0, chip < n - 1

    def block(r, j, c):
        return buf.at[r, j, pl.ds(pl.multiple_of(c * span, span), span)]

    def to_sib(r, j, c):
        at = j * rows + r
        return remote(block(r, j, c), block(r, j, c), sib_s.at[at], sib_r.at[at], sib)

    def to_right(r, j):
        at = j * rows + r
        return remote(block(r, j, core), block(r, j, core), right_s.at[at], line_r.at[at], right)

    def to_left(r, j):
        at = j * rows + r
        return remote(block(r, j, core), block(r, j, core), left_s.at[at], line_r.at[at], left)

    def pass_on(r, j, way):
        if way >= 0:

            @pl.when(have_right)
            def _():
                to_right(r, j).start()

        if way <= 0:

            @pl.when(have_left)
            def _():
                to_left(r, j).start()

        to_sib(r, j, core).start()

    def finish(j):
        for r in range(rows):
            to_sib(r, j, 1 - core).wait_recv()
        use(j)

    for r in range(rows):
        if ready is not None:
            ready(r)
        pass_on(r, chip, 0)
    if begun is not None:
        begun()
    finish(chip)

    def step(t, _):
        low, high = chip - t, chip + t
        for r in range(rows):

            @pl.when(low >= 0)
            def _():
                to_right(r, low).wait_recv()
                pass_on(r, low, 1)

            @pl.when(high < n)
            def _():
                to_left(r, high).wait_recv()
                pass_on(r, high, -1)

        def one(k, _):
            j = jnp.where(k == 0, low, high)

            @pl.when((j >= 0) & (j < n))
            def _():
                finish(j)

            return 0

        lax.fori_loop(0, 2, one, 0)
        if between is not None:
            between(t)
        return 0

    lax.fori_loop(1, n, step, 0)

    def done(j, _):
        for r in range(rows):
            to_sib(r, j, core).wait_send()

            @pl.when(have_right & (j <= chip))
            def _():
                to_right(r, j).wait_send()

            @pl.when(have_left & (j >= chip))
            def _():
                to_left(r, j).wait_send()

        return 0

    lax.fori_loop(0, n, done, 0)


def dma(*counts):
    return [pltpu.SemaphoreType.DMA((count,)) for count in counts]


class LineSum:
    def __init__(self, n, rows, emit, own, sib_out, sib_in, out, into, sems):
        self.n, self.rows, self.emit = n, rows, emit
        self.own, self.sib_out, self.sib_in, self.out, self.into = own, sib_out, sib_in, out, into
        self.sib_s, self.right_s, self.left_s, self.sib_r, self.right_r, self.left_r = sems
        self.chip, self.core, self.sib, self.left, self.right = line_place(2 * n)

    @staticmethod
    def scratch(n, rows, span, wide):
        shape = (n, rows, span, wide)
        k = n * rows
        return (
            [pltpu.VMEM(shape, F32)]
            + [pltpu.VMEM(shape, BF)] * 3
            + [pltpu.VMEM((n + 1,) + shape[1:], BF)]
            + dma(k, k, k, k, k, k)
        )

    def to_sib(self, j, r):
        at = j * self.rows + r
        return remote(self.sib_out.at[j, r], self.sib_in.at[j, r], self.sib_s.at[at], self.sib_r.at[at], self.sib)

    def to_right(self, j, r):
        at = j * self.rows + r
        return remote(self.out.at[j, r], self.into.at[j, r], self.right_s.at[at], self.right_r.at[at], self.right)

    def left_copy(self, j, r, owner, device):
        at = j * self.rows + r
        slot = jnp.where(j == owner, self.n, j)
        return remote(self.out.at[j, r], self.into.at[slot, r], self.left_s.at[at], self.left_r.at[at], device)

    def to_left(self, j, r):
        return self.left_copy(j, r, self.chip - 1, self.left)

    def from_right(self, j, r):
        return self.left_copy(j, r, self.chip, self.right)

    def make(self, j):
        self.emit(j)
        for r in range(self.rows):
            self.to_sib(j, r).start()

    def right_j(self, tau):
        j = self.n - 1 - (tau - self.chip)
        return j, (tau >= self.chip) & (j > self.chip)

    def left_j(self, tau):
        j = tau - (self.n - 1 - self.chip)
        return j, (j >= 0) & (j < self.chip)

    def prepare(self, tau):
        def one(k, _):
            jr, on_r = self.right_j(tau)
            jl, on_l = self.left_j(tau)
            j = jnp.where(k == 0, jr, jl)

            @pl.when(((k == 0) & on_r) | ((k == 1) & on_l))
            def _():
                self.make(j)

            return 0

        lax.fori_loop(0, 2, one, 0)

    def step(self, tau):
        jr, on_r = self.right_j(tau)
        jl, on_l = self.left_j(tau)
        own, sib_in, out, into = self.own, self.sib_in, self.out, self.into
        for r in range(self.rows):

            @pl.when(on_r)
            def _():
                self.to_sib(jr, r).wait_recv()

                @pl.when(self.chip > 0)
                def _():
                    self.to_right(jr, r).wait_recv()
                    out[jr, r] = (own[jr, r] + sib_in[jr, r].astype(F32) + into[jr, r].astype(F32)).astype(BF)

                @pl.when(self.chip == 0)
                def _():
                    out[jr, r] = (own[jr, r] + sib_in[jr, r].astype(F32)).astype(BF)

                self.to_right(jr, r).start()

            @pl.when(on_l)
            def _():
                self.to_sib(jl, r).wait_recv()

                @pl.when(self.chip < self.n - 1)
                def _():
                    self.from_right(jl, r).wait_recv()
                    out[jl, r] = (own[jl, r] + sib_in[jl, r].astype(F32) + into[jl, r].astype(F32)).astype(BF)

                @pl.when(self.chip == self.n - 1)
                def _():
                    out[jl, r] = (own[jl, r] + sib_in[jl, r].astype(F32)).astype(BF)

                self.to_left(jl, r).start()

    def finish(self, r):
        chip, own, into = self.chip, self.own, self.into
        self.to_sib(chip, r).wait_recv()
        own[chip, r] = own[chip, r] + self.sib_in[chip, r].astype(F32)

        @pl.when(chip > 0)
        def _():
            self.to_right(chip, r).wait_recv()
            own[chip, r] = own[chip, r] + into[chip, r].astype(F32)

        @pl.when(chip < self.n - 1)
        def _():
            self.from_right(chip, r).wait_recv()
            own[chip, r] = own[chip, r] + into[self.n, r].astype(F32)

    def end(self):
        def done(j, _):
            for r in range(self.rows):
                self.to_sib(j, r).wait_send()

                @pl.when(j > self.chip)
                def _():
                    self.to_right(j, r).wait_send()

                @pl.when(j < self.chip)
                def _():
                    self.to_left(j, r).wait_send()

            return 0

        lax.fori_loop(0, self.n, done, 0)

    def run(self, between=None, before_end=None, to_end=True):
        self.prepare(0)

        def step(tau, _):
            self.step(tau)
            self.prepare(tau + 1)
            if between is not None:
                between(tau)
            return 0

        lax.fori_loop(0, self.n - 1, step, 0)
        self.make(self.chip)
        if before_end is not None:
            before_end()
        if to_end:
            for r in range(self.rows):
                self.finish(r)
            self.end()


def halves(own, so, j, core, start, p, rows, span):
    stop = start + p.shape[1]
    for r in range(rows):
        low, high = p[r * CHUNK : r * CHUNK + span], p[r * CHUNK + span : (r + 1) * CHUNK]
        own[j, r, :, start:stop] = jnp.where(core == 0, low, high)
        so[j, r, :, start:stop] = jnp.where(core == 0, high, low).astype(BF)


def dp_neighbours():
    d = lax.axis_index("dp")
    return d, d + 1 - 2 * (d % 2), (d + 2) % 4, 3 - d


def either(even, yes, no):
    @pl.when(even)
    def _():
        yes()

    @pl.when(jnp.logical_not(even))
    def _():
        no()


class Spread:
    def __init__(self, n_dp, at, count, sems):
        self.n_dp, self.at, self.count = n_dp, at, count
        self.s, self.r = sems

    @staticmethod
    def scratch(n_dp, count):
        return dma((n_dp - 1) * count, (n_dp - 1) * count)

    def copy(self, kind, owner, i, to):
        where = self.at(owner, i)
        sem = kind * self.count + i
        return remote(where, where, self.s.at[sem], self.r.at[sem], {"dp": to})

    def hand(self, i):
        d = lax.axis_index("dp")
        if self.n_dp == 4:
            d, x, y, _ = dp_neighbours()
            self.copy(0, d, i, x).start()
            self.copy(1, d, i, y).start()
        else:
            for k in range(1, self.n_dp):
                self.copy(k - 1, d, i, (d + k) % self.n_dp).start()

    def relay(self, i):
        if self.n_dp == 4:
            d, x, y, _ = dp_neighbours()

            def by_x():
                self.copy(0, x, i, x).wait_recv()
                self.copy(2, x, i, y).start()

            def by_y():
                self.copy(1, y, i, y).wait_recv()
                self.copy(2, y, i, x).start()

            either(i % 2 == 0, by_x, by_y)

    def end(self, i):
        d = lax.axis_index("dp")
        if self.n_dp == 4:
            d, x, y, across = dp_neighbours()

            def by_x():
                self.copy(1, y, i, y).wait_recv()
                self.copy(2, across, i, y).wait_recv()
                self.copy(2, x, i, y).wait_send()

            def by_y():
                self.copy(0, x, i, x).wait_recv()
                self.copy(2, across, i, x).wait_recv()
                self.copy(2, y, i, x).wait_send()

            either(i % 2 == 0, by_x, by_y)
            self.copy(0, d, i, x).wait_send()
            self.copy(1, d, i, y).wait_send()
        else:
            for k in range(1, self.n_dp):
                source = (d - k + self.n_dp) % self.n_dp
                self.copy(k - 1, source, i, source).wait_recv()
                self.copy(k - 1, d, i, (d + k) % self.n_dp).wait_send()


def spread_halves(n_dp, place, own, sems):
    half = own.shape[0] // 2
    return Spread(n_dp, lambda owner, i: place.at[owner, pl.ds(pl.multiple_of(i * half, half), half)], 2, sems)


class DpSum:
    def __init__(self, n_dp, term, slots, piece, sems):
        self.n_dp, self.term, self.slots, self.piece = n_dp, term, slots, piece
        self.count = term.shape[1] // piece
        self.s, self.r = sems

    @staticmethod
    def scratch(n_dp, rows, cols, piece):
        count = (n_dp - 1) * (rows // piece)
        return [pltpu.VMEM((n_dp - 1, rows, cols), BF)] + dma(count, count)

    def rows_of(self, i):
        return pl.ds(pl.multiple_of(i * self.piece, self.piece), self.piece)

    def copy(self, kind, source, i, to):
        sem = kind * self.count + i
        return remote(source, self.slots.at[kind, self.rows_of(i)], self.s.at[sem], self.r.at[sem], {"dp": to})

    def part(self, kind, owner, i, to):
        return self.copy(kind, self.term.at[owner, self.rows_of(i)], i, to)

    def on(self, i):
        return self.copy(2, self.slots.at[1, self.rows_of(i)], i, self.axes(i)[1])

    def axes(self, i):
        d, x, y, across = dp_neighbours()
        even = i % 2 == 0
        return jnp.where(even, x, y), jnp.where(even, y, x), across, d

    def send(self, i):
        if self.n_dp == 4:
            first, second, across, d = self.axes(i)
            self.part(1, across, i, first).start()
            self.part(0, first, i, first).start()
        else:
            d = lax.axis_index("dp")
            for k in range(1, self.n_dp):
                to = (d + k) % self.n_dp
                self.part(k - 1, to, i, to).start()

    def middle(self, i):
        if self.n_dp == 4:
            first, second, across, d = self.axes(i)
            here = self.rows_of(i)
            self.part(1, across, i, first).wait_recv()
            self.slots[1, here] = (self.term[second, here].astype(F32) + self.slots[1, here].astype(F32)).astype(BF)
            self.on(i).start()

    def total(self, i):
        d = lax.axis_index("dp")
        here = self.rows_of(i)
        total = self.term[d, here].astype(F32)
        if self.n_dp == 4:
            first, second, across, d = self.axes(i)
            self.part(0, first, i, first).wait_recv()
            self.on(i).wait_recv()
            return total + self.slots[0, here].astype(F32) + self.slots[2, here].astype(F32)
        for k in range(1, self.n_dp):
            to = (d + k) % self.n_dp
            self.part(k - 1, to, i, to).wait_recv()
            total = total + self.slots[k - 1, here].astype(F32)
        return total

    def end(self, i):
        if self.n_dp == 4:
            first, second, across, d = self.axes(i)
            self.part(1, across, i, first).wait_send()
            self.part(0, first, i, first).wait_send()
            self.on(i).wait_send()
        else:
            d = lax.axis_index("dp")
            for k in range(1, self.n_dp):
                to = (d + k) % self.n_dp
                self.part(k - 1, to, i, to).wait_send()


class Cut:
    def __init__(self, level, w_ref, dts_ref, parts, sems):
        n_seq, _, cols = parts.shape
        inner = DI // n_seq
        groups = self.groups(n_seq, sems.shape[0])
        size = inner // groups
        bc = CONV_CH - DI
        pairs = [(dts_ref, parts.at[:, :, pl.ds(0, LANES)])]
        for s in range(n_seq):
            for kind in range(2):
                for g in range(groups):
                    source = w_ref.at[level, :, pl.ds(kind * DI + (g * n_seq + s) * size, size)]
                    pairs.append((source, parts.at[s, :, pl.ds(LANES + kind * inner + g * size, size)]))
            pairs.append((w_ref.at[level, :, pl.ds(2 * DI, bc)], parts.at[s, :, pl.ds(cols - bc, bc)]))
        self.copies = [pltpu.make_async_copy(a, b, sems.at[i]) for i, (a, b) in enumerate(pairs)]

    @staticmethod
    def count(n_seq, groups):
        return 1 + n_seq * (2 * groups + 1)

    @staticmethod
    def groups(n_seq, count):
        return ((count - 1) // n_seq - 1) // 2

    def start(self):
        for copy in self.copies:
            copy.start()

    def wait(self):
        for copy in self.copies:
            copy.wait()


class Fetch:
    def __init__(self, n_dp, n_seq, parts, wv, refs):
        self.n_dp, self.n_seq, self.parts, self.wv = n_dp, n_seq, parts, wv
        self.a_s, self.a_r = refs[:2]
        self.spread = Spread(n_dp, lambda owner, i: wv.at[owner, i], n_seq, refs[2:4])

    @staticmethod
    def scratch(n_dp, n_seq):
        return dma(n_seq, n_seq) + Spread.scratch(n_dp, n_seq)

    def across(self, i):
        me, d = lax.axis_index("seq"), lax.axis_index("dp")
        to = (me + i) % self.n_seq
        return remote(self.parts.at[to], self.wv.at[d, me], self.a_s.at[to], self.a_r.at[me], {"seq": to})

    def place(self, i):
        return (lax.axis_index("seq") - i + self.n_seq) % self.n_seq

    def arrival(self, i):
        me, d = lax.axis_index("seq"), lax.axis_index("dp")
        source = self.place(i)
        return remote(self.parts.at[me], self.wv.at[d, source], self.a_s.at[me], self.a_r.at[source], {"seq": source})

    def start(self):
        def go(i, _):
            self.across(i).start()
            return 0

        lax.fori_loop(1, self.n_seq, go, 0)
        me, d = lax.axis_index("seq"), lax.axis_index("dp")
        self.wv[d, me] = self.parts[me]
        self.spread.hand(me)

    def pull(self, first, last):
        def one(i, _):
            @pl.when(i < self.n_seq)
            def _():
                self.arrival(i).wait_recv()
                self.spread.hand(self.place(i))

                @pl.when(i >= 2)
                def _():
                    self.spread.relay(self.place(i - 2))

            return 0

        lax.fori_loop(first, last, one, 0)

    def tail(self):
        self.spread.relay(self.place(self.n_seq - 2))
        self.spread.relay(self.place(self.n_seq - 1))

    def end(self):
        def ended(i, _):
            self.spread.end(i)
            return 0

        lax.fori_loop(0, self.n_seq, ended, 0)

    def sent(self):
        def one(i, _):
            self.across(i).wait_send()
            return 0

        lax.fori_loop(1, self.n_seq, one, 0)


class Pieces:
    def __init__(self, n_dp, n_seq, term, got, refs):
        self.n_seq, self.got = n_seq, got
        self.piece = got.shape[1]
        slots, dp_s, dp_r, self.sums, self.seq_s, self.seq_r = refs
        self.sum = DpSum(n_dp, term, slots, self.piece, (dp_s, dp_r))
        self.per = LANES // self.piece
        self.tiles = term.shape[1] // LANES

    @staticmethod
    def scratch(n_dp, n_seq, rows, cols):
        piece = rows // n_seq
        return DpSum.scratch(n_dp, rows, cols, piece) + [pltpu.VMEM((n_seq, piece, cols), BF)] + dma(n_seq, n_seq)

    def tile(self, i):
        if 2 * self.tiles == self.n_seq:
            return (lax.axis_index("seq") // 2 + 1 + i) % self.tiles
        return i

    def each(self, i, act):
        def one(k, _):
            act(i * self.per + k, self.tile(i) * self.per + k)
            return 0

        lax.fori_loop(0, self.per, one, 0)

    def tiles_do(self, first, last, *acts):
        def one(i, _):
            @pl.when((i >= 0) & (i < self.tiles))
            def _():
                for act in acts:
                    act(i)

            return 0

        lax.fori_loop(first, last, one, 0)

    def over_seq(self, s):
        me = lax.axis_index("seq")
        return remote(self.sums.at[s], self.got.at[me], self.seq_s.at[s], self.seq_r.at[me], {"seq": s})

    def from_seq(self, s):
        me = lax.axis_index("seq")
        return remote(self.sums.at[me], self.got.at[s], self.seq_s.at[me], self.seq_r.at[s], {"seq": s})

    def send(self, i):
        self.each(i, lambda p, s: self.sum.send(p))

    def middle(self, i):
        self.each(i, lambda p, s: self.sum.middle(p))

    def last(self, i):
        me = lax.axis_index("seq")

        def finish(p, s):
            total = self.sum.total(p).astype(BF)

            def away():
                self.sums[s] = total
                self.over_seq(s).start()

            def stay():
                self.got[s] = total

            either(s != me, away, stay)

        self.each(i, finish)

    def end(self):
        me = lax.axis_index("seq")

        def sent(p, s):
            self.sum.end(p)

        self.tiles_do(0, self.tiles, lambda i: self.each(i, sent))

        def one(s, _):
            @pl.when(s != me)
            def _():
                self.over_seq(s).wait_send()
                self.from_seq(s).wait_recv()

            return 0

        lax.fori_loop(0, self.n_seq, one, 0)


class Loads:
    def __init__(self, sources, places, sems):
        self.copies = [pltpu.make_async_copy(s, p, sems.at[i]) for i, (s, p) in enumerate(zip(sources, places))]

    @staticmethod
    def scratch(*arrays):
        return [pltpu.VMEM(x.shape, x.dtype) for x in arrays] + dma(len(arrays))

    def start(self):
        for copy in self.copies:
            copy.start()

    def wait(self, *which):
        for i in which:
            self.copies[i].wait()


VMEM_SPEC = pl.BlockSpec(memory_space=pltpu.VMEM)
ANY_SPEC = pl.BlockSpec(memory_space=pl.ANY)


def comm_params(name):
    return pltpu.CompilerParams(collective_id=name, has_side_effects=True, vmem_limit_bytes=60 * 2**20)


def project_kernel(n, n_dp, level, x_ref, gain_ref, *refs):
    n_seq = 2 * n
    rows, span, width = x_ref.shape
    wo_ref, marks_ref, win_ref, dts_ref = refs[:4]
    hid_ref, proj_ref, w_ref, wout_ref, all_ref = refs[4:9]
    cut = Cut(level, win_ref, dts_ref, *refs[9:11])
    cut.start()
    buf, wv, po = refs[11:14]
    line, (w_sem, hid_sem, out_sem) = refs[14:19], refs[19:22]
    get = Fetch(n_dp, n_seq, refs[9], wv, refs[22:26])
    o_s, o_r, m_s, m_r, mall = refs[26:]
    chip, core, sib, left, right = line_place(n_seq)
    me = lax.axis_index("seq")
    d = lax.axis_index("dp")
    for r in range(rows):
        x = x_ref[r].astype(F32)
        scale = lax.rsqrt(jnp.mean(x * x, axis=-1, keepdims=True) + EPS)
        buf[r, chip, pl.ds(pl.multiple_of(core * span, span), span)] = (x * scale * gain_ref[...]).astype(BF)
    meet(all_peers("seq", n_seq) + all_peers("dp", n_dp))
    cut.wait()

    def out_copies(j):
        return (
            pltpu.make_async_copy(buf.at[:, j], hid_ref.at[:, j], hid_sem.at[j]),
            pltpu.make_async_copy(po.at[j], proj_ref.at[:, pl.ds(j * CHUNK, CHUNK)], out_sem.at[j]),
        )

    def use(j):
        block = buf[:, j].reshape(rows * CHUNK, width)
        res = dot(block, wv[...].reshape(width, wv.shape[-1]))
        for r in range(rows):
            po[j, r] = res[r * CHUNK : (r + 1) * CHUNK]
        for copy in out_copies(j):
            copy.start()

    def done(j, _):
        for copy in out_copies(j):
            copy.wait()
        return 0

    outs = spread_halves(n_dp, wout_ref, wo_ref, (o_s, o_r))

    def marks_copy(i):
        to = (me + i) % n_seq
        return remote(marks_ref, mall.at[me], m_s.at[to], m_r.at[me], {"seq": to})

    def marks_in(i):
        source = (me - i + n_seq) % n_seq
        return remote(marks_ref, mall.at[source], m_s.at[me], m_r.at[source], {"seq": source})

    get.start()
    for i in range(1, n_seq):
        marks_copy(i).start()
    mall[me] = marks_ref[...]

    def begun():
        get.pull(1, n_seq)
        wout_ref[d] = wo_ref[...]
        for i in range(2):
            outs.hand(i)
        get.tail()

    line_gather(n, rows, span, buf, line, lambda j: None, begun)
    for i in range(1, n_seq):
        marks_in(i).wait_recv()
    for r in range(rows):
        for j in range(n):
            all_ref[r * n + j : r * n + j + 1] = mall[2 * j, r : r + 1] + mall[2 * j + 1, r : r + 1]
    for i in range(2):
        outs.relay(i)

    get.end()
    keep = pltpu.make_async_copy(wv, w_ref, w_sem.at[0])
    keep.start()

    def each(j, _):
        use(j)
        return 0

    lax.fori_loop(0, n, each, 0)
    for i in range(2):
        outs.end(i)

    get.sent()
    for i in range(1, n_seq):
        marks_copy(i).wait_send()
    lax.fori_loop(0, n, done, 0)
    keep.wait()


def parts_shape(w_in, n_seq):
    cols = LANES + 2 * (DI // n_seq) + CONV_CH - DI
    return jax.ShapeDtypeStruct((n_seq, w_in.shape[1], cols), BF)


def project(x, gain, wo, marks, w_in, dts, level, groups, n_dp, n_seq):
    rows, span, width = x.shape
    n = n_seq // 2
    k = n * rows
    parts = parts_shape(w_in, n_seq)
    cols = parts.shape[2]
    w_shape = (n_dp, n_seq) + parts.shape[1:]
    return pl.pallas_call(
        functools.partial(project_kernel, n, n_dp, level),
        in_specs=[VMEM_SPEC] * 4 + [ANY_SPEC] * 2,
        out_specs=[ANY_SPEC] * 3 + [VMEM_SPEC] * 2,
        out_shape=[
            jax.ShapeDtypeStruct((rows, n, CHUNK, width), BF),
            jax.ShapeDtypeStruct((rows, n * CHUNK, cols), F32),
            jax.ShapeDtypeStruct(w_shape, BF),
            jax.ShapeDtypeStruct((n_dp,) + wo.shape, BF),
            jax.ShapeDtypeStruct((k, CHUNK), F32),
        ],
        scratch_shapes=[pltpu.VMEM(parts.shape, BF)]
        + dma(Cut.count(n_seq, groups))
        + [
            pltpu.VMEM((rows, n, CHUNK, width), BF),
            pltpu.VMEM(w_shape, BF),
            pltpu.VMEM((n, rows, CHUNK, cols), F32),
        ]
        + dma(k, k, k, k, k, 1, n, n)
        + Fetch.scratch(n_dp, n_seq)
        + Spread.scratch(n_dp, 2)
        + dma(n_seq, n_seq)
        + [pltpu.VMEM((n_seq,) + marks.shape, F32)],
        compiler_params=comm_params(0),
        cost_estimate=pl.CostEstimate(flops=6 * 10**9, bytes_accessed=20 * 2**20, transcendentals=0),
    )(x, gain, wo, marks, w_in, dts)


def turn_kernel(
    n, n_dp, level, ss_ref, gain_ref, gain_in_ref, wo_ref, win_ref, dts_ref, *refs,
):
    n_seq = 2 * n
    y_ref, mid_ref, scale_ref, wout_ref, next_ref, hid_ref, proj_ref = refs[3:10]
    gated_ref, w_ref, x_ref = refs[10:13]
    loads = Loads(refs[:3], refs[10:13], refs[13])
    loads.start()
    parts_ref, cut_sems, slots, share_s, share_r, own, so, *refs = refs[14:]
    cut = Cut(level, win_ref, dts_ref, parts_ref, cut_sems)
    cut.start()
    rows, span, width = x_ref.shape
    line, (wv, w_sem, buf, po, hid_sem, out_sem) = refs[:9], refs[9:15]
    get = Fetch(n_dp, n_seq, parts_ref, wv, refs[15:19])
    outs = spread_halves(n_dp, wout_ref, wo_ref, refs[19:21])
    gather = refs[21:]
    chip, core, sib, left, right = line_place(n_seq)
    meet(all_peers("seq", n_seq) + all_peers("dp", n_dp))
    copies = share_start("seq", n_seq, lambda to: ss_ref, slots, share_s, share_r)
    total = share_sum(copies, ss_ref[...], slots)
    cut.wait()
    get.start()
    loads.wait(0, 1, 2)
    scale = lax.rsqrt(total / DI + EPS)
    scale_ref[...] = scale
    cols = jnp.transpose(scale)
    for r in range(rows):
        for k in range(n):
            at = r * n + k
            g = gated_ref[r, k * CHUNK : (k + 1) * CHUNK]
            mid_ref[r, k * CHUNK : (k + 1) * CHUNK] = (g * cols[:, at : at + 1] * gain_ref[...]).astype(BF)

    def emit(j):
        here = pl.ds(pl.multiple_of(j * CHUNK, CHUNK), CHUNK)
        block = jnp.concatenate([mid_ref[r, here] for r in range(rows)], axis=0)
        for at in range(0, width, 512):
            halves(own, so, j, core, at, dot(block, w_ref[:, at : at + 512]), rows, span)

    per = -(-(n_seq - 1) // (n - 1))
    sums = LineSum(n, rows, emit, own, so, *line[:3], line[3:])
    sums.run(lambda tau: get.pull(1 + tau * per, 1 + tau * per + per), to_end=False)

    def ready(r):
        sums.finish(r)
        y = x_ref[r].astype(F32) + own[chip, r]
        y_ref[r] = y
        norm = lax.rsqrt(jnp.mean(y * y, axis=-1, keepdims=True) + EPS)
        buf[r, chip, pl.ds(pl.multiple_of(core * span, span), span)] = (y * norm * gain_in_ref[...]).astype(BF)
    keep = pltpu.make_async_copy(wv, next_ref, w_sem.at[0])

    def begun():
        get.tail()
        get.end()
        wout_ref[lax.axis_index("dp")] = wo_ref[...]
        for i in range(2):
            outs.hand(i)
        keep.start()

    def out_copies(j):
        return (
            pltpu.make_async_copy(buf.at[:, j], hid_ref.at[:, j], hid_sem.at[j]),
            pltpu.make_async_copy(po.at[j], proj_ref.at[:, pl.ds(j * CHUNK, CHUNK)], out_sem.at[j]),
        )

    def use(j):
        block = buf[:, j].reshape(rows * CHUNK, width)
        res = dot(block, wv[...].reshape(width, wv.shape[-1]))
        for r in range(rows):
            po[j, r] = res[r * CHUNK : (r + 1) * CHUNK]
        for copy in out_copies(j):
            copy.start()

    def done(j, _):
        for copy in out_copies(j):
            copy.wait()
        return 0

    def between(t):
        @pl.when(t == n - 2)
        def _():
            for i in range(2):
                outs.relay(i)

    line_gather(n, rows, span, buf, gather, use, begun, between, ready)
    sums.end()
    for i in range(2):
        outs.end(i)
    get.sent()
    share_end(copies)
    lax.fori_loop(0, n, done, 0)
    keep.wait()


def turn(gated, ss, gain, w, x, gain_in, wo, w_in, dts, level, groups, n_dp, n_seq):
    rows, span, width = x.shape
    n = n_seq // 2
    k = n * rows
    parts = parts_shape(w_in, n_seq)
    cols = parts.shape[2]
    w_shape = (n_dp, n_seq) + parts.shape[1:]
    return pl.pallas_call(
        functools.partial(turn_kernel, n, n_dp, level),
        in_specs=[VMEM_SPEC] * 4 + [ANY_SPEC] * 5,
        out_specs=[VMEM_SPEC] * 4 + [ANY_SPEC] * 3,
        out_shape=[
            jax.ShapeDtypeStruct(x.shape, F32),
            jax.ShapeDtypeStruct(gated.shape, BF),
            jax.ShapeDtypeStruct(ss.shape, F32),
            jax.ShapeDtypeStruct((n_dp,) + wo.shape, BF),
            jax.ShapeDtypeStruct(w_shape, BF),
            jax.ShapeDtypeStruct((rows, n, CHUNK, width), BF),
            jax.ShapeDtypeStruct((rows, n * CHUNK, cols), F32),
        ],
        scratch_shapes=Loads.scratch(gated, w, x)
        + [pltpu.VMEM(parts.shape, BF)]
        + dma(Cut.count(n_seq, groups))
        + [pltpu.VMEM((n_seq - 1,) + ss.shape, F32)]
        + dma(n_seq - 1, n_seq - 1)
        + LineSum.scratch(n, rows, span, width)
        + [pltpu.VMEM(w_shape, BF)]
        + dma(1)
        + [pltpu.VMEM((rows, n, CHUNK, width), BF), pltpu.VMEM((n, rows, CHUNK, cols), F32)]
        + dma(n, n)
        + Fetch.scratch(n_dp, n_seq)
        + Spread.scratch(n_dp, 2)
        + dma(k, k, k, k, k),
        compiler_params=comm_params(1),
        cost_estimate=pl.CostEstimate(flops=9 * 10**9, bytes_accessed=30 * 2**20, transcendentals=0),
    )(ss, gain, gain_in, wo, w_in, dts, gated, w, x)


def back_mix_kernel(n, n_dp, top, with_out, *refs):
    n_seq = 2 * n
    refs = list(refs)
    take = lambda k: [refs.pop(0) for _ in range(k)]
    proj_ref, prev_ref, marks_ref, cw_ref, hp_ref, ys_ref, sin_ref, gain_ref = take(8)
    if top:
        (ss_ref,) = take(1)
        sources = take(5)
    else:
        scale_ref, cols_ref, gains_ref = take(3)
        sources = take(5)
    dp_ref, gc_ref, gout_ref = take(3)
    if top:
        (y_ref,) = take(1)
    else:
        got_ref, cols_all, gains_all = take(3)
    places = take(len(sources))
    loads = Loads(sources, places, *take(1))
    gated_ref, w_ref, g_ref = places[:3]
    if top:
        x_ref, mine_ref = places[3:]
    else:
        mid_ref, term_ref = places[3:]
    mixer = take(4)
    dmid, acc, gwb, scale_scr, cube_scr, tot, slots = take(7)
    share_s, share_r = take(2)
    if with_out:
        outs = DpSum(n_dp, gwb, refs[0], gwb.shape[1] // 2, refs[1:3])
        take(3)
    rows, span, width = (x_ref if top else g_ref).shape
    inner = gated_ref.shape[2]
    chip, core, sib, left, right = line_place(n_seq)
    step = pl.program_id(1)
    k = pl.program_id(0) * n + step
    last = rows * n - 1
    ones = jnp.ones((8, inner), F32)
    if top:
        own, so = refs[:2]
        line = LineSum(n, rows, None, own, so, *refs[2:5], refs[5:11])
        mids, turn, buf = refs[11:14]
        line_sems = refs[14:19]
        span_rows = pl.ds(pl.multiple_of(core * span, span), span)
    else:
        buf, line_sems, got, cols_in, gains_in = refs[0], refs[1:6], refs[6], refs[7], refs[8]
        pieces = Pieces(n_dp, n_seq, term_ref, got, refs[9:15])
        smalls = [
            Small(n_dp, n_seq, cols_ref, cols_in, *refs[15:21]),
            Small(n_dp, n_seq, gains_ref, gains_in, *refs[21:27]),
        ]

    def through(j, block, mid):
        chunk = pl.ds(pl.multiple_of(j * CHUNK, CHUNK), CHUNK)
        res = dot(block, w_ref[...], NT)
        for at in range(0, width, 512):
            acc[:, at : at + 512] += dot(mid, block[:, at : at + 512], TN)
        for r in range(rows):
            part = res[r * CHUNK : (r + 1) * CHUNK]
            dmid[r, chunk] = part
            v = part * gain_ref[...] * gated_ref[r, chunk]
            tot[pl.ds(r * n + j, 1)] = by_head(ones, v)[:1]

    @pl.when(k == 0)
    def _():
        loads.start()
        if not top:
            acc[...] = jnp.zeros_like(acc)
        if top:
            meet(all_peers("seq", n_seq) + (all_peers("dp", n_dp) if with_out else []))
            first = share_start("seq", n_seq, lambda to: ss_ref, slots.at[0], share_s.at[0], share_r.at[0])
            scale = lax.rsqrt(share_sum(first, ss_ref[...], slots.at[0]) / DI + EPS)
            share_end(first)
            scale_scr[...] = scale
            cols = jnp.transpose(scale)
            loads.wait(0, 1)
            for r in range(rows):
                for j in range(n):
                    at = r * n + j
                    part = gated_ref[r, j * CHUNK : (j + 1) * CHUNK] * cols[:, at : at + 1] * gain_ref[...]
                    mids[at * CHUNK : (at + 1) * CHUNK] = part.astype(BF)
                    turn[:, at * CHUNK : (at + 1) * CHUNK] = jnp.transpose(part).astype(BF)

            def back(r, every, first):
                dmid[r] = dot(every, w_ref[...], NT)
                for j in range(n):
                    chunk = slice(j * CHUNK, (j + 1) * CHUNK)
                    v = dmid[r, chunk] * gain_ref[...] * gated_ref[r, chunk]
                    tot[r * n + j : r * n + j + 1] = by_head(ones, v)[:1]
                for at in range(0, width, 512):
                    value = dot(turn[:, r * n * CHUNK : (r + 1) * n * CHUNK], every[:, at : at + 512])
                    acc[:, at : at + 512] = value if first else acc[:, at : at + 512] + value

            def begun():
                for at in range(0, width, 512):
                    out = dot(mids[...], w_ref[:, at : at + 512])
                    for j in range(n):
                        for r in range(rows):
                            low = (r * n + j) * CHUNK
                            p, q = out[low : low + span], out[low + span : low + CHUNK]
                            own[j, r, :, at : at + 512] = jnp.where(core == 0, p, q)
                            so[j, r, :, at : at + 512] = jnp.where(core == 0, q, p).astype(BF)
                for j in range(n):
                    for r in range(rows):
                        line.to_sib(j, r).start()
                line.step(0)
                loads.wait(2)
                back(0, g_ref[...].reshape(n * CHUNK, width), True)

            def between(t):
                @pl.when(t == n - 2)
                def _():
                    line.step(1)

            loads.wait(4)
            for r in range(1, rows):
                buf[r - 1, chip, span_rows] = mine_ref[r]
            line_gather(n, rows - 1, span, buf, line_sems, lambda j: None, begun, between)
            for r in range(1, rows):
                back(r, buf[r - 1].reshape(n * CHUNK, width), False)
            second = share_start("seq", n_seq, lambda to: tot, slots.at[1], share_s.at[1], share_r.at[1])
        else:
            scale = scale_ref[...]
            scale_scr[...] = scale
            here = pl.ds(pl.multiple_of(core * span, span), span)
            loads.wait(2)
            for r in range(rows):
                buf[r, chip, here] = g_ref[r].astype(BF)
            meet(all_peers("seq", n_seq) + all_peers("dp", n_dp))
            loads.wait(4)

            for small in smalls:
                small.start()
            pieces.tiles_do(0, pieces.tiles, pieces.send)

            def use(j):
                chunk = pl.ds(pl.multiple_of(j * CHUNK, CHUNK), CHUNK)
                mid = jnp.concatenate([mid_ref[r, chunk] for r in range(rows)], axis=0)
                through(j, buf[:, j].reshape(rows * CHUNK, width), mid)

            def between(t):
                at = jnp.maximum(2 * (t - 2), 0)
                pieces.tiles_do(at, jnp.where(t < 2, at, at + 2), pieces.middle)

            line_gather(n, rows, span, buf, line_sems, use, lambda: loads.wait(0, 1, 3), between)
            second = share_start("seq", n_seq, lambda to: tot, slots.at[1], share_s.at[1], share_r.at[1])
        for d in range(n_dp):
            size = inner // n_dp
            gwb[d] = acc[d * size : (d + 1) * size].astype(BF)
        if with_out:
            for i in range(2):
                outs.send(i)
        else:
            gout_ref[...] = gwb[...]
        cube_scr[...] = scale * scale * scale * (share_sum(second, tot[...], slots.at[1]) / DI)
        share_end(second)

    at = pl.multiple_of((n - 1 - step) * CHUNK, CHUNK)
    mix_bwd_step(
        inner, n, proj_ref, prev_ref, marks_ref, cw_ref, hp_ref, ys_ref, sin_ref,
        dmid[pl.program_id(0), pl.ds(at, CHUNK)], scale_scr, cube_scr, gain_ref, dp_ref, gc_ref, *mixer,
    )

    if top:

        @pl.when((k % 2 == 1) & (k < last - 1))
        def _():
            line.step((k + 3) // 2)
    else:

        @pl.when(k == 0)
        def _():
            for small in smalls:
                small.middle()

        @pl.when(2 * k < pieces.tiles)
        def _():
            pieces.tiles_do(2 * k, 2 * k + 2, pieces.last)

    if with_out:

        @pl.when(k == last // 2)
        def _():
            for i in range(2):
                outs.middle(i)

    @pl.when(k == last)
    def _():
        if with_out:
            for i in range(2):
                gout_ref[outs.rows_of(i)] = outs.total(i)
                outs.end(i)
        if top:
            loads.wait(3)
            for r in range(rows):
                line.finish(r)
                y_ref[r] = (x_ref[r] + own[chip, r]).astype(BF)
            line.end()
        else:
            for small in smalls:
                small.end()
            pieces.end()

            got_ref[...] = got[...]
            cols_all[...] = cols_in[...]
            gains_all[...] = gains_in[...]


def back_mix(proj, marks, cws, hps, level, ys, sin, gain, gated, w, g, more, n_dp, n_seq, with_out):
    small, big = more
    top = len(small) == 1
    rows, length, cols = proj.shape
    span, width = g.shape[-2:]
    n = n_seq // 2
    inner = gated.shape[2]
    k = rows * n
    bc = CONV_CH - DI
    at = lambda r, c: (r, n - 1 - c, 0)

    def whole(x):
        zeros = (0,) * len(x.shape)
        return pl.BlockSpec(x.shape, lambda r, c: zeros, pipeline_mode=pl.Buffered(1))

    if with_out:
        gout = jax.ShapeDtypeStruct((inner // n_dp, width), F32)
    else:
        gout = jax.ShapeDtypeStruct((n_dp, inner // n_dp, width), BF)
    outs = [
        jax.ShapeDtypeStruct((rows, length, cols), BF),
        jax.ShapeDtypeStruct((8, inner + bc), F32),
        gout,
    ]
    big = (gated, w, g) + tuple(big)
    scratch = Loads.scratch(*big) + [
        pltpu.VMEM((STATE, inner), F32),
        pltpu.VMEM((8, LANES), F32),
        pltpu.VMEM((TAPS - 1, 8, inner + bc), F32),
        pltpu.VMEM((2, 8, CHUNK), F32),
        pltpu.VMEM((rows, length, inner), F32),
        pltpu.VMEM((inner, width), F32),
        pltpu.VMEM((n_dp, inner // n_dp, width), BF),
        pltpu.VMEM((k, CHUNK), F32),
        pltpu.VMEM((k, CHUNK), F32),
        pltpu.VMEM((k, CHUNK), F32),
        pltpu.VMEM((2, n_seq - 1, k, CHUNK), F32),
        pltpu.SemaphoreType.DMA((2, n_seq - 1)),
        pltpu.SemaphoreType.DMA((2, n_seq - 1)),
    ]
    if with_out:
        scratch += DpSum.scratch(n_dp, inner // n_dp, width, inner // n_dp // 2)
    if top:
        outs.append(jax.ShapeDtypeStruct((rows, span, width), BF))
        scratch += LineSum.scratch(n, rows, span, width)
        scratch += [pltpu.VMEM((length * rows, inner), BF), pltpu.VMEM((inner, length * rows), BF)]
        scratch += [pltpu.VMEM((rows - 1, n, CHUNK, width), BF)] + dma(*[k - n] * 5)
    else:
        (_, *vecs), (_, term) = more
        outs.append(jax.ShapeDtypeStruct((n_seq, width // (n_dp * n_seq), term.shape[2]), BF))
        outs += [jax.ShapeDtypeStruct((n_seq,) + vec.shape, F32) for vec in vecs]
        scratch += [pltpu.VMEM((rows, n, CHUNK, width), BF)] + dma(k, k, k, k, k)
        scratch += [pltpu.VMEM(out.shape, out.dtype) for out in outs[-3:]]
        scratch += Pieces.scratch(n_dp, n_seq, term.shape[1], term.shape[2])
        for vec in vecs:
            scratch += Small.scratch(n_dp, n_seq, vec)
    def of_level(x):
        zeros = (0,) * (len(x.shape) - 1)
        return pl.BlockSpec((1,) + x.shape[1:], lambda r, c: (level,) + zeros)

    rest = (gain,) + tuple(small)
    return pl.pallas_call(
        functools.partial(back_mix_kernel, n, n_dp, top, with_out),
        grid=(rows, n),
        in_specs=[
            pl.BlockSpec((1, CHUNK, cols), at),
            pl.BlockSpec((1, 8, cols), lambda r, c: (r, jnp.maximum((n - 1 - c) * (CHUNK // 8) - 1, 0), 0)),
        ]
        + [whole(marks), of_level(cws), of_level(hps)]
        + [
            pl.BlockSpec((1, CHUNK, inner), at),
            pl.BlockSpec((1, 1, STATE, inner), lambda r, c: (r, n - 1 - c, 0, 0)),
        ]
        + [whole(x) for x in rest]
        + [ANY_SPEC] * len(big),
        out_specs=[pl.BlockSpec((1, CHUNK, cols), at)] + [whole(x) for x in outs[1:]],
        out_shape=outs,
        scratch_shapes=scratch,
        compiler_params=pltpu.CompilerParams(
            dimension_semantics=("arbitrary", "arbitrary"),
            collective_id=2 if top else 4,
            has_side_effects=True,
            vmem_limit_bytes=60 * 2**20,
        ),
        cost_estimate=pl.CostEstimate(flops=14 * 10**9, bytes_accessed=40 * 2**20, transcendentals=2 * 10**6),
    )(proj, proj, marks, cws, hps, ys, sin, *rest, *big)


def back_project_kernel(n, n_dp, final, gain_ref, *refs):
    n_seq = 2 * n
    refs = list(refs)
    take = lambda k: [refs.pop(0) for _ in range(k)]
    if final:
        (cols_ref,) = take(1)
    sources = take(5)
    if final:
        out_ref, got_ref, cols_all, gains_all = take(4)
    else:
        out_ref, gains_ref, term_ref = take(3)
    dp_ref, w_ref, x_ref, g_ref, hid = places = take(5)
    loads = Loads(sources, places, *take(1))
    loads.start()
    own, so = take(2)
    line = take(9)
    rows, span, width = x_ref.shape
    part = dp_ref.shape[2]
    group = width // n_dp
    tiles = group // LANES
    chip, core, sib, left, right = line_place(n_seq)
    (term,) = take(1)
    if not final:
        (term_sem,) = take(1)
    if final:
        pieces = Pieces(n_dp, n_seq, term, got_ref, take(6))
        (gains_ref,) = take(1)
        small = Small(n_dp, n_seq, cols_ref, cols_all, *take(6))
        gain_sum = Small(n_dp, n_seq, gains_ref, gains_all, *take(6))
        meet(all_peers("seq", n_seq) + all_peers("dp", n_dp))
        small.start()
    else:
        meet(line_peers(n))
    loads.wait(0, 1)

    def term_copy(i):
        here = pl.ds(pl.multiple_of(i * LANES, LANES), LANES)
        return pltpu.make_async_copy(term.at[:, here], term_ref.at[:, here], term_sem.at[i])

    def emit(j):
        here = pl.ds(pl.multiple_of(j * CHUNK, CHUNK), CHUNK)
        block = jnp.concatenate([dp_ref[r, here] for r in range(rows)], axis=0)
        for at in range(0, width, 512):
            halves(own, so, j, core, at, dot(block, w_ref[at : at + 512], NT), rows, span)

    def product(i):
        right_side = dp_ref[...].reshape(rows * n * CHUNK, part)
        tile = (chip + 1 + i) % tiles if 2 * tiles == n_seq else i

        def one(owner, _):
            col = pl.ds(pl.multiple_of(owner * group + tile * LANES, LANES), LANES)
            h = hid[:, :, :, col].reshape(rows * n * CHUNK, LANES)
            term[owner, pl.ds(pl.multiple_of(i * LANES, LANES), LANES)] = dot(h, right_side, TN).astype(BF)
            return 0

        lax.fori_loop(0, n_dp, one, 0)

    def products(first, last):
        def one(i, _):
            @pl.when(i < tiles)
            def _():
                product(i)
                if final:
                    pieces.send(i)
                else:
                    term_copy(i).start()

            return 0

        lax.fori_loop(first, last, one, 0)

    def between(tau):
        @pl.when(tau == 0)
        def _():
            loads.wait(4)

        if final:
            pieces.tiles_do(tau - 1, tau, pieces.middle)
            pieces.tiles_do(tau - 2, tau - 1, pieces.last)
        products(jnp.where(tau == 0, 0, tau + 1), tau + 2)
        if final:

            @pl.when(tau == 1)
            def _():
                small.middle()

    def before_end():
        products(n, tiles)
        if final:
            pieces.tiles_do(n - 2, tiles, pieces.middle)
            pieces.tiles_do(n - 3, n - 2, pieces.last)

    LineSum(n, rows, emit, own, so, *line[:3], line[3:]).run(between, before_end)
    if final:
        pieces.tiles_do(n - 2, tiles, pieces.last)
    loads.wait(2, 3)
    d_gain = jnp.zeros((1, width), F32)
    for r in range(rows):
        d_hid = own[chip, r]
        x = x_ref[r].astype(F32)
        scale = lax.rsqrt(jnp.mean(x * x, axis=-1, keepdims=True) + EPS)
        m = d_hid * gain_ref[...]
        mean = jnp.mean(m * x, axis=-1, keepdims=True)
        out_ref[r] = g_ref[r].astype(F32) + scale * m - x * (scale * scale * scale * mean)
        d_gain = d_gain + jnp.sum(d_hid * x * scale, axis=0, keepdims=True)
    for t in range(width // LANES):
        gains_ref[t : t + 1] = d_gain[:, t * LANES : (t + 1) * LANES]
    if final:
        gain_sum.start()
        gain_sum.middle()
        small.end()
        gain_sum.end()
        pieces.end()
    else:
        for i in range(tiles):
            term_copy(i).wait()


def back_project(dp, w, x, g, gain, hidden, cols, n_dp, n_seq):
    rows, span, width = x.shape
    n = n_seq // 2
    part = dp.shape[2]
    group = width // n_dp
    final = cols is not None
    gains = jax.ShapeDtypeStruct((width // LANES, LANES), F32)
    outs = [jax.ShapeDtypeStruct(x.shape, F32)]
    scratch = Loads.scratch(dp, w, x, g, hidden) + LineSum.scratch(n, rows, span, width)
    scratch += [pltpu.VMEM((n_dp, group, part), BF)]
    out_specs = [VMEM_SPEC] * (4 if final else 2) + [ANY_SPEC] * (not final)
    if final:
        outs += [jax.ShapeDtypeStruct((n_seq, group // n_seq, part), BF)]
        outs += [jax.ShapeDtypeStruct((n_seq,) + x.shape, F32) for x in (cols, gains)]
        scratch += Pieces.scratch(n_dp, n_seq, group, part)
        scratch += [pltpu.VMEM(gains.shape, F32)]
        scratch += Small.scratch(n_dp, n_seq, cols) + Small.scratch(n_dp, n_seq, gains)
    else:
        outs += [gains, jax.ShapeDtypeStruct((n_dp, group, part), BF)]
        scratch += dma(group // LANES)
    return pl.pallas_call(
        functools.partial(back_project_kernel, n, n_dp, final),
        in_specs=[VMEM_SPEC] * (1 + final) + [ANY_SPEC] * 5,
        out_specs=out_specs,
        out_shape=outs,
        scratch_shapes=scratch,
        compiler_params=comm_params(5 if final else 3),
        cost_estimate=pl.CostEstimate(flops=11 * 10**9, bytes_accessed=24 * 2**20, transcendentals=0),
    )(gain, *([cols] if final else []), dp, w, x, g, hidden)


class Small:
    def __init__(self, n_dp, n_seq, vec, vall, vsum, vslots, v_s, v_r, a_s, a_r):
        self.n_dp, self.n_seq, self.vec, self.vall = n_dp, n_seq, vec, vall
        self.vsum, self.vslots, self.v_s, self.v_r, self.a_s, self.a_r = vsum, vslots, v_s, v_r, a_s, a_r

    @staticmethod
    def scratch(n_dp, n_seq, vec):
        return [pltpu.VMEM(vec.shape, F32), pltpu.VMEM((n_dp - 1,) + vec.shape, F32)] + dma(
            n_dp - 1, n_dp - 1, n_seq, n_seq
        )

    def over_dp(self, k):
        to = (lax.axis_index("dp") + k) % self.n_dp
        return remote(self.vec, self.vslots.at[k - 1], self.v_s.at[k - 1], self.v_r.at[k - 1], {"dp": to})

    def give(self, k):
        me = lax.axis_index("seq")
        to = (me + k) % self.n_seq
        return remote(self.vsum, self.vall.at[me], self.a_s.at[to], self.a_r.at[me], {"seq": to})

    def take(self, k):
        me = lax.axis_index("seq")
        source = (me + k) % self.n_seq
        return remote(self.vsum, self.vall.at[source], self.a_s.at[me], self.a_r.at[source], {"seq": source})

    def start(self):
        for k in range(1, self.n_dp):
            self.over_dp(k).start()

    def middle(self):
        total = self.vec[...]
        for k in range(1, self.n_dp):
            self.over_dp(k).wait_recv()
            total = total + self.vslots[k - 1]
        self.vsum[...] = total
        for k in range(1, self.n_seq):
            self.give(k).start()
        self.vall[lax.axis_index("seq")] = total

    def end(self):
        for k in range(1, self.n_seq):
            self.take(k).wait_recv()
        for k in range(1, self.n_seq):
            self.give(k).wait_send()
        for k in range(1, self.n_dp):
            self.over_dp(k).wait_send()


def arrange_kernel(
    groups, own_heads, got0, got1, vec0, vec1, gains0, gains1,
    *refs,
):
    gout0, gout1, gin_ref, gout_ref, gain_ref, mid_ref, cw_ref, cb_ref, dtb_ref, al_ref, ds_ref, sem = refs
    copies = [pltpu.make_async_copy(g, gout_ref.at[i], sem.at[i]) for i, g in enumerate((gout0, gout1))]
    for copy in copies:
        copy.start()
    n_seq = got0.shape[0]
    inner = DI // n_seq
    bc = CONV_CH - DI
    cols = inner // groups
    per = own_heads // groups
    for level, got in enumerate((got0, got1)):
        dts = jnp.zeros((got.shape[1], HEADS), F32)
        shared = jnp.zeros((got.shape[1], bc), F32)
        for s in range(n_seq):
            dts = dts + dot(got[s, :, :LANES].astype(F32), head_place(LANES, s, n_seq, own_heads, per), precision=HIGH)
            shared = shared + got[s, :, LANES + 2 * inner :].astype(F32)
            for g in range(groups):
                at = (g * n_seq + s) * cols
                for kind in range(2):
                    src = LANES + kind * inner + g * cols
                    gin_ref[level, :, kind * DI + at : kind * DI + at + cols] = got[s, :, src : src + cols].astype(F32)
        gin_ref[level, :, 2 * DI : 2 * DI + bc] = shared
        gin_ref[level, :, 2 * DI + bc :] = dts
    wide = (inner + bc) // LANES
    for level, (vec, gains_all) in enumerate(((vec0, gains0), (vec1, gains1))):
        total = jnp.zeros((8, bc), F32)
        heads = [jnp.zeros((1, HEADS), F32)] * 3
        for s in range(n_seq):
            tiles = [vec[s, :, t * LANES : (t + 1) * LANES] for t in range(wide)]
            for g in range(groups):
                for t in range(cols // LANES):
                    tile = tiles[g * cols // LANES + t]
                    at = (g * n_seq + s) * cols + t * LANES
                    cw_ref[level, :, at : at + LANES] = tile[:TAPS]
                    cb_ref[level : level + 1, at : at + LANES] = tile[4:5]
                    mid_ref[level : level + 1, at : at + LANES] = tile[6:7]
            total = total + jnp.concatenate(tiles[inner // LANES :], axis=1)
            skip = jnp.concatenate(tiles[: inner // LANES], axis=1)
            skip = dot(skip, head_matrix(inner), NT, HIGH)
            heads[2] = heads[2] + dot(skip, head_place(8, s, n_seq, own_heads, per), precision=HIGH)[5:6]
            place = head_place(LANES, s, n_seq, own_heads, per)
            for kind in range(2):
                heads[kind] = heads[kind] + dot(tiles[kind], place, precision=HIGH)[7:8]
        cw_ref[level, :, DI:] = total[:TAPS]
        cb_ref[level : level + 1, DI:] = total[4:5]
        for ref, value in zip((dtb_ref, al_ref, ds_ref), heads):
            ref[level : level + 1] = value
        gains = gains_all[0]
        for s in range(1, n_seq):
            gains = gains + gains_all[s]
        for t in range(gains.shape[0]):
            gain_ref[level : level + 1, t * LANES : (t + 1) * LANES] = gains[t : t + 1]
    for copy in copies:
        copy.wait()


def head_place(size, s, n_seq, own_heads, per):
    i = lax.broadcasted_iota(jnp.int32, (size, HEADS), 0)
    h = lax.broadcasted_iota(jnp.int32, (size, HEADS), 1)
    return ((i < own_heads) & (h == (i // per * n_seq + s) * per + i % per)).astype(F32)


def arrange(gots, vecs, gains, gouts, groups, own_heads, width):
    piece = gots[0].shape[1]
    shapes = [
        (2, piece, 2 * DI + CONV_CH - DI + HEADS),
        (2,) + gouts[0].shape,
        (2, width),
        (2, DI),
        (2, TAPS, CONV_CH),
        (2, CONV_CH),
        (2, HEADS),
        (2, HEADS),
        (2, HEADS),
    ]
    return pl.pallas_call(
        functools.partial(arrange_kernel, groups, own_heads),
        in_specs=[VMEM_SPEC] * 8,
        out_specs=[VMEM_SPEC, ANY_SPEC] + [VMEM_SPEC] * 7,
        out_shape=[jax.ShapeDtypeStruct(shape, F32) for shape in shapes],
        scratch_shapes=dma(2),
        compiler_params=pltpu.CompilerParams(vmem_limit_bytes=60 * 2**20),
    )(*gots, *vecs, *gains, *gouts)


def split_cols(x, groups, size):
    cols = x.shape[-1] // (groups * size)
    x = x.reshape(x.shape[:-1] + (groups, size, cols))
    x = jnp.moveaxis(x, -2, 0)
    return x.reshape(x.shape[:-2] + (groups * cols,))


def shards(
    tokens, resets, cotangent, w_in, w_out, gain_in, gain_mid, conv_w, conv_b, dt_bias, a_log, d_skip
):
    rows, span, width = tokens.shape
    layers = w_in.shape[0]
    n_dp, n_seq = lax.axis_size("dp"), lax.axis_size("seq")
    place = lax.axis_index("seq")
    length = span * n_seq
    own_heads = HEADS // n_seq
    groups = n_dp if own_heads % n_dp == 0 else 1
    inner = DI // n_seq
    bc_all = CONV_CH - DI

    dts = split_cols(w_in[..., DI + CONV_CH :], groups, n_seq)
    dts = jnp.pad(dts, ((0, 0),) * 3 + ((0, LANES - own_heads),))
    cols = LANES + 2 * inner + bc_all

    marks = jnp.pad(resets.astype(F32), ((0, 8 - rows), (0, CHUNK - span)))
    marks = jnp.where(place % 2 == 0, marks, jnp.roll(marks, span, axis=1))

    def columns(x, by_head):
        x = split_cols(x, groups, n_seq)
        x = lax.dynamic_index_in_dim(x, place, 0, False)
        return jnp.repeat(x, HEAD, axis=-1) if by_head else x

    taps = jnp.concatenate([conv_w, conv_b[:, None]], axis=1)
    rest = jnp.concatenate([d_skip[:, None], jnp.zeros((layers, 2, HEADS), F32)], axis=1)
    cws = jnp.concatenate([columns(taps[..., :DI], False), columns(rest, True)], axis=1)
    cws = jnp.concatenate([cws, jnp.pad(taps[..., DI:], ((0, 0), (0, 7 - TAPS), (0, 0)))], axis=2)
    hps = columns(jnp.stack([dt_bias, a_log], axis=1), False)
    hps = jnp.broadcast_to(jnp.pad(hps, ((0, 0), (0, 0), (0, 8 - own_heads)))[..., None], (layers, 2, 8, LANES))
    gains = columns(gain_mid[:, None], False)

    def whole_rows(w):
        return lax.dynamic_slice_in_dim(lax.all_gather(w, BOTH, axis=0, tiled=True), place * inner, inner, 0)

    resid = tokens
    stored = []
    for level in range(layers):
        gain = gains[level]
        before = resid
        if level == 0:
            hidden, proj, w_all, wo_all, marks_all = project(
                before, gain_in[level][None], w_out[level], marks, w_in, dts[:, level], level, groups, n_dp, n_seq
            )
            win = [w_all.reshape(width, cols)]
            wout = [wo_all.reshape(DI // n_seq, width) if groups == n_dp else whole_rows(w_out[level])]
            proj, own_cot = lax.optimization_barrier((proj, cotangent[0]))
            cot = lax.all_gather(own_cot, "seq")
        gated, squares, ys, sin = mix_fwd(proj, marks_all, cws, hps, level, inner)
        if level < layers - 1:
            resid, mid, scale, wo_all, w_all, next_hidden, next_proj = turn(
                gated, squares, gain, wout[level], before, gain_in[level + 1][None],
                w_out[level + 1], w_in, dts[:, level + 1], level + 1, groups, n_dp, n_seq,
            )
            wout.append(wo_all.reshape(inner, width) if groups == n_dp else whole_rows(w_out[level + 1]))
            win.append(w_all.reshape(width, cols))
            stored.append((before, hidden, proj, gain, gated, ys, sin, mid, scale))
            hidden, proj = next_hidden, next_proj
    grad = cotangent
    gots = [None] * layers
    grads_out = [None] * layers
    vecs = [None] * layers
    gain_sums = [None] * layers
    with_out = groups == n_dp
    for level in reversed(range(layers)):
        if level == layers - 1:
            given, more = cot, ((squares,), (before, cotangent))
        else:
            before, hidden, proj, gain, gated, ys, sin, mid, scale = stored[level]
            given, more = grad, ((scale, gc, gain_rows), (mid, term))
        d_proj, gc, out_term, *rest = back_mix(
            proj, marks_all, cws, hps, level, ys, sin, gain, gated, wout[level], given, more, n_dp, n_seq, with_out
        )
        if level == layers - 1:
            (outputs,) = rest
        else:
            gots[level + 1], vecs[level + 1], gain_sums[level + 1] = rest
        if with_out:
            grads_out[level] = out_term
        else:
            padded = jnp.zeros((DI, width), BF)
            padded = lax.dynamic_update_slice_in_dim(padded, out_term.reshape(inner, width), place * inner, 0)
            grads_out[level] = lax.psum_scatter(padded, BOTH, scatter_dimension=0, tiled=True).astype(F32)
        grad, *rest = back_project(
            d_proj, win[level], before, grad, gain_in[level][None], hidden, gc if level == 0 else None, n_dp, n_seq
        )
        if level == 0:
            gots[0], vecs[0], gain_sums[0] = rest
        else:
            gain_rows, term = rest
    grads = arrange(gots, vecs, gain_sums, grads_out, groups, own_heads, width)
    return (outputs, grad, *grads)


def solution(mesh):
    placed = (
        P("dp", "seq", None),
        P("dp", "seq"),
        P("dp", "seq", None),
        P(None, BOTH, None),
        P(None, BOTH, None),
    ) + (P(),) * 7
    return jax.shard_map(
        shards,
        mesh=mesh,
        in_specs=placed,
        out_specs=(
            P("dp", "seq", None),
            P("dp", "seq", None),
            P(None, BOTH, None),
            P(None, BOTH, None),
        )
        + (P(),) * 7,
        check_vma=False,
    )
```
